32 devices in a mesh: row: 8 (over z, y), rep: 4 (over x, core).
Axes of the slice: x: 2, y: 2, z: 4, core: 2. Of those that a mesh axis runs over, the one named last changes fastest.
Arguments:
- node_features: bfloat16 [16384, 256], P('row'), may hold values from -6 to 6
- weight: bfloat16 [256, 256], replicated, may hold values from -0.375 to 0.375
- out_grad: bfloat16 [16384, 256], P(('row', 'rep')), may hold values from -6 to 6
- blocks: bfloat16 [6144, 128, 128], P(('row', 'rep')), may hold values from -0.109375 to 0.109375
- block_rows: int32 [6144], P(('row', 'rep')), may hold values from 0 to 15
- block_fetch: int32 [6144], P(('row', 'rep')), may hold values from 0 to 15, as said below
- fetch_lists: int32 [32, 8, 2], P(('row', 'rep')), may hold values from 0 to 15, as said below
- block_count: int32 [32], P(('row', 'rep')), may hold values from 27 to 192, as said below
Outputs:
- output: bfloat16 [16384, 256], P(('row', 'rep'))
- weight_grad: float32 [256, 256], replicated
- node_grad: float32 [16384, 256], P(('row', 'rep'))
The draws below stay inside these ranges and needn't reach their ends.
Inputs may be any that keep to these rules, and one draw needn't show every extreme that they name: `fetch_lists`: each fetch list of one device and one source group holds 2 different node blocks, and all devices of one row group hold the same fetch lists. `block_fetch`: within each device, the first 16 slots name every value once. `block_count`: some device has all 192 slots live.
All inputs are finite; a program needn't handle non-finite values.
Results may differ from the reference program's by a relative error of at most 0.0056.
Values may be sent and summed in bfloat16 or wider, within the bound.
No kernel may reach another device: no remote copies, remote signals or barrier semaphores. Data moves between devices by JAX's collectives and lax.ppermute only.
A program may use at most 128 MiB of HBM per device.

```python
import jax
import jax.numpy as jnp
from jax import lax

F = 256
BLK = 128
RB = 16
NB = 192
C = 2
NODES = 16384
BLOCKS = 6144
N_ROW = 8
N_REP = 4


def draw_fetch_lists(key, part):
    key = jax.random.fold_in(key, 11)
    scores = jax.random.randint(key, (N_ROW, N_ROW, RB), 0, 1 << 20) * RB + jnp.arange(RB, dtype=jnp.int32)
    ordering = jnp.argsort(scores, axis=-1, stable=True)[..., :C]
    return jnp.repeat(ordering, N_REP, axis=0).astype(jnp.int32)


def draw_block_fetch(key, part):
    key = jax.random.fold_in(key, 12)
    first_key, rest_key = jax.random.split(key)
    dev_count = N_ROW * N_REP
    pairs = N_ROW * C
    scores = jax.random.randint(first_key, (dev_count, pairs), 0, 1 << 20) * pairs + jnp.arange(pairs, dtype=jnp.int32)
    leading = jnp.argsort(scores, axis=-1, stable=True).astype(jnp.int32)
    trailing = jax.random.randint(rest_key, (dev_count, NB - pairs), 0, pairs).astype(jnp.int32)
    return jnp.concatenate([leading, trailing], axis=1).reshape(-1).astype(jnp.int32)


def draw_block_count(key, part):
    key = jax.random.fold_in(key, 13)
    level_key, chosen_key = jax.random.split(key)
    dev_count = N_ROW * N_REP
    levels = jax.random.randint(level_key, (dev_count,), 3, 9)
    counts = NB * levels * levels // 64
    chosen = jax.random.randint(chosen_key, (), 0, dev_count)
    return jnp.where(jnp.arange(dev_count) == chosen, NB, counts).astype(jnp.int32)


def set_ends(result, key, least, top_value):
    place = [jax.random.randint(jax.random.fold_in(key, axis), (), 0, length) for axis, length in enumerate(result.shape)]
    main_axis = result.shape.index(max(result.shape))
    neighbour = place[:main_axis] + [(place[main_axis] + 1) % result.shape[main_axis]] + place[main_axis + 1:]
    return result.at[tuple(place)].set(least).at[tuple(neighbour)].set(top_value)


def shard_levels(stream_key, shape, cuts, smallest, top_value):
    loudness, own = 1.0, jax.random.fold_in(stream_key, 6)
    for dim, parts in cuts:
        draws = jnp.exp(jax.random.uniform(jax.random.fold_in(own, dim), (parts,), jnp.float32, smallest / len(cuts), top_value / len(cuts)))
        loudness = loudness * jnp.repeat(draws, shape[dim] // parts).reshape([-1 if axis == dim else 1 for axis in range(len(shape))])
    return loudness


def gaussian(rng, shape, width, limit, pieces=(), kind=jnp.bfloat16):
    entries = width * jax.random.normal(rng, shape, jnp.float32)
    if pieces:
        entries = entries * shard_levels(rng, shape, pieces, -0.22, 0.18)
    return jnp.clip(entries, -limit, limit).astype(kind)


def setup_inputs(seed: int = 0) -> dict:
    seeds = jax.random.split(jax.random.key(seed), 9)
    node_features = gaussian(seeds[0], (NODES, F), 1.0, 6.0, ((0, 8),))
    weight = gaussian(seeds[1], (F, F), F ** -0.5, 0.375)
    out_grad = gaussian(seeds[2], (NODES, F), 1.0, 6.0, ((0, 32),))
    blocks = gaussian(seeds[3], (BLOCKS, BLK, BLK), (2 * NB * BLK // RB) ** -0.5, 0.109375, ((0, 32),))
    block_rows = set_ends(jax.random.randint(seeds[4], (BLOCKS,), 0, RB), jax.random.fold_in(seeds[4], 1), 0, RB - 1).astype(jnp.int32)
    block_fetch = draw_block_fetch(jax.random.fold_in(seeds[8], 71), 0)
    fetch_lists = draw_fetch_lists(jax.random.fold_in(seeds[8], 71), 0)
    block_count = draw_block_count(jax.random.fold_in(seeds[8], 71), 0)
    return {"node_features": node_features, "weight": weight, "out_grad": out_grad, "blocks": blocks, "block_rows": block_rows, "block_fetch": block_fetch, "fetch_lists": fetch_lists, "block_count": block_count}


def silu_grad(pre_act):
    sigmoid_part = jax.nn.sigmoid(pre_act)
    return sigmoid_part * (1.0 + pre_act * (1.0 - sigmoid_part))

def reference(node_features, weight, out_grad, blocks, block_rows, block_fetch, fetch_lists, block_count):
    dev_count = N_ROW * N_REP
    positions = jnp.arange(dev_count * NB, dtype=jnp.int32)
    owners = positions // NB
    live_mask = (positions % NB < block_count[owners]).astype(jnp.float32)
    sources = block_fetch // C
    slot_index = block_fetch % C
    col_blocks = (sources * RB + fetch_lists[owners, sources, slot_index]).astype(jnp.int32)
    row_blocks = (owners // N_REP * RB + block_rows).astype(jnp.int32)
    feature_blocks = node_features.astype(jnp.float32).reshape(-1, BLK, F)
    block_total = feature_blocks.shape[0]
    stacked = (blocks.reshape(dev_count, NB, BLK, BLK), live_mask.reshape(dev_count, NB), col_blocks.reshape(dev_count, NB), row_blocks.reshape(dev_count, NB))

    def forward_step(accum, inputs):
        adjacency, mask_here, columns, rows_here = inputs
        adj_values = adjacency.astype(jnp.float32) * mask_here[:, None, None]
        products = jnp.einsum('bkj,bjf->bkf', adj_values, feature_blocks[columns])
        return (accum.at[rows_here].add(products), None)
    aggregate, _ = lax.scan(forward_step, jnp.zeros((block_total, BLK, F), jnp.float32), stacked)
    hidden_in = aggregate.reshape(-1, F).astype(jnp.bfloat16)
    pre_act = jnp.dot(hidden_in, weight, preferred_element_type=jnp.float32)
    output = jax.nn.silu(pre_act).astype(jnp.bfloat16)
    pre_grad = (out_grad.astype(jnp.float32) * silu_grad(pre_act)).astype(jnp.bfloat16)
    factor = float(hidden_in.shape[0]) ** (-0.5)
    weight_grad = jnp.dot(hidden_in.T, pre_grad, preferred_element_type=jnp.float32) * factor
    input_grad = jnp.dot(pre_grad, weight.T, preferred_element_type=jnp.float32).astype(jnp.bfloat16)
    grad_blocks = input_grad.astype(jnp.float32).reshape(-1, BLK, F)

    def backward_step(accum, inputs):
        adjacency, mask_here, columns, rows_here = inputs
        adj_values = adjacency.astype(jnp.float32) * mask_here[:, None, None]
        products = jnp.einsum('bjk,bjf->bkf', adj_values, grad_blocks[rows_here])
        return (accum.at[columns].add(products), None)
    gradient, _ = lax.scan(backward_step, jnp.zeros((block_total, BLK, F), jnp.float32), stacked)
    node_grad = gradient.reshape(-1, F)
    return (output, weight_grad, node_grad)
```

```python
import functools

import jax
import jax.numpy as jnp
from jax import lax
from jax.experimental import pallas as pl
from jax.experimental.pallas import tpu as pltpu
from jax.sharding import PartitionSpec as P

BF16 = jnp.bfloat16
F32 = jnp.float32
SLOT_GROUP = 16
COL_CHUNK = 16
ROW_TILE = 256
COL_TILE = 512
WHOLE = pl.BlockSpec(memory_space=pltpu.VMEM)
SMEM = pl.BlockSpec(memory_space=pltpu.SMEM)
ANY = pl.BlockSpec(memory_space=pl.ANY)


def params(*parts):
    size = sum(parts) + (6 << 20)
    return pltpu.CompilerParams(vmem_limit_bytes=min(size, 60 << 20))


def shape(dims, dtype):
    return jax.ShapeDtypeStruct(tuple(dims), dtype)


def dot(a, b, dims=((1,), (0,))):
    return lax.dot_general(a, b, (dims, ((), ())), preferred_element_type=F32)


def xor_perm(count, offset):
    return [(i, i ^ offset) for i in range(count)]


def densify_body(
    rows_ref, fetch_ref, count_ref, blocks_ref, out_ref, acc_ref, *, half, n_rep, n_hi, per_list, quarter
):
    r, q = lax.axis_index("row"), lax.axis_index("rep")
    chunk, step = pl.program_id(0), pl.program_id(1)
    group, blk = blocks_ref.shape[0], blocks_ref.shape[1]
    half_cells = acc_ref.shape[0]

    @pl.when(step == 0)
    def _():
        @pl.loop(0, half_cells)
        def _(i):
            acc_ref[i] = jnp.zeros(acc_ref.shape[1:], F32)

    live = count_ref[0]

    @pl.loop(0, group)
    def _(i):
        slot = step * group + i
        row = rows_ref[slot]
        fetch = fetch_ref[slot]
        j = lax.div(row, quarter) ^ q
        row_cell = (n_rep - 1 - j) * quarter + lax.rem(row, quarter) - half * half_cells
        k = lax.div(fetch, per_list) ^ r
        piece = (lax.rem(k, n_rep) ^ q) * n_hi + lax.div(k, n_rep)
        col_cell = piece * per_list + lax.rem(fetch, per_list) - chunk * COL_CHUNK
        here = (row_cell >= 0) & (row_cell < half_cells) & (col_cell >= 0) & (col_cell < COL_CHUNK)

        @pl.when(here & (slot < live))
        def _():
            cols = pl.ds(pl.multiple_of(col_cell * blk, blk), blk)
            acc_ref[row_cell, :, cols] += blocks_ref[i].astype(F32)

    @pl.when(step == pl.num_programs(1) - 1)
    def _():
        @pl.loop(0, half_cells)
        def _(i):
            out_ref[pl.ds(pl.multiple_of(i * blk, blk), blk), :] = acc_ref[i].astype(BF16)


def densify(block_rows, block_fetch, block_count, blocks, half, n_row, n_rep, per_list, row_blocks):
    slots, blk, _ = blocks.shape
    half_cells = row_blocks // 2
    cols = n_row * per_list * blk
    width = COL_CHUNK * blk
    body = functools.partial(
        densify_body,
        half=half,
        n_rep=n_rep,
        n_hi=n_row // n_rep,
        per_list=per_list,
        quarter=row_blocks // n_rep,
    )
    return pl.pallas_call(
        body,
        out_shape=shape((half_cells * blk, cols), BF16),
        grid_spec=pltpu.PrefetchScalarGridSpec(
            num_scalar_prefetch=3,
            grid=(cols // width, slots // SLOT_GROUP),
            in_specs=[pl.BlockSpec((SLOT_GROUP, blk, blk), lambda c, s, *_: (s, 0, 0))],
            out_specs=pl.BlockSpec((half_cells * blk, width), lambda c, s, *_: (0, c)),
            scratch_shapes=[pltpu.VMEM((half_cells, blk, width), F32)],
        ),
        compiler_params=params(half_cells * blk * width * 8, SLOT_GROUP * blk * blk * 4),
        cost_estimate=pl.CostEstimate(
            flops=slots * blk * blk, bytes_accessed=blocks.size * 2 + 8 * cols * half_cells * blk, transcendentals=0
        ),
        name=f"densify_{half}",
    )(block_rows, block_fetch, block_count, blocks)


def pack_body(*refs, n_hi, per_list, blk):
    lists = refs[:n_hi]
    features = refs[n_hi]
    outs = refs[n_hi + 1 : 2 * n_hi + 1]
    sems = refs[-1]
    r = lax.axis_index("row")
    copies = []
    for hi in range(n_hi):
        for c in range(per_list):
            b = lists[hi][0, r, c]
            copy = pltpu.make_async_copy(
                features.at[pl.ds(pl.multiple_of(b * blk, blk), blk)],
                outs[hi].at[pl.ds(c * blk, blk)],
                sems.at[hi * per_list + c],
            )
            copy.start()
            copies.append(copy)
    for copy in copies:
        copy.wait()


def pack(lists, features, per_list, blk):
    n_hi = len(lists)
    return pl.pallas_call(
        functools.partial(pack_body, n_hi=n_hi, per_list=per_list, blk=blk),
        out_shape=[shape((per_list * blk, features.shape[1]), BF16)] * n_hi,
        in_specs=[SMEM] * n_hi + [ANY],
        out_specs=[ANY] * n_hi,
        scratch_shapes=[pltpu.SemaphoreType.DMA((n_hi * per_list,))],
        compiler_params=params(0),
        name="pack",
    )(*lists, features)


def forward_body(*refs, n_pieces):
    pieces = refs[:n_pieces]
    adj_ref, send_ref, keep_ref = refs[n_pieces:]
    i = pl.program_id(0)
    depth = pieces[0].shape[0]
    total = dot(adj_ref[:, :depth], pieces[0][...])
    for n in range(1, n_pieces):
        total += dot(adj_ref[:, n * depth : (n + 1) * depth], pieces[n][...])

    half = pl.num_programs(0) // 2

    @pl.when(i < half)
    def _():
        send_ref[...] = total.astype(BF16)

    @pl.when(i >= half)
    def _():
        keep_ref[...] = total


def forward(pieces, adj):
    rows, cols = adj.shape
    features = pieces[0].shape[1]
    tiles = rows // ROW_TILE
    half = tiles // 2
    return pl.pallas_call(
        functools.partial(forward_body, n_pieces=len(pieces)),
        grid=(tiles,),
        out_shape=[shape((rows // 2, features), BF16), shape((rows // 2, features), F32)],
        in_specs=[pl.BlockSpec(x.shape, lambda i: (0, 0)) for x in pieces]
        + [pl.BlockSpec((ROW_TILE, cols), lambda i: (i, 0))],
        out_specs=[
            pl.BlockSpec((ROW_TILE, features), lambda i: (jnp.minimum(i, half - 1), 0)),
            pl.BlockSpec((ROW_TILE, features), lambda i: (jnp.maximum(i - half, 0), 0)),
        ],
        compiler_params=params(ROW_TILE * cols * 4, cols * features * 4),
        cost_estimate=pl.CostEstimate(
            flops=2 * rows * cols * features, bytes_accessed=adj.size * 2 + cols * features * 2, transcendentals=0
        ),
        name="forward",
    )(*pieces, adj)


def middle_body(
    keep_ref, near_ref, far_ref, weight_ref, cot_ref, out_ref, grad_ref, wsend_ref, w2_ref, w0_ref, acc_ref
):
    q = lax.axis_index("rep")
    hidden = (keep_ref[...] + near_ref[...].astype(F32) + far_ref[...].astype(F32)).astype(BF16)
    weight = weight_ref[...]
    pre_act = dot(hidden, weight)
    sig = jax.nn.sigmoid(pre_act)
    out_ref[...] = (pre_act * sig).astype(BF16)
    pre_grad = (cot_ref[...].astype(F32) * (sig * (1.0 + pre_act * (1.0 - sig)))).astype(BF16)
    grad_ref[...] = dot(weight, pre_grad, ((1,), (1,))).astype(BF16)
    acc_ref[...] = dot(hidden, pre_grad, ((0,), (0,)))
    part = w0_ref.shape[0]

    def piece(j):
        return acc_ref[pl.ds(pl.multiple_of((q ^ j) * part, part), part), :]

    wsend_ref[:part] = piece(3)
    wsend_ref[part:] = piece(1)
    w2_ref[...] = piece(2)
    w0_ref[...] = piece(0)


def middle(keep, near, far, weight, cot, n_rep):
    rows, features = keep.shape
    part = features // n_rep
    return pl.pallas_call(
        middle_body,
        out_shape=[
            shape((rows, features), BF16),
            shape((features, rows), BF16),
            shape((2 * part, features), F32),
            shape((part, features), F32),
            shape((part, features), F32),
        ],
        in_specs=[WHOLE] * 5,
        out_specs=[WHOLE] * 5,
        scratch_shapes=[pltpu.VMEM((features, features), F32)],
        compiler_params=params(12 << 20),
        cost_estimate=pl.CostEstimate(
            flops=6 * rows * features * features, bytes_accessed=rows * features * 14, transcendentals=rows * features
        ),
        name="middle",
    )(keep, near, far, weight, cot)


def back_first_body(odd_ref, even_ref, adj_ref, out_ref):
    rows = odd_ref.shape[1]
    out_ref[...] = dot(odd_ref[...], adj_ref[:rows]) + dot(even_ref[...], adj_ref[rows:])


def back_first(odd, even, adj):
    rows, cols = adj.shape
    features = odd.shape[0]
    return pl.pallas_call(
        back_first_body,
        grid=(cols // COL_TILE,),
        out_shape=shape((features, cols), F32),
        in_specs=[
            pl.BlockSpec(odd.shape, lambda i: (0, 0)),
            pl.BlockSpec(even.shape, lambda i: (0, 0)),
            pl.BlockSpec((rows, COL_TILE), lambda i: (0, i)),
        ],
        out_specs=pl.BlockSpec((features, COL_TILE), lambda i: (0, i)),
        compiler_params=params(4 << 20),
        cost_estimate=pl.CostEstimate(
            flops=2 * rows * cols * features, bytes_accessed=adj.size * 2 + cols * features * 4, transcendentals=0
        ),
        name="back_first",
    )(odd, even, adj)


def back_second_body(odd_ref, even_ref, adj_ref, first_ref, o3_ref, o2_ref, o1_ref, o0_ref, acc_ref):
    q = lax.axis_index("rep")
    rows = odd_ref.shape[1]
    acc_ref[...] = first_ref[...] + dot(odd_ref[...], adj_ref[:rows]) + dot(even_ref[...], adj_ref[rows:])
    part = o0_ref.shape[0]

    def piece(j):
        return acc_ref[pl.ds(pl.multiple_of((q ^ j) * part, part), part), :]

    o3_ref[...] = piece(3).astype(BF16)
    o2_ref[...] = piece(2)
    o1_ref[...] = piece(1).astype(BF16)
    o0_ref[...] = piece(0)


def back_second(odd, even, adj, first, n_rep):
    rows, cols = adj.shape
    features = odd.shape[0]
    part = features // n_rep
    per_piece = cols // n_rep // COL_TILE
    keep_spec = pl.BlockSpec((part, COL_TILE), lambda i: (0, i))
    send_spec = pl.BlockSpec(
        (part, COL_TILE), lambda i: (0, (lax.div(i, per_piece) ^ 1) * per_piece + lax.rem(i, per_piece))
    )
    return pl.pallas_call(
        back_second_body,
        grid=(cols // COL_TILE,),
        out_shape=[shape((part, cols), dtype) for dtype in (BF16, F32, BF16, F32)],
        in_specs=[
            pl.BlockSpec(odd.shape, lambda i: (0, 0)),
            pl.BlockSpec(even.shape, lambda i: (0, 0)),
            pl.BlockSpec((rows, COL_TILE), lambda i: (0, i)),
            pl.BlockSpec((features, COL_TILE), lambda i: (0, i)),
        ],
        out_specs=[send_spec, keep_spec, send_spec, keep_spec],
        scratch_shapes=[pltpu.VMEM((features, COL_TILE), F32)],
        compiler_params=params(6 << 20),
        cost_estimate=pl.CostEstimate(
            flops=2 * rows * cols * features, bytes_accessed=adj.size * 2 + cols * features * 7, transcendentals=0
        ),
        name="back_second",
    )(odd, even, adj, first)


def split_body(own_ref, near_ref, far_ref, *outs, n_rep, n_hi):
    q = lax.axis_index("rep")
    width = outs[0].shape[1]
    for k, out in enumerate(outs):
        j, hi = (k % n_rep) ^ q, k // n_rep
        cols = pl.ds(pl.multiple_of((j * n_hi + hi) * width, width), width)
        far_cols = pl.ds(pl.multiple_of(((j ^ 2) * n_hi + hi) * width, width), width)
        total = own_ref[:, cols] + near_ref[:, cols].astype(F32) + far_ref[:, far_cols].astype(F32)
        out[...] = total.astype(out.dtype)


def split(own, near, far, n_row, n_rep):
    part, cols = own.shape
    width = cols // n_row
    return pl.pallas_call(
        functools.partial(split_body, n_rep=n_rep, n_hi=n_row // n_rep),
        out_shape=[shape((part, width), F32 if k == 0 else BF16) for k in range(n_row)],
        in_specs=[WHOLE] * 3,
        out_specs=[WHOLE] * n_row,
        compiler_params=params(own.size * 12),
        cost_estimate=pl.CostEstimate(flops=2 * own.size, bytes_accessed=own.size * 10, transcendentals=0),
        name="split",
    )(own, near, far)


def collect_body(lists_ref, *refs, n_row, per_list, quarter, blk):
    messages = refs[:n_row]
    outs = refs[n_row:-1]
    acc_ref = refs[-1]
    r, q = lax.axis_index("row"), lax.axis_index("rep")
    acc_ref[...] = jnp.zeros(acc_ref.shape, F32)
    for k in range(n_row):
        for c in range(per_list):
            b = lists_ref[(r ^ k) * per_list + c]
            cell = (lax.div(b, quarter) ^ q) * quarter + lax.rem(b, quarter)
            cols = pl.ds(pl.multiple_of(cell * blk, blk), blk)
            acc_ref[:, cols] += messages[k][:, c * blk : (c + 1) * blk].astype(F32)
    width = outs[0].shape[1]
    for j, out in enumerate(outs):
        out[...] = acc_ref[:, j * width : (j + 1) * width].astype(out.dtype)


def collect(lists, messages, n_rep, per_list, row_blocks, blk):
    part = messages[0].shape[0]
    quarter = row_blocks // n_rep
    return pl.pallas_call(
        functools.partial(collect_body, n_row=len(messages), per_list=per_list, quarter=quarter, blk=blk),
        out_shape=[shape((part, quarter * blk), F32 if j == 0 else BF16) for j in range(n_rep)],
        in_specs=[SMEM] + [WHOLE] * len(messages),
        out_specs=[WHOLE] * n_rep,
        scratch_shapes=[pltpu.VMEM((part, row_blocks * blk), F32)],
        compiler_params=params(4 << 20),
        cost_estimate=pl.CostEstimate(
            flops=part * row_blocks * blk, bytes_accessed=part * row_blocks * blk * 5, transcendentals=0
        ),
        name="collect",
    )(lists, *messages)


def finish_body(*refs, n_rep, factor):
    grads = refs[:n_rep]
    weights = refs[n_rep : 2 * n_rep]
    node_ref, weight_ref, acc_ref = refs[2 * n_rep :]
    q = lax.axis_index("rep")
    part = grads[0].shape[0]
    for j in range(n_rep):
        rows = pl.ds(pl.multiple_of((q ^ j) * part, part), part)
        acc_ref[rows, :] = grads[j][...].astype(F32)
        weight_ref[rows, :] = weights[j][...] * factor
    node_ref[...] = acc_ref[...].T


def finish(grads, weights, factor):
    n_rep = len(grads)
    part, rows = grads[0].shape
    features = weights[0].shape[1]
    return pl.pallas_call(
        functools.partial(finish_body, n_rep=n_rep, factor=factor),
        out_shape=[shape((rows, part * n_rep), F32), shape((features, features), F32)],
        in_specs=[WHOLE] * (2 * n_rep),
        out_specs=[WHOLE] * 2,
        scratch_shapes=[pltpu.VMEM((part * n_rep, rows), F32)],
        compiler_params=params(6 << 20),
        cost_estimate=pl.CostEstimate(flops=0, bytes_accessed=rows * part * n_rep * 8, transcendentals=0),
        name="finish",
    )(*grads, *weights)


def local(
    node_features, weight, out_grad, blocks, block_rows, block_fetch, fetch_lists, block_count
):
    n_row = lax.axis_size("row")
    n_rep = lax.axis_size("rep")
    n_hi = n_row // n_rep
    band_rows, features = node_features.shape
    blk = blocks.shape[1]
    row_blocks = band_rows // blk
    per_list = fetch_lists.shape[2]

    def to_rep(x, j):
        return lax.ppermute(x, "rep", xor_perm(n_rep, j))

    def to_row(x, k):
        return lax.ppermute(x, "row", xor_perm(n_row, k))

    def spread(x, hi):
        perm = [
            (r * n_rep + q, (r ^ (hi * n_rep + q)) * n_rep + q) for r in range(n_row) for q in range(n_rep)
        ]
        return lax.ppermute(x, ("row", "rep"), perm)

    wanted = [spread(fetch_lists, hi) for hi in range(n_hi)]
    all_lists = lax.all_gather(fetch_lists[0], "row", axis=0, tiled=False)
    lists = lax.dynamic_index_in_dim(all_lists, lax.axis_index("row"), 1, keepdims=False).reshape(-1)

    outgoing = pack(wanted, node_features, per_list, blk)
    own = [spread(x, hi) for hi, x in enumerate(outgoing)]
    far = [to_rep(x, 2) for x in own]
    near = [to_rep(x, 1) for x in own]
    diag = [to_rep(x, 1) for x in far]
    pieces = own + near + far + diag

    adj_far, adj_near = [
        densify(block_rows, block_fetch, block_count, blocks, half, n_row, n_rep, per_list, row_blocks)
        for half in range(2)
    ]

    send3, keep2 = forward(pieces, adj_far)
    across = (keep2 + to_rep(send3, 1).astype(F32)).astype(BF16)
    arrived = to_rep(across, 2)
    send1, keep0 = forward(pieces, adj_near)
    output, grad0, wsend, w2, w0 = middle(keep0, to_rep(send1, 1), arrived, weight, out_grad, n_rep)

    grad2 = to_rep(grad0, 2)
    grad1 = to_rep(grad0, 1)
    grad3 = to_rep(grad2, 1)
    first = back_first(grad1, grad0, adj_near)
    o3, o2, o1, o0 = back_second(grad3, grad2, adj_far, first, n_rep)
    back_across = (o2 + to_rep(o3, 1).astype(F32)).astype(BF16)
    messages = split(o0, to_rep(o1, 1), to_rep(back_across, 2), n_row, n_rep)
    returned = [messages[0]] + [to_row(messages[k], k) for k in range(1, n_row)]
    grads = collect(lists, returned, n_rep, per_list, row_blocks, blk)

    part = features // n_rep
    got = to_rep(wsend, 1)
    w = w0 + got[part:] + to_rep(w2 + got[:part], 2)
    step = 1
    while step < n_row:
        w = w + to_row(w, step)
        step *= 2

    all_grads = [grads[0]] + [to_rep(grads[j], j) for j in range(1, n_rep)]
    all_w = [w] + [to_rep(w, j) for j in range(1, n_rep)]
    factor = float(n_row * band_rows) ** (-0.5)
    node_grad, weight_grad = finish(all_grads, all_w, factor)
    return (output, weight_grad, node_grad)


def solution(mesh):
    in_specs = (
        P("row", None),
        P(),
        P(("row", "rep"), None),
        P(("row", "rep"), None, None),
        P(("row", "rep")),
        P(("row", "rep")),
        P(("row", "rep"), None, None),
        P(("row", "rep")),
    )
    out_specs = (P(("row", "rep"), None), P(), P(("row", "rep"), None))
    return jax.shard_map(local, mesh=mesh, in_specs=in_specs, out_specs=out_specs, check_vma=False)
```

```python
import functools

import jax
import jax.numpy as jnp
from jax import lax
from jax.experimental import pallas as pl
from jax.experimental.pallas import tpu as pltpu
from jax.sharding import PartitionSpec as P

BF16 = jnp.bfloat16
F32 = jnp.float32
SLOT_GROUP = 16
COL_CHUNK = 16
ROW_TILE = 256
COL_TILE = 512
WHOLE = pl.BlockSpec(memory_space=pltpu.VMEM)
SMEM = pl.BlockSpec(memory_space=pltpu.SMEM)
ANY = pl.BlockSpec(memory_space=pl.ANY)


def params(*parts):
    return pltpu.CompilerParams(vmem_limit_bytes=min(sum(parts) + (6 << 20), 62 << 20))


def shape(dims, dtype):
    return jax.ShapeDtypeStruct(tuple(dims), dtype)


def dot(a, b, dims=((1,), (0,))):
    return lax.dot_general(a, b, (dims, ((), ())), preferred_element_type=F32)


def xor_perm(count, offset):
    return [(i, i ^ offset) for i in range(count)]


def densify_body(
    rows_ref, fetch_ref, count_ref, blocks_ref, out_ref, acc_ref, held_ref, sems, *, half, n_rep, n_hi, per_list, quarter
):
    r, q = lax.axis_index("row"), lax.axis_index("rep")
    chunk = pl.program_id(0)
    slots, blk = blocks_ref.shape[0], blocks_ref.shape[1]
    groups = slots // SLOT_GROUP
    half_cells = acc_ref.shape[0]

    def fetch_group(g):
        part = pl.ds(g * SLOT_GROUP, SLOT_GROUP)
        return pltpu.make_async_copy(blocks_ref.at[part], held_ref.at[part], sems.at[g])

    @pl.when(chunk == 0)
    def _():
        @pl.loop(0, groups)
        def _(g):
            fetch_group(g).start()

    @pl.loop(0, half_cells)
    def _(i):
        acc_ref[i] = jnp.zeros(acc_ref.shape[1:], F32)

    live = count_ref[0]

    @pl.loop(0, groups)
    def _(g):
        @pl.when(chunk == 0)
        def _():
            fetch_group(g).wait()

        @pl.loop(0, SLOT_GROUP)
        def _(i):
            slot = g * SLOT_GROUP + i
            row = rows_ref[slot]
            fetch = fetch_ref[slot]
            j = lax.div(row, quarter) ^ q
            row_cell = (n_rep - 1 - j) * quarter + lax.rem(row, quarter) - half * half_cells
            k = lax.div(fetch, per_list) ^ r
            piece = (lax.rem(k, n_rep) ^ q) * n_hi + lax.div(k, n_rep)
            col_cell = piece * per_list + lax.rem(fetch, per_list) - chunk * COL_CHUNK
            here = (row_cell >= 0) & (row_cell < half_cells) & (col_cell >= 0) & (col_cell < COL_CHUNK)

            @pl.when(here & (slot < live))
            def _():
                cols = pl.ds(pl.multiple_of(col_cell * blk, blk), blk)
                acc_ref[row_cell, :, cols] += held_ref[slot].astype(F32)

    @pl.loop(0, half_cells)
    def _(i):
        out_ref[pl.ds(pl.multiple_of(i * blk, blk), blk), :] = acc_ref[i].astype(BF16)


def densify(block_rows, block_fetch, block_count, blocks, half, n_row, n_rep, per_list, row_blocks):
    slots, blk, _ = blocks.shape
    half_cells = row_blocks // 2
    cols = n_row * per_list * blk
    width = COL_CHUNK * blk
    body = functools.partial(
        densify_body,
        half=half,
        n_rep=n_rep,
        n_hi=n_row // n_rep,
        per_list=per_list,
        quarter=row_blocks // n_rep,
    )
    return pl.pallas_call(
        body,
        out_shape=shape((half_cells * blk, cols), BF16),
        grid_spec=pltpu.PrefetchScalarGridSpec(
            num_scalar_prefetch=3,
            grid=(cols // width,),
            in_specs=[pl.BlockSpec(memory_space=pltpu.HBM)],
            out_specs=pl.BlockSpec((half_cells * blk, width), lambda c, *_: (0, c)),
            scratch_shapes=[
                pltpu.VMEM((half_cells, blk, width), F32),
                pltpu.VMEM(blocks.shape, BF16),
                pltpu.SemaphoreType.DMA((slots // SLOT_GROUP,)),
            ],
        ),
        compiler_params=params((52 if half else 56) << 20),
        cost_estimate=pl.CostEstimate(
            flops=slots * blk * blk, bytes_accessed=blocks.size * 2 + 8 * cols * half_cells * blk, transcendentals=0
        ),
        name=f"densify_{half}",
    )(block_rows, block_fetch, block_count, blocks)


def pack_body(*refs, n_hi, per_list, blk):
    lists = refs[:n_hi]
    features = refs[n_hi]
    outs = refs[n_hi + 1 : 2 * n_hi + 1]
    own_list, sems = refs[2 * n_hi + 1 :]
    r = lax.axis_index("row")
    copies = []
    for hi in range(n_hi):
        for c in range(per_list):
            b = lists[hi][0, r, c]
            own_list[hi * per_list + c] = b
            copy = pltpu.make_async_copy(
                features.at[pl.ds(pl.multiple_of(b * blk, blk), blk)],
                outs[hi].at[pl.ds(c * blk, blk)],
                sems.at[hi * per_list + c],
            )
            copy.start()
            copies.append(copy)
    for copy in copies:
        copy.wait()


def pack(lists, features, per_list, blk):
    n_hi = len(lists)
    return pl.pallas_call(
        functools.partial(pack_body, n_hi=n_hi, per_list=per_list, blk=blk),
        out_shape=[shape((per_list * blk, features.shape[1]), BF16)] * n_hi + [shape((128,), jnp.int32)],
        in_specs=[SMEM] * n_hi + [pl.BlockSpec(memory_space=pltpu.HBM)],
        out_specs=[ANY] * n_hi + [SMEM],
        scratch_shapes=[pltpu.SemaphoreType.DMA((n_hi * per_list,))],
        compiler_params=params(0),
        name="pack",
    )(*lists, features)


def forward_body(*refs, n_pieces):
    pieces = refs[:n_pieces]
    adj_ref, send_ref, keep_ref = refs[n_pieces:]
    i = pl.program_id(0)
    depth = pieces[0].shape[0]
    total = dot(adj_ref[:, :depth], pieces[0][...])
    for n in range(1, n_pieces):
        total += dot(adj_ref[:, n * depth : (n + 1) * depth], pieces[n][...])

    half = pl.num_programs(0) // 2

    @pl.when(i < half)
    def _():
        send_ref[...] = total.astype(BF16)

    @pl.when(i >= half)
    def _():
        keep_ref[...] = total


def forward(pieces, adj):
    rows, cols = adj.shape
    features = pieces[0].shape[1]
    tiles = rows // ROW_TILE
    half = tiles // 2
    return pl.pallas_call(
        functools.partial(forward_body, n_pieces=len(pieces)),
        grid=(tiles,),
        out_shape=[shape((rows // 2, features), BF16), shape((rows // 2, features), F32)],
        in_specs=[pl.BlockSpec(x.shape, lambda i: (0, 0)) for x in pieces]
        + [pl.BlockSpec((ROW_TILE, cols), lambda i: (i, 0))],
        out_specs=[
            pl.BlockSpec((ROW_TILE, features), lambda i: (jnp.minimum(i, half - 1), 0)),
            pl.BlockSpec((ROW_TILE, features), lambda i: (jnp.maximum(i - half, 0), 0)),
        ],
        compiler_params=params(ROW_TILE * cols * 4, cols * features * 4),
        cost_estimate=pl.CostEstimate(
            flops=2 * rows * cols * features, bytes_accessed=adj.size * 2 + cols * features * 2, transcendentals=0
        ),
        name="forward",
    )(*pieces, adj)


def middle_body(
    keep_ref, near_ref, far_ref, weight_ref, cot_ref, out_ref, grad_ref, wsend_ref, w2_ref, w0_ref, acc_ref
):
    q = lax.axis_index("rep")
    hidden = (keep_ref[...] + near_ref[...].astype(F32) + far_ref[...].astype(F32)).astype(BF16)
    weight = weight_ref[...]
    pre_act = dot(hidden, weight)
    sig = jax.nn.sigmoid(pre_act)
    out_ref[...] = (pre_act * sig).astype(BF16)
    pre_grad = (cot_ref[...].astype(F32) * (sig * (1.0 + pre_act * (1.0 - sig)))).astype(BF16)
    grad_ref[...] = dot(weight, pre_grad, ((1,), (1,))).astype(BF16)
    acc_ref[...] = dot(hidden, pre_grad, ((0,), (0,)))
    part = w0_ref.shape[0]

    def piece(j):
        return acc_ref[pl.ds(pl.multiple_of((q ^ j) * part, part), part), :]

    wsend_ref[:part] = piece(3)
    wsend_ref[part:] = piece(1)
    w2_ref[...] = piece(2)
    w0_ref[...] = piece(0)


def middle(keep, near, far, weight, cot, n_rep):
    rows, features = keep.shape
    part = features // n_rep
    return pl.pallas_call(
        middle_body,
        out_shape=[
            shape((rows, features), BF16),
            shape((features, rows), BF16),
            shape((2 * part, features), F32),
            shape((part, features), F32),
            shape((part, features), F32),
        ],
        in_specs=[WHOLE] * 5,
        out_specs=[WHOLE] * 5,
        scratch_shapes=[pltpu.VMEM((features, features), F32)],
        compiler_params=params(12 << 20),
        cost_estimate=pl.CostEstimate(
            flops=6 * rows * features * features, bytes_accessed=rows * features * 14, transcendentals=rows * features
        ),
        name="middle",
    )(keep, near, far, weight, cot)


def back_first_body(odd_ref, even_ref, adj_ref, w2_ref, w0_ref, got_ref, out_ref, w2_out, w0_out):
    rows = odd_ref.shape[1]
    part = w0_ref.shape[0]

    @pl.when(pl.program_id(0) == 0)
    def _():
        w2_out[...] = w2_ref[...] + got_ref[:part]
        w0_out[...] = w0_ref[...] + got_ref[part:]

    out_ref[...] = dot(odd_ref[...], adj_ref[:rows]) + dot(even_ref[...], adj_ref[rows:])


def back_first(odd, even, adj, w2, w0, got):
    rows, cols = adj.shape
    features = odd.shape[0]
    w_spec = pl.BlockSpec(w0.shape, lambda i: (0, 0))
    return pl.pallas_call(
        back_first_body,
        grid=(cols // COL_TILE,),
        out_shape=[shape((features, cols), F32), shape(w0.shape, F32), shape(w0.shape, F32)],
        in_specs=[
            pl.BlockSpec(odd.shape, lambda i: (0, 0)),
            pl.BlockSpec(even.shape, lambda i: (0, 0)),
            pl.BlockSpec((rows, COL_TILE), lambda i: (0, i)),
            w_spec,
            w_spec,
            pl.BlockSpec(got.shape, lambda i: (0, 0)),
        ],
        out_specs=[pl.BlockSpec((features, COL_TILE), lambda i: (0, i)), w_spec, w_spec],
        compiler_params=params(4 << 20),
        cost_estimate=pl.CostEstimate(
            flops=2 * rows * cols * features, bytes_accessed=adj.size * 2 + cols * features * 4, transcendentals=0
        ),
        name="back_first",
    )(odd, even, adj, w2, w0, got)


def back_second_body(
    odd_ref, even_ref, adj_ref, first_ref, w_ref, got_ref, o3_ref, o2_ref, o1_ref, o0_ref, w_out, acc_ref
):
    q = lax.axis_index("rep")

    @pl.when(pl.program_id(0) == 0)
    def _():
        w_out[...] = w_ref[...] + got_ref[...]

    rows = odd_ref.shape[1]
    acc_ref[...] = first_ref[...] + dot(odd_ref[...], adj_ref[:rows]) + dot(even_ref[...], adj_ref[rows:])
    part = o0_ref.shape[0]

    def piece(j):
        return acc_ref[pl.ds(pl.multiple_of((q ^ j) * part, part), part), :]

    o3_ref[...] = piece(3).astype(BF16)
    o2_ref[...] = piece(2)
    o1_ref[...] = piece(1).astype(BF16)
    o0_ref[...] = piece(0)


def back_second(odd, even, adj, first, w, got, n_rep):
    rows, cols = adj.shape
    features = odd.shape[0]
    part = features // n_rep
    per_piece = cols // n_rep // COL_TILE
    keep_spec = pl.BlockSpec((part, COL_TILE), lambda i: (0, i))
    w_spec = pl.BlockSpec(w.shape, lambda i: (0, 0))
    send_spec = pl.BlockSpec(
        (part, COL_TILE), lambda i: (0, (lax.div(i, per_piece) ^ 1) * per_piece + lax.rem(i, per_piece))
    )
    return pl.pallas_call(
        back_second_body,
        grid=(cols // COL_TILE,),
        out_shape=[shape((part, cols), dtype) for dtype in (BF16, F32, BF16, F32)] + [shape(w.shape, F32)],
        in_specs=[
            pl.BlockSpec(odd.shape, lambda i: (0, 0)),
            pl.BlockSpec(even.shape, lambda i: (0, 0)),
            pl.BlockSpec((rows, COL_TILE), lambda i: (0, i)),
            pl.BlockSpec((features, COL_TILE), lambda i: (0, i)),
            w_spec,
            w_spec,
        ],
        out_specs=[send_spec, keep_spec, send_spec, keep_spec, w_spec],
        scratch_shapes=[pltpu.VMEM((features, COL_TILE), F32)],
        compiler_params=params(6 << 20),
        cost_estimate=pl.CostEstimate(
            flops=2 * rows * cols * features, bytes_accessed=adj.size * 2 + cols * features * 7, transcendentals=0
        ),
        name="back_second",
    )(odd, even, adj, first, w, got)


def across_body(keep_ref, near_ref, w_ref, got_ref, out_ref, w_out):
    out_ref[...] = (keep_ref[...] + near_ref[...].astype(F32)).astype(BF16)
    w_out[...] = w_ref[...] + got_ref[...]


def across_sum(keep, near, w, got):
    return pl.pallas_call(
        across_body,
        out_shape=[shape(keep.shape, BF16), shape(w.shape, F32)],
        in_specs=[WHOLE] * 4,
        out_specs=[WHOLE] * 2,
        compiler_params=params(keep.size * 8),
        cost_estimate=pl.CostEstimate(flops=keep.size, bytes_accessed=keep.size * 8, transcendentals=0),
        name="across_sum",
    )(keep, near, w, got)


def split_body(own_ref, near_ref, far_ref, w_ref, got_ref, *outs, n_rep, n_hi):
    q = lax.axis_index("rep")
    *outs, w_out = outs
    w_out[...] = w_ref[...] + got_ref[...]
    width = outs[0].shape[1]
    for k, out in enumerate(outs):
        j, hi = (k % n_rep) ^ q, k // n_rep
        cols = pl.ds(pl.multiple_of((j * n_hi + hi) * width, width), width)
        far_cols = pl.ds(pl.multiple_of(((j ^ 2) * n_hi + hi) * width, width), width)
        total = own_ref[:, cols] + near_ref[:, cols].astype(F32) + far_ref[:, far_cols].astype(F32)
        out[...] = total.astype(out.dtype)


def split(own, near, far, w, got, n_row, n_rep):
    part, cols = own.shape
    width = cols // n_row
    return pl.pallas_call(
        functools.partial(split_body, n_rep=n_rep, n_hi=n_row // n_rep),
        out_shape=[shape((part, width), F32 if k == 0 else BF16) for k in range(n_row)] + [shape(w.shape, F32)],
        in_specs=[WHOLE] * 5,
        out_specs=[WHOLE] * (n_row + 1),
        compiler_params=params(own.size * 12),
        cost_estimate=pl.CostEstimate(flops=2 * own.size, bytes_accessed=own.size * 10, transcendentals=0),
        name="split",
    )(own, near, far, w, got)


def collect_body(*refs, n_row, n_rep, per_list, quarter, blk):
    lists = refs[:n_rep]
    messages = refs[n_rep : n_rep + n_row]
    w_ref, got_ref = refs[n_rep + n_row : n_rep + n_row + 2]
    outs = refs[n_rep + n_row + 2 : -2]
    w_out, acc_ref = refs[-2:]
    q = lax.axis_index("rep")
    acc_ref[...] = jnp.zeros(acc_ref.shape, F32)
    for k in range(n_row):
        j = (k % n_rep) ^ q
        for c in range(per_list):
            at = k // n_rep * per_list + c
            b = lists[0][at]
            for other in range(1, n_rep):
                b = jnp.where(j == other, lists[other][at], b)
            cell = (lax.div(b, quarter) ^ q) * quarter + lax.rem(b, quarter)
            cols = pl.ds(pl.multiple_of(cell * blk, blk), blk)
            acc_ref[:, cols] += messages[k][:, c * blk : (c + 1) * blk].astype(F32)
    width = outs[0].shape[1]
    for j, out in enumerate(outs):
        out[...] = acc_ref[:, j * width : (j + 1) * width].astype(out.dtype)
    w_out[...] = (w_ref[...] + got_ref[...]).astype(w_out.dtype)


def collect(lists, messages, w, got, per_list, row_blocks, blk, last):
    n_rep = len(lists)
    n_row = len(messages)
    part = messages[0].shape[0]
    quarter = row_blocks // n_rep
    body = functools.partial(
        collect_body, n_row=n_row, n_rep=n_rep, per_list=per_list, quarter=quarter, blk=blk
    )
    return pl.pallas_call(
        body,
        out_shape=[shape((part, quarter * blk), F32 if j == 0 else BF16) for j in range(n_rep)]
        + [shape(w.shape, BF16 if last else F32)],
        in_specs=[SMEM] * n_rep + [WHOLE] * (n_row + 2),
        out_specs=[WHOLE] * (n_rep + 1),
        scratch_shapes=[pltpu.VMEM((part, row_blocks * blk), F32)],
        compiler_params=params(4 << 20),
        cost_estimate=pl.CostEstimate(
            flops=part * row_blocks * blk, bytes_accessed=part * row_blocks * blk * 5, transcendentals=0
        ),
        name="collect",
    )(*lists, *messages, w, got)


def finish_body(*refs, n_rep, factor):
    grads = refs[:n_rep]
    weights = refs[n_rep : 2 * n_rep]
    node_ref, weight_ref, acc_ref = refs[2 * n_rep :]
    q = lax.axis_index("rep")
    part = grads[0].shape[0]
    for j in range(n_rep):
        rows = pl.ds(pl.multiple_of((q ^ j) * part, part), part)
        acc_ref[rows, :] = grads[j][...].astype(F32)
        weight_ref[rows, :] = weights[j][...].astype(F32) * factor
    node_ref[...] = acc_ref[...].T


def finish(grads, weights, factor):
    n_rep = len(grads)
    part, rows = grads[0].shape
    features = weights[0].shape[1]
    return pl.pallas_call(
        functools.partial(finish_body, n_rep=n_rep, factor=factor),
        out_shape=[shape((rows, part * n_rep), F32), shape((features, features), F32)],
        in_specs=[WHOLE] * (2 * n_rep),
        out_specs=[WHOLE] * 2,
        scratch_shapes=[pltpu.VMEM((part * n_rep, rows), F32)],
        compiler_params=params(6 << 20),
        cost_estimate=pl.CostEstimate(flops=0, bytes_accessed=rows * part * n_rep * 8, transcendentals=0),
        name="finish",
    )(*grads, *weights)


def local(
    node_features, weight, out_grad, blocks, block_rows, block_fetch, fetch_lists, block_count
):
    n_row = lax.axis_size("row")
    n_rep = lax.axis_size("rep")
    n_hi = n_row // n_rep
    band_rows, features = node_features.shape
    blk = blocks.shape[1]
    row_blocks = band_rows // blk
    per_list = fetch_lists.shape[2]

    def to_rep(x, j):
        return lax.ppermute(x, "rep", xor_perm(n_rep, j))

    def to_row(x, k):
        return lax.ppermute(x, "row", xor_perm(n_row, k))

    def spread(x, hi):
        perm = [
            (r * n_rep + q, (r ^ (hi * n_rep + q)) * n_rep + q) for r in range(n_row) for q in range(n_rep)
        ]
        return lax.ppermute(x, ("row", "rep"), perm)

    def after(x, *done):
        return lax.optimization_barrier((x, *done))[0]

    wanted = [spread(fetch_lists, hi) for hi in range(n_hi)]
    adj_far, adj_near = [
        densify(block_rows, block_fetch, block_count, blocks, half, n_row, n_rep, per_list, row_blocks)
        for half in range(2)
    ]
    *outgoing, own_list = pack(after(wanted, adj_far), node_features, per_list, blk)
    own = [spread(x, hi) for hi, x in enumerate(outgoing)]
    lists = [own_list] + [to_rep(own_list, j) for j in range(1, n_rep)]
    own = after(own, adj_near, lists)
    far = [to_rep(x, 2) for x in own]
    near = [to_rep(x, 1) for x in own]
    diag = [to_rep(x, 1) for x in far]
    pieces = own + near + far + diag

    send3, keep2 = forward(pieces, adj_far)
    across = (keep2 + to_rep(send3, 1).astype(F32)).astype(BF16)
    arrived = to_rep(across, 2)
    send1, keep0 = forward(pieces, after(adj_near, across))
    arrived = after(arrived, keep0)
    output, grad0, wsend, w2, w0 = middle(keep0, to_rep(send1, 1), arrived, weight, out_grad, n_rep)

    grad2 = to_rep(grad0, 2)
    grad1 = to_rep(grad0, 1)
    first, w2, w0 = back_first(grad1, grad0, adj_near, w2, w0, to_rep(wsend, 1))
    grad2 = after(grad2, first)
    grad3 = to_rep(grad2, 1)
    o3, o2, o1, o0, w = back_second(grad3, grad2, adj_far, first, w0, to_rep(w2, 2), n_rep)
    back_across, w = across_sum(o2, to_rep(o3, 1), w, to_row(w, 1))
    *messages, w = split(o0, to_rep(o1, 1), to_rep(back_across, 2), w, to_row(w, 2), n_row, n_rep)
    returned = [messages[0]] + [to_row(messages[k], k) for k in range(1, n_row)]
    *grads, w = collect(lists, returned, w, to_row(w, 4), per_list, row_blocks, blk, n_row == 8)

    step = 8
    while step < n_row:
        w = w + to_row(w, step)
        step *= 2
    w = w.astype(BF16)
    all_grads = [grads[0]] + [to_rep(grads[j], j) for j in range(1, n_rep)]
    all_w = [w] + [to_rep(w, j) for j in range(1, n_rep)]
    factor = float(n_row * band_rows) ** (-0.5)
    node_grad, weight_grad = finish(all_grads, all_w, factor)
    return (output, weight_grad, node_grad)


def solution(mesh):
    in_specs = (
        P("row", None),
        P(),
        P(("row", "rep"), None),
        P(("row", "rep"), None, None),
        P(("row", "rep")),
        P(("row", "rep")),
        P(("row", "rep"), None, None),
        P(("row", "rep")),
    )
    out_specs = (P(("row", "rep"), None), P(), P(("row", "rep"), None))
    return jax.shard_map(local, mesh=mesh, in_specs=in_specs, out_specs=out_specs, check_vma=False)
```

```python
import functools

import jax
import jax.numpy as jnp
from jax import lax
from jax.experimental import pallas as pl
from jax.experimental.pallas import tpu as pltpu
from jax.sharding import PartitionSpec as P

BF16 = jnp.bfloat16
F32 = jnp.float32
COL_CHUNK = 16
ROW_TILE = 256
COL_TILE = 512
WHOLE = pl.BlockSpec(memory_space=pltpu.VMEM)
SMEM = pl.BlockSpec(memory_space=pltpu.SMEM)
ANY = pl.BlockSpec(memory_space=pl.ANY)


def params(*parts):
    return pltpu.CompilerParams(vmem_limit_bytes=min(sum(parts) + (6 << 20), 62 << 20))


def shape(dims, dtype):
    return jax.ShapeDtypeStruct(tuple(dims), dtype)


def dot(a, b, dims=((1,), (0,))):
    return lax.dot_general(a, b, (dims, ((), ())), preferred_element_type=F32)


def xor_perm(count, offset):
    return [(i, i ^ offset) for i in range(count)]


def densify_body(
    rows_ref, fetch_ref, count_ref, blocks_ref, out_ref, head_ref, next_ref, *, n_rep, n_hi, per_list, quarter
):
    chunk, row_cell = pl.program_id(0), pl.program_id(1)
    slots, blk = blocks_ref.shape[0], blocks_ref.shape[1]
    all_cols = n_rep * n_hi * per_list

    @pl.when((chunk == 0) & (row_cell == 0))
    def _():
        r, q = lax.axis_index("row"), lax.axis_index("rep")

        @pl.loop(0, n_rep * quarter * all_cols, unroll=16)
        def _(cell):
            head_ref[cell] = -1

        def link(slot):
            row, fetch = rows_ref[slot], fetch_ref[slot]
            j = lax.div(row, quarter) ^ q
            k = lax.div(fetch, per_list) ^ r
            piece = (lax.rem(k, n_rep) ^ q) * n_hi + lax.div(k, n_rep)
            col = piece * per_list + lax.rem(fetch, per_list)
            cell = ((n_rep - 1 - j) * quarter + lax.rem(row, quarter)) * all_cols + col
            next_ref[slot] = head_ref[cell]
            head_ref[cell] = slot

        pl.loop(0, count_ref[0])(link)

    for col in range(COL_CHUNK):
        first = head_ref[row_cell * all_cols + chunk * COL_CHUNK + col]
        place = (slice(None), slice(col * blk, (col + 1) * blk))

        @pl.when(first < 0)
        def _():
            out_ref[place] = jnp.zeros((blk, blk), BF16)

        @pl.when(first >= 0)
        def _():
            second = next_ref[first]

            @pl.when(second < 0)
            def _():
                out_ref[place] = blocks_ref[first]

            @pl.when(second >= 0)
            def _():
                def more(carry):
                    slot, total = carry
                    return next_ref[slot], total + blocks_ref[slot].astype(F32)

                start = (second, blocks_ref[first].astype(F32))
                _, total = lax.while_loop(lambda carry: carry[0] >= 0, more, start)
                out_ref[place] = total.astype(BF16)


def densify(block_rows, block_fetch, block_count, blocks, n_row, n_rep, per_list, row_blocks):
    slots, blk, _ = blocks.shape
    cols = n_row * per_list * blk
    width = COL_CHUNK * blk
    body = functools.partial(
        densify_body,
        n_rep=n_rep,
        n_hi=n_row // n_rep,
        per_list=per_list,
        quarter=row_blocks // n_rep,
    )
    return pl.pallas_call(
        body,
        out_shape=shape((row_blocks * blk, cols), BF16),
        grid_spec=pltpu.PrefetchScalarGridSpec(
            num_scalar_prefetch=3,
            grid=(cols // width, row_blocks),
            in_specs=[WHOLE],
            out_specs=pl.BlockSpec((blk, width), lambda c, i, *_: (i, c)),
            scratch_shapes=[
                pltpu.SMEM((row_blocks * n_row * per_list,), jnp.int32),
                pltpu.SMEM((slots,), jnp.int32),
            ],
        ),
        compiler_params=params(12 << 20),
        cost_estimate=pl.CostEstimate(
            flops=slots * blk * blk, bytes_accessed=blocks.size * 2 + 2 * cols * row_blocks * blk, transcendentals=0
        ),
        name="densify",
    )(block_rows, block_fetch, block_count, blocks)


def pack_body(*refs, n_hi, per_list, blk):
    lists = refs[:n_hi]
    features = refs[n_hi]
    outs = refs[n_hi + 1 : 2 * n_hi + 1]
    own_list, sems = refs[2 * n_hi + 1 :]
    r = lax.axis_index("row")
    copies = []
    for hi in range(n_hi):
        for c in range(per_list):
            b = lists[hi][0, r, c]
            own_list[hi * per_list + c] = b
            copy = pltpu.make_async_copy(
                features.at[pl.ds(pl.multiple_of(b * blk, blk), blk)],
                outs[hi].at[pl.ds(c * blk, blk)],
                sems.at[hi * per_list + c],
            )
            copy.start()
            copies.append(copy)
    for copy in copies:
        copy.wait()


def pack(lists, features, per_list, blk):
    n_hi = len(lists)
    return pl.pallas_call(
        functools.partial(pack_body, n_hi=n_hi, per_list=per_list, blk=blk),
        out_shape=[shape((per_list * blk, features.shape[1]), BF16)] * n_hi + [shape((128,), jnp.int32)],
        in_specs=[SMEM] * n_hi + [pl.BlockSpec(memory_space=pltpu.HBM)],
        out_specs=[ANY] * n_hi + [SMEM],
        scratch_shapes=[pltpu.SemaphoreType.DMA((n_hi * per_list,))],
        compiler_params=params(0),
        name="pack",
    )(*lists, features)


def forward_body(*refs, n_pieces):
    pieces = refs[:n_pieces]
    adj_ref, send_ref, keep_ref = refs[n_pieces:]
    i = pl.program_id(0)
    depth = pieces[0].shape[0]
    total = dot(adj_ref[:, :depth], pieces[0][...])
    for n in range(1, n_pieces):
        total += dot(adj_ref[:, n * depth : (n + 1) * depth], pieces[n][...])

    half = pl.num_programs(0) // 2

    @pl.when(i < half)
    def _():
        send_ref[...] = total.astype(BF16)

    @pl.when(i >= half)
    def _():
        keep_ref[...] = total


def forward(pieces, adj, half_index):
    rows, cols = adj.shape[0] // 2, adj.shape[1]
    features = pieces[0].shape[1]
    tiles = rows // ROW_TILE
    half = tiles // 2
    return pl.pallas_call(
        functools.partial(forward_body, n_pieces=len(pieces)),
        grid=(tiles,),
        out_shape=[shape((rows // 2, features), BF16), shape((rows // 2, features), F32)],
        in_specs=[pl.BlockSpec(x.shape, lambda i: (0, 0)) for x in pieces]
        + [pl.BlockSpec((ROW_TILE, cols), lambda i: (i + half_index * tiles, 0))],
        out_specs=[
            pl.BlockSpec((ROW_TILE, features), lambda i: (jnp.minimum(i, half - 1), 0)),
            pl.BlockSpec((ROW_TILE, features), lambda i: (jnp.maximum(i - half, 0), 0)),
        ],
        compiler_params=params(ROW_TILE * cols * 4, cols * features * 4),
        cost_estimate=pl.CostEstimate(
            flops=2 * rows * cols * features, bytes_accessed=adj.size + cols * features * 2, transcendentals=0
        ),
        name="forward",
    )(*pieces, adj)


def middle_body(
    keep_ref, near_ref, far_ref, weight_ref, cot_ref, out_ref, grad_ref, wsend_ref, wkeep_ref, acc_ref, *, factor
):
    q = lax.axis_index("rep")
    hidden = (keep_ref[...] + near_ref[...].astype(F32) + far_ref[...].astype(F32)).astype(BF16)
    weight = weight_ref[...]
    pre_act = dot(hidden, weight)
    sig = jax.nn.sigmoid(pre_act)
    out_ref[...] = (pre_act * sig).astype(BF16)
    pre_grad = (cot_ref[...].astype(F32) * (sig * (1.0 + pre_act * (1.0 - sig)))).astype(BF16)
    grad_ref[...] = dot(weight, pre_grad, ((1,), (1,))).astype(BF16)
    acc_ref[...] = dot(hidden, pre_grad, ((0,), (0,))) * factor
    part = wkeep_ref.shape[0] // 2
    for j in range(4):
        out = wsend_ref if j & 1 else wkeep_ref
        at = j // 2 * part
        out[at : at + part] = acc_ref[pl.ds(pl.multiple_of((q ^ j) * part, part), part), :]


def middle(keep, near, far, weight, cot, factor):
    rows, features = keep.shape
    return pl.pallas_call(
        functools.partial(middle_body, factor=factor),
        out_shape=[
            shape((rows, features), BF16),
            shape((features, rows), BF16),
            shape((features // 2, features), F32),
            shape((features // 2, features), F32),
        ],
        in_specs=[WHOLE] * 5,
        out_specs=[WHOLE] * 4,
        scratch_shapes=[pltpu.VMEM((features, features), F32)],
        compiler_params=params(12 << 20),
        cost_estimate=pl.CostEstimate(
            flops=6 * rows * features * features, bytes_accessed=rows * features * 14, transcendentals=rows * features
        ),
        name="middle",
    )(keep, near, far, weight, cot)


def back_first_body(odd_ref, even_ref, adj_ref, wkeep_ref, got_ref, out_ref, wsend_out, wkeep_out):
    rows = odd_ref.shape[1]
    part = wsend_out.shape[0]

    @pl.when(pl.program_id(0) == 0)
    def _():
        mine = lax.rem(lax.axis_index("row"), 2) ^ lax.div(lax.axis_index("rep"), 2)
        for out, at in ((wkeep_out, mine), (wsend_out, 1 - mine)):
            rows_here = pl.ds(pl.multiple_of(at * part, part), part)
            out[...] = wkeep_ref[rows_here, :] + got_ref[rows_here, :]

    out_ref[...] = dot(odd_ref[...], adj_ref[:rows]) + dot(even_ref[...], adj_ref[rows:])


def back_first(odd, even, adj, wkeep, got):
    rows, cols = adj.shape[0] // 2, adj.shape[1]
    features = odd.shape[0]
    return pl.pallas_call(
        back_first_body,
        grid=(cols // COL_TILE,),
        out_shape=[shape((features, cols), F32)] + [shape((wkeep.shape[0] // 2, features), F32)] * 2,
        in_specs=[
            pl.BlockSpec(odd.shape, lambda i: (0, 0)),
            pl.BlockSpec(even.shape, lambda i: (0, 0)),
            pl.BlockSpec((rows, COL_TILE), lambda i: (1, i)),
            pl.BlockSpec(wkeep.shape, lambda i: (0, 0)),
            pl.BlockSpec(wkeep.shape, lambda i: (0, 0)),
        ],
        out_specs=[pl.BlockSpec((features, COL_TILE), lambda i: (0, i))]
        + [pl.BlockSpec((wkeep.shape[0] // 2, features), lambda i: (0, 0))] * 2,
        compiler_params=params(4 << 20),
        cost_estimate=pl.CostEstimate(
            flops=2 * rows * cols * features, bytes_accessed=adj.size + cols * features * 4, transcendentals=0
        ),
        name="back_first",
    )(odd, even, adj, wkeep, got)


def back_second_body(odd_ref, even_ref, adj_ref, first_ref, o3_ref, o2_ref, o1_ref, o0_ref, acc_ref):
    q = lax.axis_index("rep")
    rows = odd_ref.shape[1]
    acc_ref[...] = first_ref[...] + dot(odd_ref[...], adj_ref[:rows]) + dot(even_ref[...], adj_ref[rows:])
    part = o0_ref.shape[0]

    def piece(j):
        return acc_ref[pl.ds(pl.multiple_of((q ^ j) * part, part), part), :]

    o3_ref[...] = piece(3).astype(BF16)
    o2_ref[...] = piece(2)
    o1_ref[...] = piece(1).astype(BF16)
    o0_ref[...] = piece(0)


def back_second(odd, even, adj, first, n_rep):
    rows, cols = adj.shape[0] // 2, adj.shape[1]
    features = odd.shape[0]
    part = features // n_rep
    per_piece = cols // n_rep // COL_TILE
    keep_spec = pl.BlockSpec((part, COL_TILE), lambda i: (0, i))
    send_spec = pl.BlockSpec(
        (part, COL_TILE), lambda i: (0, (lax.div(i, per_piece) ^ 1) * per_piece + lax.rem(i, per_piece))
    )
    return pl.pallas_call(
        back_second_body,
        grid=(cols // COL_TILE,),
        out_shape=[shape((part, cols), dtype) for dtype in (BF16, F32, BF16, F32)],
        in_specs=[
            pl.BlockSpec(odd.shape, lambda i: (0, 0)),
            pl.BlockSpec(even.shape, lambda i: (0, 0)),
            pl.BlockSpec((rows, COL_TILE), lambda i: (0, i)),
            pl.BlockSpec((features, COL_TILE), lambda i: (0, i)),
        ],
        out_specs=[send_spec, keep_spec, send_spec, keep_spec],
        scratch_shapes=[pltpu.VMEM((features, COL_TILE), F32)],
        compiler_params=params(6 << 20),
        cost_estimate=pl.CostEstimate(
            flops=2 * rows * cols * features, bytes_accessed=adj.size + cols * features * 7, transcendentals=0
        ),
        name="back_second",
    )(odd, even, adj, first)


def across_body(keep_ref, near_ref, w_ref, got_ref, *outs, n_rep, n_hi):
    *outs, w_out = outs
    width = keep_ref.shape[1] // (n_rep * n_hi)
    for half, out in enumerate(outs):
        for piece in range(n_rep * n_hi // 2):
            j, hi = piece // (n_hi // 2), piece % (n_hi // 2) + half * n_hi // 2
            cols = slice((j * n_hi + hi) * width, (j * n_hi + hi + 1) * width)
            total = keep_ref[:, cols] + near_ref[:, cols].astype(F32)
            out[:, piece * width : (piece + 1) * width] = total.astype(BF16)
    w_out[...] = w_ref[...] + got_ref[...]


def across_sum(keep, near, w, got, n_rep, n_hi):
    part, cols = keep.shape
    return pl.pallas_call(
        functools.partial(across_body, n_rep=n_rep, n_hi=n_hi),
        out_shape=[shape((part, cols // 2), BF16)] * 2 + [shape(w.shape, F32)],
        in_specs=[WHOLE] * 4,
        out_specs=[WHOLE] * 3,
        compiler_params=params(keep.size * 8),
        cost_estimate=pl.CostEstimate(flops=keep.size, bytes_accessed=keep.size * 8, transcendentals=0),
        name="across_sum",
    )(keep, near, w, got)


def split_body(own_ref, near_ref, far_ref, *outs, n_rep, n_hi, half):
    q = lax.axis_index("rep")
    width = outs[0].shape[1]
    for i, out in enumerate(outs):
        low, hi = i % n_rep, i // n_rep
        j = low ^ q
        cols = pl.ds(pl.multiple_of((j * n_hi + hi + half * n_hi // 2) * width, width), width)
        far_cols = pl.ds(pl.multiple_of(((j ^ 2) * (n_hi // 2) + hi) * width, width), width)
        total = own_ref[:, cols] + near_ref[:, cols].astype(F32) + far_ref[:, far_cols].astype(F32)
        out[...] = total.astype(out.dtype)


def split(own, near, far, half, n_row, n_rep):
    part, cols = own.shape
    width = cols // n_row
    count = n_row // 2
    return pl.pallas_call(
        functools.partial(split_body, n_rep=n_rep, n_hi=n_row // n_rep, half=half),
        out_shape=[shape((part, width), F32 if half * count + i == 0 else BF16) for i in range(count)],
        in_specs=[WHOLE] * 3,
        out_specs=[WHOLE] * count,
        compiler_params=params(own.size * 10),
        cost_estimate=pl.CostEstimate(flops=own.size, bytes_accessed=own.size * 5, transcendentals=0),
        name=f"split_{half}",
    )(own, near, far)


def collect_body(*refs, n_row, n_rep, per_list, quarter, blk):
    lists = refs[:n_rep]
    messages = refs[n_rep : n_rep + n_row]
    outs = refs[n_rep + n_row : -1]
    acc_ref = refs[-1]
    q = lax.axis_index("rep")
    acc_ref[...] = jnp.zeros(acc_ref.shape, F32)
    for k in range(n_row):
        j = (k % n_rep) ^ q
        for c in range(per_list):
            at = k // n_rep * per_list + c
            b = lists[0][at]
            for other in range(1, n_rep):
                b = jnp.where(j == other, lists[other][at], b)
            cell = (lax.div(b, quarter) ^ q) * quarter + lax.rem(b, quarter)
            cols = pl.ds(pl.multiple_of(cell * blk, blk), blk)
            acc_ref[:, cols] += messages[k][:, c * blk : (c + 1) * blk].astype(F32)
    width = outs[0].shape[1]
    for j, out in enumerate(outs):
        out[...] = acc_ref[:, j * width : (j + 1) * width].astype(out.dtype)


def collect(lists, messages, per_list, row_blocks, blk):
    n_rep = len(lists)
    n_row = len(messages)
    part = messages[0].shape[0]
    quarter = row_blocks // n_rep
    body = functools.partial(
        collect_body, n_row=n_row, n_rep=n_rep, per_list=per_list, quarter=quarter, blk=blk
    )
    return pl.pallas_call(
        body,
        out_shape=[shape((part, quarter * blk), F32 if j == 0 else BF16) for j in range(n_rep)],
        in_specs=[SMEM] * n_rep + [WHOLE] * n_row,
        out_specs=[WHOLE] * n_rep,
        scratch_shapes=[pltpu.VMEM((part, row_blocks * blk), F32)],
        compiler_params=params(4 << 20),
        cost_estimate=pl.CostEstimate(
            flops=part * row_blocks * blk, bytes_accessed=part * row_blocks * blk * 5, transcendentals=0
        ),
        name="collect",
    )(*lists, *messages)


def finish_body(*refs, n_rep):
    grads = refs[:n_rep]
    weights = refs[n_rep : 2 * n_rep]
    node_ref, weight_ref, acc_ref = refs[2 * n_rep :]
    q = lax.axis_index("rep")
    part = grads[0].shape[0]
    first = lax.rem(q, 2) + 2 * lax.rem(lax.axis_index("row"), 2)
    for j in range(n_rep):
        acc_ref[pl.ds(pl.multiple_of((q ^ j) * part, part), part), :] = grads[j][...].astype(F32)
        weight_ref[pl.ds(pl.multiple_of((first ^ j) * part, part), part), :] = weights[j][...]
    node_ref[...] = acc_ref[...].T


def finish(grads, weights):
    n_rep = len(grads)
    part, rows = grads[0].shape
    features = weights[0].shape[1]
    return pl.pallas_call(
        functools.partial(finish_body, n_rep=n_rep),
        out_shape=[shape((rows, part * n_rep), F32), shape((features, features), F32)],
        in_specs=[WHOLE] * (2 * n_rep),
        out_specs=[WHOLE] * 2,
        scratch_shapes=[pltpu.VMEM((part * n_rep, rows), F32)],
        compiler_params=params(6 << 20),
        cost_estimate=pl.CostEstimate(flops=0, bytes_accessed=rows * part * n_rep * 8, transcendentals=0),
        name="finish",
    )(*grads, *weights)


def local(
    node_features, weight, out_grad, blocks, block_rows, block_fetch, fetch_lists, block_count
):
    n_row = lax.axis_size("row")
    n_rep = lax.axis_size("rep")
    n_hi = n_row // n_rep
    band_rows, features = node_features.shape
    blk = blocks.shape[1]
    row_blocks = band_rows // blk
    per_list = fetch_lists.shape[2]

    def to_rep(x, j):
        return lax.ppermute(x, "rep", xor_perm(n_rep, j))

    def to_row(x, k):
        return lax.ppermute(x, "row", xor_perm(n_row, k))

    def spread(x, hi):
        perm = [
            (r * n_rep + q, (r ^ (hi * n_rep + q)) * n_rep + q) for r in range(n_row) for q in range(n_rep)
        ]
        return lax.ppermute(x, ("row", "rep"), perm)

    def after(x, *done):
        return lax.optimization_barrier((x, *done))[0]

    wanted = [spread(fetch_lists, hi) for hi in range(n_hi)]
    *outgoing, own_list = pack(wanted, node_features, per_list, blk)
    own = [spread(x, hi) for hi, x in enumerate(outgoing)]
    adj = densify(
        block_rows, block_fetch, after(block_count, outgoing), blocks, n_row, n_rep, per_list, row_blocks
    )
    own[0] = after(own[0], adj)
    far = [to_rep(x, 2) for x in own]
    near = [to_rep(x, 1) for x in own]
    diag = [to_rep(x, 1) for x in far]
    pieces = own + near + far + diag

    send3, keep2 = forward(pieces, adj, 0)
    across = (keep2 + to_rep(send3, 1).astype(F32)).astype(BF16)
    arrived = to_rep(across, 2)
    send1, keep0 = forward(pieces, after(adj, across), 1)
    own_list = after(own_list, keep0)
    lists = [own_list] + [to_rep(own_list, j) for j in range(1, n_rep)]
    arrived = after(arrived, keep0, lists)
    factor = float(n_row * band_rows) ** (-0.5)
    output, grad0, wsend, wkeep = middle(keep0, to_rep(send1, 1), arrived, weight, out_grad, factor)

    grad2 = to_rep(grad0, 2)
    grad1 = to_rep(grad0, 1)
    first, wsend, wkeep = back_first(grad1, grad0, adj, wkeep, to_rep(wsend, 1))
    grad2 = after(grad2, first)
    grad3 = to_rep(grad2, 1)
    o3, o2, o1, o0 = back_second(grad3, grad2, adj, first, n_rep)
    to_low, to_high, w = across_sum(o2, to_rep(o3, 1), wkeep, to_row(wsend, 1), n_rep, n_hi)
    o1 = to_rep(o1, 1)
    from_high = to_rep(to_high, 2)
    from_low = to_rep(to_low, 2)
    w = w + to_row(w, 2)
    got = to_row(w, 4)
    high = split(o0, o1, from_high, 1, n_row, n_rep)
    half = n_row // 2
    back_high = [to_row(x, half + i) for i, x in enumerate(high)]
    w = w + after(got, high)
    step = 8
    while step < n_row:
        w = w + to_row(w, step)
        step *= 2
    low = split(o0, o1, after(from_low, back_high[:-1]), 0, n_row, n_rep)
    returned = [low[0]] + [to_row(low[i], i) for i in range(1, half)] + back_high
    w = w + to_rep(w, 2)
    grads = collect(lists, after(returned, w), per_list, row_blocks, blk)
    other = to_row(w, 1)
    weights = [w, to_rep(w, 1), other, to_rep(other, 1)]
    node_grad, weight_grad = finish(
        [grads[0]] + [to_rep(grads[j], j) for j in range(1, n_rep)], weights
    )
    return (output, weight_grad, node_grad)


def solution(mesh):
    in_specs = (
        P("row", None),
        P(),
        P(("row", "rep"), None),
        P(("row", "rep"), None, None),
        P(("row", "rep")),
        P(("row", "rep")),
        P(("row", "rep"), None, None),
        P(("row", "rep")),
    )
    out_specs = (P(("row", "rep"), None), P(), P(("row", "rep"), None))
    return jax.shard_map(local, mesh=mesh, in_specs=in_specs, out_specs=out_specs, check_vma=False)
```

```python
import functools

import jax
import jax.numpy as jnp
from jax import lax
from jax.experimental import pallas as pl
from jax.experimental.pallas import tpu as pltpu
from jax.sharding import PartitionSpec as P

BF16 = jnp.bfloat16
F32 = jnp.float32
COL_CHUNK = 16
ROW_TILE = 256
COL_TILE = 512
WHOLE = pl.BlockSpec(memory_space=pltpu.VMEM)
SMEM = pl.BlockSpec(memory_space=pltpu.SMEM)
ANY = pl.BlockSpec(memory_space=pl.ANY)


def params(*parts):
    return pltpu.CompilerParams(vmem_limit_bytes=min(sum(parts) + (6 << 20), 62 << 20))


WIDE = pltpu.CompilerParams(vmem_limit_bytes=46 << 20)


def shape(dims, dtype):
    return jax.ShapeDtypeStruct(tuple(dims), dtype)


def dot(a, b, dims=((1,), (0,))):
    return lax.dot_general(a, b, (dims, ((), ())), preferred_element_type=F32)


def xor_perm(count, offset):
    return [(i, i ^ offset) for i in range(count)]


def div_rem(x, n):
    if n & (n - 1) == 0:
        return x >> (n.bit_length() - 1), x & (n - 1)
    return lax.div(x, n), lax.rem(x, n)


def densify_body(
    rows_ref, fetch_ref, count_ref, blocks_ref, out_ref, held, first, second, older, wide_at, wide_cell, wide_next, sem,
    *, n_rep, n_hi, per_list, quarter
):
    chunk, row_cell = pl.program_id(0), pl.program_id(1)
    slots, blk = blocks_ref.shape[0], blocks_ref.shape[1]
    all_cols = n_rep * n_hi * per_list
    chunks = all_cols // COL_CHUNK
    deep = n_hi // 2

    @pl.when((chunk == 0) & (row_cell == 0))
    def _():
        r, q = lax.axis_index("row"), lax.axis_index("rep")
        copy = pltpu.make_async_copy(blocks_ref, held.at[pl.ds(0, slots)], sem)
        copy.start()
        held[slots] = jnp.zeros((blk, blk), BF16)

        @pl.loop(0, n_rep * quarter * all_cols, unroll=16)
        def _(cell):
            first[cell] = slots
            second[cell] = slots

        @pl.loop(0, n_rep * quarter * chunks, unroll=16)
        def _(at):
            wide_at[at] = -1

        def link(slot, wide):
            row_high, row_low = div_rem(rows_ref[slot], quarter)
            source, c = div_rem(fetch_ref[slot], per_list)
            hi, low = div_rem(source ^ r, n_rep)
            half, hi = div_rem(hi, deep)
            row = (n_rep - 1 - (row_high ^ q)) * quarter + row_low
            col = ((half * n_rep + (low ^ q)) * deep + hi) * per_list + c
            cell = row * all_cols + col
            at = row * chunks + div_rem(col, COL_CHUNK)[0]
            one, two, begin = first[cell], second[cell], wide_at[at]
            first[cell] = slot
            second[cell] = one
            older[slot] = one
            full = two != slots
            wide_cell[wide] = cell
            wide_next[wide] = begin
            wide_at[at] = jnp.where(full, wide, begin)
            return wide + full.astype(jnp.int32)

        lax.fori_loop(0, count_ref[0], link, jnp.int32(0))
        copy.wait()

    for col in range(COL_CHUNK):
        cell = row_cell * all_cols + chunk * COL_CHUNK + col
        out_ref[:, col * blk : (col + 1) * blk] = held[first[cell]] + held[second[cell]]

    def redo(wide):
        cell = wide_cell[wide]

        def more(carry):
            slot, total = carry
            return older[slot], total + held[slot].astype(F32)

        _, total = lax.while_loop(lambda carry: carry[0] < slots, more, (first[cell], jnp.zeros((blk, blk), F32)))
        col = cell - row_cell * all_cols - chunk * COL_CHUNK
        out_ref[:, pl.ds(pl.multiple_of(col * blk, blk), blk)] = total.astype(BF16)
        return wide_next[wide]

    lax.while_loop(lambda wide: wide >= 0, redo, wide_at[row_cell * chunks + chunk])


def densify(block_rows, block_fetch, block_count, blocks, n_row, n_rep, per_list, row_blocks):
    slots, blk, _ = blocks.shape
    all_cols = n_row * per_list
    width = COL_CHUNK * blk
    body = functools.partial(
        densify_body,
        n_rep=n_rep,
        n_hi=n_row // n_rep,
        per_list=per_list,
        quarter=row_blocks // n_rep,
    )
    smem = [row_blocks * all_cols] * 2 + [slots, row_blocks * all_cols // COL_CHUNK, slots, slots]
    return pl.pallas_call(
        body,
        out_shape=shape((row_blocks * blk, all_cols * blk), BF16),
        grid_spec=pltpu.PrefetchScalarGridSpec(
            num_scalar_prefetch=3,
            grid=(all_cols // COL_CHUNK, row_blocks),
            in_specs=[pl.BlockSpec(memory_space=pltpu.HBM)],
            out_specs=pl.BlockSpec((blk, width), lambda c, i, *_: (i, c)),
            scratch_shapes=[pltpu.VMEM((slots + 1, blk, blk), BF16)]
            + [pltpu.SMEM((n,), jnp.int32) for n in smem]
            + [pltpu.SemaphoreType.DMA],
        ),
        compiler_params=pltpu.CompilerParams(vmem_limit_bytes=52 << 20),
        cost_estimate=pl.CostEstimate(
            flops=slots * blk * blk,
            bytes_accessed=blocks.size * 2 + 2 * all_cols * row_blocks * blk * blk,
            transcendentals=0,
        ),
        name="densify",
    )(block_rows, block_fetch, block_count, blocks)


def pack_body(*refs, n_hi, per_list, blk):
    lists = refs[:n_hi]
    features = refs[n_hi]
    outs = refs[n_hi + 1 : 2 * n_hi + 1]
    own_list, sems = refs[2 * n_hi + 1 :]
    r = lax.axis_index("row")
    copies = []
    for hi in range(n_hi):
        for c in range(per_list):
            b = lists[hi][0, r, c]
            own_list[hi * per_list + c] = b
            copy = pltpu.make_async_copy(
                features.at[pl.ds(pl.multiple_of(b * blk, blk), blk)],
                outs[hi].at[pl.ds(c * blk, blk)],
                sems.at[hi * per_list + c],
            )
            copy.start()
            copies.append(copy)
    for copy in copies:
        copy.wait()


def pack(lists, features, per_list, blk):
    n_hi = len(lists)
    return pl.pallas_call(
        functools.partial(pack_body, n_hi=n_hi, per_list=per_list, blk=blk),
        out_shape=[shape((per_list * blk, features.shape[1]), BF16)] * n_hi + [shape((128,), jnp.int32)],
        in_specs=[SMEM] * n_hi + [pl.BlockSpec(memory_space=pltpu.HBM)],
        out_specs=[ANY] * n_hi + [SMEM],
        scratch_shapes=[pltpu.SemaphoreType.DMA((n_hi * per_list,))],
        compiler_params=params(0),
        name="pack",
    )(*lists, features)


def forward_body(*refs, n_pieces):
    pieces = refs[:n_pieces]
    adj_ref, send_ref, keep_ref = refs[n_pieces:]
    i = pl.program_id(0)
    depth = pieces[0].shape[0]
    total = dot(adj_ref[:, :depth], pieces[0][...])
    for n in range(1, n_pieces):
        total += dot(adj_ref[:, n * depth : (n + 1) * depth], pieces[n][...])

    half = pl.num_programs(0) // 2

    @pl.when(i < half)
    def _():
        send_ref[...] = total.astype(BF16)

    @pl.when(i >= half)
    def _():
        keep_ref[...] = total


def forward(pieces, adj, half_index):
    rows, cols = adj.shape[0] // 2, adj.shape[1]
    features = pieces[0].shape[1]
    tiles = rows // ROW_TILE
    half = tiles // 2
    return pl.pallas_call(
        functools.partial(forward_body, n_pieces=len(pieces)),
        grid=(tiles,),
        out_shape=[shape((rows // 2, features), BF16), shape((rows // 2, features), F32)],
        in_specs=[pl.BlockSpec(x.shape, lambda i: (0, 0)) for x in pieces]
        + [pl.BlockSpec((ROW_TILE, cols), lambda i: (i + half_index * tiles, 0))],
        out_specs=[
            pl.BlockSpec((ROW_TILE, features), lambda i: (jnp.minimum(i, half - 1), 0)),
            pl.BlockSpec((ROW_TILE, features), lambda i: (jnp.maximum(i - half, 0), 0)),
        ],
        compiler_params=WIDE,
        cost_estimate=pl.CostEstimate(
            flops=2 * rows * cols * features, bytes_accessed=adj.size + cols * features * 2, transcendentals=0
        ),
        name="forward",
    )(*pieces, adj)


def middle_body(
    keep_ref, near_ref, far_ref, weight_ref, cot_ref, out_ref, grad_ref, wsend_ref, wkeep_ref, acc_ref, *, factor
):
    q = lax.axis_index("rep")
    hidden = (keep_ref[...] + near_ref[...].astype(F32) + far_ref[...].astype(F32)).astype(BF16)
    weight = weight_ref[...]
    pre_act = dot(hidden, weight)
    sig = jax.nn.sigmoid(pre_act)
    out_ref[...] = (pre_act * sig).astype(BF16)
    pre_grad = (cot_ref[...].astype(F32) * (sig * (1.0 + pre_act * (1.0 - sig)))).astype(BF16)
    grad_ref[...] = dot(weight, pre_grad, ((1,), (1,))).astype(BF16)
    acc_ref[...] = dot(hidden, pre_grad, ((0,), (0,))) * factor
    part = wkeep_ref.shape[0] // 2
    for j in range(4):
        out = wsend_ref if j & 1 else wkeep_ref
        at = j // 2 * part
        out[at : at + part] = acc_ref[pl.ds(pl.multiple_of((q ^ j) * part, part), part), :]


def middle(keep, near, far, weight, cot, factor):
    rows, features = keep.shape
    return pl.pallas_call(
        functools.partial(middle_body, factor=factor),
        out_shape=[
            shape((rows, features), BF16),
            shape((features, rows), BF16),
            shape((features // 2, features), F32),
            shape((features // 2, features), F32),
        ],
        in_specs=[WHOLE] * 5,
        out_specs=[WHOLE] * 4,
        scratch_shapes=[pltpu.VMEM((features, features), F32)],
        compiler_params=params(12 << 20),
        cost_estimate=pl.CostEstimate(
            flops=6 * rows * features * features, bytes_accessed=rows * features * 14, transcendentals=rows * features
        ),
        name="middle",
    )(keep, near, far, weight, cot)


def back_first_body(odd_ref, even_ref, adj_ref, wkeep_ref, got_ref, out_ref, wsend_out, wkeep_out):
    rows = odd_ref.shape[1]
    part = wsend_out.shape[0]

    @pl.when(pl.program_id(0) == 0)
    def _():
        mine = lax.rem(lax.axis_index("row"), 2) ^ lax.div(lax.axis_index("rep"), 2)
        for out, at in ((wkeep_out, mine), (wsend_out, 1 - mine)):
            rows_here = pl.ds(pl.multiple_of(at * part, part), part)
            out[...] = wkeep_ref[rows_here, :] + got_ref[rows_here, :]

    out_ref[...] = dot(odd_ref[...], adj_ref[:rows]) + dot(even_ref[...], adj_ref[rows:])


def back_first(odd, even, adj, wkeep, got):
    rows, cols = adj.shape[0] // 2, adj.shape[1]
    features = odd.shape[0]
    return pl.pallas_call(
        back_first_body,
        grid=(cols // COL_TILE,),
        out_shape=[shape((features, cols), F32)] + [shape((wkeep.shape[0] // 2, features), F32)] * 2,
        in_specs=[
            pl.BlockSpec(odd.shape, lambda i: (0, 0)),
            pl.BlockSpec(even.shape, lambda i: (0, 0)),
            pl.BlockSpec((rows, COL_TILE), lambda i: (1, i)),
            pl.BlockSpec(wkeep.shape, lambda i: (0, 0)),
            pl.BlockSpec(wkeep.shape, lambda i: (0, 0)),
        ],
        out_specs=[pl.BlockSpec((features, COL_TILE), lambda i: (0, i))]
        + [pl.BlockSpec((wkeep.shape[0] // 2, features), lambda i: (0, 0))] * 2,
        compiler_params=WIDE,
        cost_estimate=pl.CostEstimate(
            flops=2 * rows * cols * features, bytes_accessed=adj.size + cols * features * 4, transcendentals=0
        ),
        name="back_first",
    )(odd, even, adj, wkeep, got)


def back_second_body(odd_ref, even_ref, adj_ref, first_ref, send_ref, keep_ref, acc_ref):
    q = lax.axis_index("rep")
    rows = odd_ref.shape[1]
    acc_ref[...] = first_ref[...] + dot(odd_ref[...], adj_ref[:rows]) + dot(even_ref[...], adj_ref[rows:])
    part = send_ref.shape[0] // 2
    for j in range(4):
        out = send_ref if j & 1 else keep_ref
        at = (3 - j) // 2 * part
        piece = acc_ref[pl.ds(pl.multiple_of((q ^ j) * part, part), part), :]
        out[at : at + part] = piece.astype(out.dtype)


def back_second(odd, even, adj, first, half, n_rep, per_piece):
    rows, cols = adj.shape[0] // 2, adj.shape[1] // 2
    features = odd.shape[0]
    width = cols // n_rep // per_piece
    tiles = cols // width
    return pl.pallas_call(
        back_second_body,
        grid=(tiles,),
        out_shape=[shape((features // 2, cols), BF16), shape((features // 2, cols), F32)],
        in_specs=[
            pl.BlockSpec(odd.shape, lambda i: (0, 0)),
            pl.BlockSpec(even.shape, lambda i: (0, 0)),
            pl.BlockSpec((rows, width), lambda i: (0, i + half * tiles)),
            pl.BlockSpec((features, width), lambda i: (0, i + half * tiles)),
        ],
        out_specs=[
            pl.BlockSpec(
                (features // 2, width), lambda i: (0, (lax.div(i, per_piece) ^ 1) * per_piece + lax.rem(i, per_piece))
            ),
            pl.BlockSpec((features // 2, width), lambda i: (0, i)),
        ],
        scratch_shapes=[pltpu.VMEM((features, width), F32)],
        compiler_params=WIDE,
        cost_estimate=pl.CostEstimate(
            flops=2 * rows * cols * features, bytes_accessed=rows * cols * 2 + cols * features * 7, transcendentals=0
        ),
        name=f"back_second_{half}",
    )(odd, even, adj, first)


def split_body(own_ref, near_ref, far_ref, *outs, n_rep, deep):
    q = lax.axis_index("rep")
    part, width = outs[0].shape
    for i, out in enumerate(outs):
        low, hi = i % n_rep, i // n_rep
        j = low ^ q
        cols = pl.ds(pl.multiple_of((j * deep + hi) * width, width), width)
        far_cols = pl.ds(pl.multiple_of(((j ^ 2) * deep + hi) * width, width), width)
        total = own_ref[part:, cols] + near_ref[part:, cols].astype(F32) + far_ref[:, far_cols].astype(F32)
        out[...] = total.astype(out.dtype)


def split(own, near, far, half, n_rep, deep):
    part, cols = far.shape
    count = n_rep * deep
    return pl.pallas_call(
        functools.partial(split_body, n_rep=n_rep, deep=deep),
        out_shape=[shape((part, cols // count), F32 if half + i == 0 else BF16) for i in range(count)],
        in_specs=[WHOLE] * 3,
        out_specs=[WHOLE] * count,
        compiler_params=params(own.size * 10),
        cost_estimate=pl.CostEstimate(flops=own.size, bytes_accessed=own.size * 5, transcendentals=0),
        name=f"split_{half}",
    )(own, near, far)


def collect_body(*refs, n_row, n_rep, per_list, quarter, blk):
    lists = refs[:n_rep]
    messages = refs[n_rep : n_rep + n_row]
    outs = refs[n_rep + n_row : -1]
    acc_ref = refs[-1]
    q = lax.axis_index("rep")
    acc_ref[...] = jnp.zeros(acc_ref.shape, F32)
    for k in range(n_row):
        j = (k % n_rep) ^ q
        for c in range(per_list):
            at = k // n_rep * per_list + c
            b = lists[0][at]
            for other in range(1, n_rep):
                b = jnp.where(j == other, lists[other][at], b)
            cell = (lax.div(b, quarter) ^ q) * quarter + lax.rem(b, quarter)
            cols = pl.ds(pl.multiple_of(cell * blk, blk), blk)
            acc_ref[:, cols] += messages[k][:, c * blk : (c + 1) * blk].astype(F32)
    width = outs[0].shape[1]
    for j, out in enumerate(outs):
        out[...] = acc_ref[:, j * width : (j + 1) * width].astype(out.dtype)


def collect(lists, messages, per_list, row_blocks, blk):
    n_rep = len(lists)
    n_row = len(messages)
    part = messages[0].shape[0]
    quarter = row_blocks // n_rep
    body = functools.partial(
        collect_body, n_row=n_row, n_rep=n_rep, per_list=per_list, quarter=quarter, blk=blk
    )
    return pl.pallas_call(
        body,
        out_shape=[shape((part, quarter * blk), F32 if j == 0 else BF16) for j in range(n_rep)],
        in_specs=[SMEM] * n_rep + [WHOLE] * n_row,
        out_specs=[WHOLE] * n_rep,
        scratch_shapes=[pltpu.VMEM((part, row_blocks * blk), F32)],
        compiler_params=params(4 << 20),
        cost_estimate=pl.CostEstimate(
            flops=part * row_blocks * blk, bytes_accessed=part * row_blocks * blk * 5, transcendentals=0
        ),
        name="collect",
    )(*lists, *messages)


def finish_body(*refs, n_rep):
    grads = refs[:n_rep]
    weights = refs[n_rep : 2 * n_rep]
    node_ref, weight_ref, acc_ref = refs[2 * n_rep :]
    q = lax.axis_index("rep")
    part = grads[0].shape[0]
    first = lax.rem(q, 2) + 2 * lax.rem(lax.axis_index("row"), 2)
    for j in range(n_rep):
        acc_ref[pl.ds(pl.multiple_of((q ^ j) * part, part), part), :] = grads[j][...].astype(F32)
        weight_ref[pl.ds(pl.multiple_of((first ^ j) * part, part), part), :] = weights[j][...]
    node_ref[...] = acc_ref[...].T


def finish(grads, weights):
    n_rep = len(grads)
    part, rows = grads[0].shape
    features = weights[0].shape[1]
    return pl.pallas_call(
        functools.partial(finish_body, n_rep=n_rep),
        out_shape=[shape((rows, part * n_rep), F32), shape((features, features), F32)],
        in_specs=[WHOLE] * (2 * n_rep),
        out_specs=[WHOLE] * 2,
        scratch_shapes=[pltpu.VMEM((part * n_rep, rows), F32)],
        compiler_params=params(6 << 20),
        cost_estimate=pl.CostEstimate(flops=0, bytes_accessed=rows * part * n_rep * 8, transcendentals=0),
        name="finish",
    )(*grads, *weights)


def local(
    node_features, weight, out_grad, blocks, block_rows, block_fetch, fetch_lists, block_count
):
    n_row = lax.axis_size("row")
    n_rep = lax.axis_size("rep")
    n_hi = n_row // n_rep
    band_rows, features = node_features.shape
    blk = blocks.shape[1]
    row_blocks = band_rows // blk
    per_list = fetch_lists.shape[2]

    def to_rep(x, j):
        return lax.ppermute(x, "rep", xor_perm(n_rep, j))

    def to_row(x, k):
        return lax.ppermute(x, "row", xor_perm(n_row, k))

    def spread(x, hi):
        perm = [
            (r * n_rep + q, (r ^ (hi * n_rep + q)) * n_rep + q) for r in range(n_row) for q in range(n_rep)
        ]
        return lax.ppermute(x, ("row", "rep"), perm)

    def after(x, *done):
        return lax.optimization_barrier((x, *done))[0]

    wanted = [spread(fetch_lists, hi) for hi in range(n_hi)]
    *outgoing, own_list = pack(wanted, node_features, per_list, blk)
    own = [spread(x, hi) for hi, x in enumerate(outgoing)]
    adj = densify(
        block_rows, block_fetch, after(block_count, outgoing), blocks, n_row, n_rep, per_list, row_blocks
    )
    own[0] = after(own[0], adj)
    far = [to_rep(x, 2) for x in own]
    near = [to_rep(x, 1) for x in own]
    diag = [to_rep(x, 1) for x in far]
    deep = n_hi // 2
    by_rep = [own, near, far, diag]
    pieces = [by_rep[j][half * deep + i] for half in range(2) for j in range(n_rep) for i in range(deep)]

    send3, keep2 = forward(pieces, adj, 0)
    across = (keep2 + to_rep(send3, 1).astype(F32)).astype(BF16)
    arrived = to_rep(across, 2)
    send1, keep0 = forward(pieces, after(adj, across), 1)
    own_list = after(own_list, keep0)
    lists = [own_list] + [to_rep(own_list, j) for j in range(1, n_rep)]
    arrived = after(arrived, keep0, lists)
    factor = float(n_row * band_rows) ** (-0.5)
    output, grad0, wsend, wkeep = middle(keep0, to_rep(send1, 1), arrived, weight, out_grad, factor)

    grad2 = to_rep(grad0, 2)
    grad1 = to_rep(grad0, 1)
    first, wsend, wkeep = back_first(grad1, grad0, adj, wkeep, to_rep(wsend, 1))
    w = wkeep + to_row(wsend, 1)
    grad2 = after(grad2, first)
    grad3 = after(to_rep(grad2, 1), w)
    got = to_row(w, 2)
    send_high, keep_high = back_second(grad3, grad2, adj, first, 1, n_rep, deep)
    near_high = to_rep(send_high, 1)
    send_low, keep_low = back_second(grad3, grad2, adj, after(first, send_high), 0, n_rep, deep)
    near_low = to_rep(send_low, 1)
    part = features // n_rep

    def across_sum(keep, near):
        return (keep[:part] + near[:part].astype(F32)).astype(BF16)

    far_high = to_rep(across_sum(keep_high, after(near_high, send_low)), 2)
    far_low = to_rep(across_sum(keep_low, near_low), 2)
    w = w + got
    got = to_row(w, 4)
    high = split(keep_high, near_high, far_high, 1, n_rep, deep)
    half_rows = n_row // 2
    back_high = [to_row(x, half_rows + i) for i, x in enumerate(high)]
    w = w + after(got, high)
    step = 8
    while step < n_row:
        w = w + to_row(w, step)
        step *= 2
    got = to_rep(w, 2)
    low = split(keep_low, near_low, after(far_low, back_high[:-1]), 0, n_rep, deep)
    w = w + after(got, low)
    returned = [low[0]] + [to_row(low[i], i) for i in range(1, half_rows)] + back_high
    grads = collect(lists, after(returned, w), per_list, row_blocks, blk)
    other = to_row(w, 1)
    weights = [w, to_rep(w, 1), other, to_rep(other, 1)]
    node_grad, weight_grad = finish(
        [grads[0]] + [to_rep(grads[j], j) for j in range(1, n_rep)], weights
    )
    return (output, weight_grad, node_grad)


def solution(mesh):
    in_specs = (
        P("row", None),
        P(),
        P(("row", "rep"), None),
        P(("row", "rep"), None, None),
        P(("row", "rep")),
        P(("row", "rep")),
        P(("row", "rep"), None, None),
        P(("row", "rep")),
    )
    out_specs = (P(("row", "rep"), None), P(), P(("row", "rep"), None))
    return jax.shard_map(local, mesh=mesh, in_specs=in_specs, out_specs=out_specs, check_vma=False)
```

```python
import functools

import jax
import jax.numpy as jnp
from jax import lax
from jax.experimental import pallas as pl
from jax.experimental.pallas import tpu as pltpu
from jax.sharding import PartitionSpec as P

BF16 = jnp.bfloat16
F32 = jnp.float32
COL_CHUNK = 16
ROW_TILE = 256
COL_TILE = 512
WHOLE = pl.BlockSpec(memory_space=pltpu.VMEM)
SMEM = pl.BlockSpec(memory_space=pltpu.SMEM)
ANY = pl.BlockSpec(memory_space=pl.ANY)


def params(*parts):
    return pltpu.CompilerParams(vmem_limit_bytes=min(sum(parts) + (6 << 20), 62 << 20))


def shape(dims, dtype):
    return jax.ShapeDtypeStruct(tuple(dims), dtype)


def dot(a, b, dims=((1,), (0,))):
    return lax.dot_general(a, b, (dims, ((), ())), preferred_element_type=F32)


def xor_perm(count, offset):
    return [(i, i ^ offset) for i in range(count)]


def div_rem(x, n):
    if n & (n - 1) == 0:
        return x >> (n.bit_length() - 1), x & (n - 1)
    return lax.div(x, n), lax.rem(x, n)


def densify_body(
    rows_ref, fetch_ref, count_ref, held, out_ref, first, second, older, wide_at, wide_cell, wide_next,
    *, n_rep, n_hi, per_list, quarter
):
    chunk, row_cell = pl.program_id(0), pl.program_id(1)
    slots, blk = held.shape[0], held.shape[1]
    all_cols = n_rep * n_hi * per_list
    chunks = all_cols // COL_CHUNK
    deep = n_hi // 2

    @pl.when((chunk == 0) & (row_cell == 0))
    def _():
        r, q = lax.axis_index("row"), lax.axis_index("rep")
        @pl.loop(0, n_rep * quarter * all_cols, unroll=16)
        def _(cell):
            first[cell] = slots
            second[cell] = slots

        @pl.loop(0, n_rep * quarter * chunks, unroll=16)
        def _(at):
            wide_at[at] = -1

        def link(slot, wide):
            row_high, row_low = div_rem(rows_ref[slot], quarter)
            source, c = div_rem(fetch_ref[slot], per_list)
            hi, low = div_rem(source ^ r, n_rep)
            half, hi = div_rem(hi, deep)
            row = (n_rep - 1 - (row_high ^ q)) * quarter + row_low
            col = ((half * n_rep + (low ^ q)) * deep + hi) * per_list + c
            cell = row * all_cols + col
            at = row * chunks + div_rem(col, COL_CHUNK)[0]
            one, two, begin = first[cell], second[cell], wide_at[at]
            first[cell] = slot
            second[cell] = one
            older[slot] = one
            full = two != slots
            wide_cell[wide] = cell
            wide_next[wide] = begin
            wide_at[at] = jnp.where(full, wide, begin)
            return wide + full.astype(jnp.int32)

        lax.fori_loop(0, count_ref[0], link, jnp.int32(0))

    zero = jnp.zeros((blk, blk), BF16)

    def block(slot):
        return jnp.where(slot < slots, held[jnp.minimum(slot, slots - 1)], zero)

    for col in range(COL_CHUNK):
        cell = row_cell * all_cols + chunk * COL_CHUNK + col
        out_ref[:, col * blk : (col + 1) * blk] = block(first[cell]) + block(second[cell])

    def redo(wide):
        cell = wide_cell[wide]

        def more(carry):
            slot, total = carry
            return older[slot], total + held[slot].astype(F32)

        _, total = lax.while_loop(lambda carry: carry[0] < slots, more, (first[cell], jnp.zeros((blk, blk), F32)))
        col = cell - row_cell * all_cols - chunk * COL_CHUNK
        out_ref[:, pl.ds(pl.multiple_of(col * blk, blk), blk)] = total.astype(BF16)
        return wide_next[wide]

    lax.while_loop(lambda wide: wide >= 0, redo, wide_at[row_cell * chunks + chunk])


def densify(block_rows, block_fetch, block_count, blocks, n_row, n_rep, per_list, row_blocks):
    slots, blk, _ = blocks.shape
    all_cols = n_row * per_list
    width = COL_CHUNK * blk
    body = functools.partial(
        densify_body,
        n_rep=n_rep,
        n_hi=n_row // n_rep,
        per_list=per_list,
        quarter=row_blocks // n_rep,
    )
    smem = [row_blocks * all_cols] * 2 + [slots, row_blocks * all_cols // COL_CHUNK, slots, slots]
    return pl.pallas_call(
        body,
        out_shape=shape((row_blocks * blk, all_cols * blk), BF16),
        grid_spec=pltpu.PrefetchScalarGridSpec(
            num_scalar_prefetch=3,
            grid=(all_cols // COL_CHUNK, row_blocks),
            in_specs=[WHOLE],
            out_specs=pl.BlockSpec((blk, width), lambda c, i, *_: (i, c)),
            scratch_shapes=[pltpu.SMEM((n,), jnp.int32) for n in smem],
        ),
        compiler_params=params(blocks.size * 2, blk * width * 4),
        cost_estimate=pl.CostEstimate(
            flops=slots * blk * blk,
            bytes_accessed=blocks.size * 2 + 2 * all_cols * row_blocks * blk * blk,
            transcendentals=0,
        ),
        name="densify",
    )(block_rows, block_fetch, block_count, blocks)


def pack_body(*refs, n_hi, per_list, blk):
    lists = refs[:n_hi]
    features = refs[n_hi]
    outs = refs[n_hi + 1 : 2 * n_hi + 1]
    own_list, sems = refs[2 * n_hi + 1 :]
    r = lax.axis_index("row")
    copies = []
    for hi in range(n_hi):
        for c in range(per_list):
            b = lists[hi][0, r, c]
            own_list[hi * per_list + c] = b
            copy = pltpu.make_async_copy(
                features.at[pl.ds(pl.multiple_of(b * blk, blk), blk)],
                outs[hi].at[pl.ds(c * blk, blk)],
                sems.at[hi * per_list + c],
            )
            copy.start()
            copies.append(copy)
    for copy in copies:
        copy.wait()


def pack(lists, features, per_list, blk):
    n_hi = len(lists)
    return pl.pallas_call(
        functools.partial(pack_body, n_hi=n_hi, per_list=per_list, blk=blk),
        out_shape=[shape((per_list * blk, features.shape[1]), BF16)] * n_hi + [shape((128,), jnp.int32)],
        in_specs=[SMEM] * n_hi + [pl.BlockSpec(memory_space=pltpu.HBM)],
        out_specs=[ANY] * n_hi + [SMEM],
        scratch_shapes=[pltpu.SemaphoreType.DMA((n_hi * per_list,))],
        compiler_params=pltpu.CompilerParams(vmem_limit_bytes=53 << 20),
        name="pack",
    )(*lists, features)


def forward_body(*refs, n_pieces):
    pieces = refs[:n_pieces]
    adj_ref, send_ref, keep_ref = refs[n_pieces:]
    i = pl.program_id(0)
    depth = pieces[0].shape[0]
    total = dot(adj_ref[:, :depth], pieces[0][...])
    for n in range(1, n_pieces):
        total += dot(adj_ref[:, n * depth : (n + 1) * depth], pieces[n][...])

    half = pl.num_programs(0) // 2

    @pl.when(i < half)
    def _():
        send_ref[...] = total.astype(BF16)

    @pl.when(i >= half)
    def _():
        keep_ref[...] = total


def forward(pieces, adj, half_index):
    rows, cols = adj.shape[0] // 2, adj.shape[1]
    features = pieces[0].shape[1]
    tiles = rows // ROW_TILE
    half = tiles // 2
    return pl.pallas_call(
        functools.partial(forward_body, n_pieces=len(pieces)),
        grid=(tiles,),
        out_shape=[shape((rows // 2, features), BF16), shape((rows // 2, features), F32)],
        in_specs=[pl.BlockSpec(x.shape, lambda i: (0, 0)) for x in pieces]
        + [pl.BlockSpec((ROW_TILE, cols), lambda i: (i + half_index * tiles, 0))],
        out_specs=[
            pl.BlockSpec((ROW_TILE, features), lambda i: (jnp.minimum(i, half - 1), 0)),
            pl.BlockSpec((ROW_TILE, features), lambda i: (jnp.maximum(i - half, 0), 0)),
        ],
        compiler_params=params(ROW_TILE * cols * 4, cols * features * 4),
        cost_estimate=pl.CostEstimate(
            flops=2 * rows * cols * features, bytes_accessed=adj.size + cols * features * 2, transcendentals=0
        ),
        name="forward",
    )(*pieces, adj)


def middle_body(
    keep_ref, near_ref, far_ref, weight_ref, cot_ref, out_ref, near_out, far_out, wkeep_ref, acc_ref, *, factor
):
    q = lax.axis_index("rep")
    hidden = (keep_ref[...] + near_ref[...].astype(F32) + far_ref[...].astype(F32)).astype(BF16)
    weight = weight_ref[...]
    pre_act = dot(hidden, weight)
    sig = jax.nn.sigmoid(pre_act)
    pre_grad = (cot_ref[...].astype(F32) * (sig * (1.0 + pre_act * (1.0 - sig)))).astype(BF16)
    features, rows = weight.shape[0], hidden.shape[0]
    input_grad = dot(weight, pre_grad, ((1,), (1,))).astype(BF16)
    near_out[:features] = input_grad
    far_out[:features] = input_grad
    out_ref[...] = (pre_act * sig).astype(BF16)
    acc_ref[...] = dot(hidden, pre_grad, ((0,), (0,))) * factor
    part = wkeep_ref.shape[0]
    wkeep_ref[...] = acc_ref[pl.ds(pl.multiple_of(q * part, part), part), :]
    for j, out, at in ((1, near_out, 0), (2, far_out, 0), (3, far_out, 1)):
        fold_in(out, features, at, acc_ref[pl.ds(pl.multiple_of((q ^ j) * part, part), part), :])


def fold_in(ref, base, at, piece):
    part, features = piece.shape
    folds = ref.shape[1] // features
    depth = part // folds
    for i in range(folds):
        ref[base + at * depth : base + (at + 1) * depth, i * features : (i + 1) * features] = piece[
            i * depth : (i + 1) * depth
        ].astype(ref.dtype)


def fold_out(ref, base, at, part, features):
    folds = ref.shape[1] // features
    depth = part // folds
    rows = ref[base + at * depth : base + (at + 1) * depth, :].astype(F32)
    return jnp.concatenate([rows[:, i * features : (i + 1) * features] for i in range(folds)], axis=0)


def middle(keep, near, far, weight, cot, n_rep, factor):
    rows, features = keep.shape
    part = features // n_rep
    extra = part * features // rows
    return pl.pallas_call(
        functools.partial(middle_body, factor=factor),
        out_shape=[
            shape((rows, features), BF16),
            shape((features + extra, rows), BF16),
            shape((features + 2 * extra, rows), BF16),
            shape((part, features), F32),
        ],
        in_specs=[WHOLE] * 5,
        out_specs=[WHOLE] * 4,
        scratch_shapes=[pltpu.VMEM((features, features), F32)],
        compiler_params=params(12 << 20),
        cost_estimate=pl.CostEstimate(
            flops=6 * rows * features * features, bytes_accessed=rows * features * 14, transcendentals=rows * features
        ),
        name="middle",
    )(keep, near, far, weight, cot)


def back_first_body(odd_ref, even_ref, adj_ref, wkeep_ref, out_ref, w_out):
    features, rows = out_ref.shape[0], odd_ref.shape[1]
    out_ref[...] = dot(odd_ref[:features], adj_ref[:rows]) + dot(even_ref[:features], adj_ref[rows:])

    @pl.when(pl.program_id(0) == 0)
    def _():
        w_out[...] = wkeep_ref[...] + fold_out(odd_ref, features, 0, *w_out.shape)


def back_first(odd, even, adj, wkeep):
    rows, cols = adj.shape[0] // 2, adj.shape[1]
    features = wkeep.shape[1]
    whole = lambda x: pl.BlockSpec(x.shape, lambda i: (0, 0))
    return pl.pallas_call(
        back_first_body,
        grid=(cols // COL_TILE,),
        out_shape=[shape((features, cols), F32), shape(wkeep.shape, F32)],
        in_specs=[whole(odd), whole(even), pl.BlockSpec((rows, COL_TILE), lambda i: (1, i)), whole(wkeep)],
        out_specs=[pl.BlockSpec((features, COL_TILE), lambda i: (0, i)), whole(wkeep)],
        compiler_params=params(4 << 20),
        cost_estimate=pl.CostEstimate(
            flops=2 * rows * cols * features, bytes_accessed=adj.size + cols * features * 4, transcendentals=0
        ),
        name="back_first",
    )(odd, even, adj, wkeep)


def back_second_body(odd_ref, even_ref, adj_ref, first_ref, w_ref, send_ref, keep_ref, w_out, acc_ref):
    q = lax.axis_index("rep")
    features, rows = first_ref.shape[0], odd_ref.shape[1]
    acc_ref[...] = (
        first_ref[...] + dot(odd_ref[:features], adj_ref[:rows]) + dot(even_ref[:features], adj_ref[rows:])
    )
    part = send_ref.shape[0] // 2
    for j in range(4):
        out = send_ref if j & 1 else keep_ref
        at = (3 - j) // 2 * part
        piece = acc_ref[pl.ds(pl.multiple_of((q ^ j) * part, part), part), :]
        out[at : at + part] = piece.astype(out.dtype)

    @pl.when(pl.program_id(0) == 0)
    def _():
        w_out[...] = (
            w_ref[...]
            + fold_out(even_ref, features, 0, *w_out.shape)
            + fold_out(odd_ref, features, 1, *w_out.shape)
        )


def back_second(odd, even, adj, first, w, half, n_rep, per_piece):
    rows, cols = adj.shape[0] // 2, adj.shape[1] // 2
    features = first.shape[0]
    width = cols // n_rep // per_piece
    tiles = cols // width
    whole = lambda x: pl.BlockSpec(x.shape, lambda i: (0, 0))
    return pl.pallas_call(
        back_second_body,
        grid=(tiles,),
        out_shape=[shape((features // 2, cols), BF16), shape((features // 2, cols), F32), shape(w.shape, F32)],
        in_specs=[
            whole(odd),
            whole(even),
            pl.BlockSpec((rows, width), lambda i: (0, i + half * tiles)),
            pl.BlockSpec((features, width), lambda i: (0, i + half * tiles)),
            whole(w),
        ],
        out_specs=[
            pl.BlockSpec(
                (features // 2, width), lambda i: (0, (lax.div(i, per_piece) ^ 1) * per_piece + lax.rem(i, per_piece))
            ),
            pl.BlockSpec((features // 2, width), lambda i: (0, i)),
            whole(w),
        ],
        scratch_shapes=[pltpu.VMEM((features, width), F32)],
        compiler_params=params(4 << 20),
        cost_estimate=pl.CostEstimate(
            flops=2 * rows * cols * features, bytes_accessed=rows * cols * 2 + cols * features * 7, transcendentals=0
        ),
        name=f"back_second_{half}",
    )(odd, even, adj, first, w)


def split_body(own_ref, near_ref, far_ref, *outs, n_rep, deep):
    q = lax.axis_index("rep")
    part, width = outs[0].shape
    for i, out in enumerate(outs):
        low, hi = i % n_rep, i // n_rep
        j = low ^ q
        cols = pl.ds(pl.multiple_of((j * deep + hi) * width, width), width)
        far_cols = pl.ds(pl.multiple_of(((j ^ 2) * deep + hi) * width, width), width)
        total = own_ref[part:, cols] + near_ref[part:, cols].astype(F32) + far_ref[:, far_cols].astype(F32)
        out[...] = total.astype(out.dtype)


def split(own, near, far, half, n_rep, deep):
    part, cols = far.shape
    count = n_rep * deep
    return pl.pallas_call(
        functools.partial(split_body, n_rep=n_rep, deep=deep),
        out_shape=[shape((part, cols // count), F32 if half + i == 0 else BF16) for i in range(count)],
        in_specs=[WHOLE] * 3,
        out_specs=[WHOLE] * count,
        compiler_params=params(own.size * 10),
        cost_estimate=pl.CostEstimate(flops=own.size, bytes_accessed=own.size * 5, transcendentals=0),
        name=f"split_{half}",
    )(own, near, far)


def collect_body(*refs, n_row, n_rep, per_list, quarter, blk):
    lists = refs[:n_rep]
    messages = refs[n_rep : n_rep + n_row]
    w_ref, got_ref = refs[n_rep + n_row : n_rep + n_row + 2]
    outs = refs[n_rep + n_row + 2 : -2]
    w_out, acc_ref = refs[-2:]
    q = lax.axis_index("rep")
    acc_ref[...] = jnp.zeros(acc_ref.shape, F32)
    for k in range(n_row):
        j = (k % n_rep) ^ q
        for c in range(per_list):
            at = k // n_rep * per_list + c
            b = lists[0][at]
            for other in range(1, n_rep):
                b = jnp.where(j == other, lists[other][at], b)
            cell = (lax.div(b, quarter) ^ q) * quarter + lax.rem(b, quarter)
            cols = pl.ds(pl.multiple_of(cell * blk, blk), blk)
            acc_ref[:, cols] += messages[k][:, c * blk : (c + 1) * blk].astype(F32)
    width = outs[0].shape[1]
    part = acc_ref.shape[0]
    w = (w_ref[...] + got_ref[...]).astype(BF16)
    w_out[...] = w
    for j, out in enumerate(outs):
        out[:part] = acc_ref[:, j * width : (j + 1) * width].astype(out.dtype)
        if j:
            fold_in(out, part, 0, w)


def collect(lists, messages, w, got, per_list, row_blocks, blk):
    n_rep = len(lists)
    n_row = len(messages)
    part = messages[0].shape[0]
    quarter = row_blocks // n_rep
    body = functools.partial(
        collect_body, n_row=n_row, n_rep=n_rep, per_list=per_list, quarter=quarter, blk=blk
    )
    return pl.pallas_call(
        body,
        out_shape=[shape((part, quarter * blk), F32)]
        + [shape((part + w.size // (quarter * blk), quarter * blk), BF16)] * (n_rep - 1)
        + [shape(w.shape, BF16)],
        in_specs=[SMEM] * n_rep + [WHOLE] * (n_row + 2),
        out_specs=[WHOLE] * (n_rep + 1),
        scratch_shapes=[pltpu.VMEM((part, row_blocks * blk), F32)],
        compiler_params=params(4 << 20),
        cost_estimate=pl.CostEstimate(
            flops=part * row_blocks * blk, bytes_accessed=part * row_blocks * blk * 5, transcendentals=0
        ),
        name="collect",
    )(*lists, *messages, w, got)


def finish_body(*refs, n_rep):
    grads = refs[:n_rep]
    w_ref, node_ref, weight_ref, acc_ref = refs[n_rep:]
    q = lax.axis_index("rep")
    part = w_ref.shape[0]
    for j in range(n_rep):
        rows = pl.ds(pl.multiple_of((q ^ j) * part, part), part)
        acc_ref[rows, :] = grads[j][:part].astype(F32)
        weight_ref[rows, :] = fold_out(grads[j], part, 0, *w_ref.shape) if j else w_ref[...].astype(F32)
    node_ref[...] = acc_ref[...].T


def finish(grads, w):
    n_rep = len(grads)
    part, rows = grads[0].shape
    features = w.shape[1]
    return pl.pallas_call(
        functools.partial(finish_body, n_rep=n_rep),
        out_shape=[shape((rows, part * n_rep), F32), shape((features, features), F32)],
        in_specs=[WHOLE] * (n_rep + 1),
        out_specs=[WHOLE] * 2,
        scratch_shapes=[pltpu.VMEM((part * n_rep, rows), F32)],
        compiler_params=params(6 << 20),
        cost_estimate=pl.CostEstimate(flops=0, bytes_accessed=rows * part * n_rep * 8, transcendentals=0),
        name="finish",
    )(*grads, w)


def local(
    node_features, weight, out_grad, blocks, block_rows, block_fetch, fetch_lists, block_count
):
    n_row = lax.axis_size("row")
    n_rep = lax.axis_size("rep")
    n_hi = n_row // n_rep
    band_rows, features = node_features.shape
    blk = blocks.shape[1]
    row_blocks = band_rows // blk
    per_list = fetch_lists.shape[2]

    def to_rep(x, j):
        return lax.ppermute(x, "rep", xor_perm(n_rep, j))

    def to_row(x, k):
        return lax.ppermute(x, "row", xor_perm(n_row, k))

    def spread(x, hi):
        perm = [
            (r * n_rep + q, (r ^ (hi * n_rep + q)) * n_rep + q) for r in range(n_row) for q in range(n_rep)
        ]
        return lax.ppermute(x, ("row", "rep"), perm)

    def after(x, *done):
        return lax.optimization_barrier((x, *done))[0]

    wanted = [spread(fetch_lists, hi) for hi in range(n_hi)]
    *outgoing, own_list = pack(wanted, node_features, per_list, blk)
    own = [spread(x, hi) for hi, x in enumerate(outgoing)]
    adj = densify(
        block_rows, block_fetch, after(block_count, outgoing), blocks, n_row, n_rep, per_list, row_blocks
    )
    own[0] = after(own[0], adj)
    far = [to_rep(x, 2) for x in own]
    near = [to_rep(x, 1) for x in own]
    diag = [to_rep(x, 1) for x in far]
    deep = n_hi // 2
    by_rep = [own, near, far, diag]
    pieces = [by_rep[j][half * deep + i] for half in range(2) for j in range(n_rep) for i in range(deep)]

    send3, keep2 = forward(pieces, adj, 0)
    across = (keep2 + to_rep(send3, 1).astype(F32)).astype(BF16)
    arrived = to_rep(across, 2)
    send1, keep0 = forward(pieces, after(adj, across), 1)
    own_list = after(own_list, keep0)
    lists = [own_list] + [to_rep(own_list, j) for j in range(1, n_rep)]
    arrived = after(arrived, keep0, lists)
    factor = float(n_row * band_rows) ** (-0.5)
    output, grad0, to_far, w = middle(keep0, to_rep(send1, 1), arrived, weight, out_grad, n_rep, factor)

    grad2 = to_rep(to_far, 2)
    grad1 = to_rep(grad0, 1)
    first, w = back_first(grad1, grad0, adj, w)
    grad2 = after(grad2, first)
    grad3 = to_rep(grad2, 1)
    send_high, keep_high, w = back_second(grad3, grad2, adj, first, w, 1, n_rep, deep)
    near_high = to_rep(send_high, 1)
    send_low, keep_low, _ = back_second(grad3, grad2, adj, after(first, send_high), w, 0, n_rep, deep)
    near_low = to_rep(send_low, 1)
    part = features // n_rep

    def across_sum(keep, near):
        return (keep[:part] + near[:part].astype(F32)).astype(BF16)

    far_high = to_rep(across_sum(keep_high, after(near_high, send_low)), 2)
    far_low = to_rep(across_sum(keep_low, near_low), 2)
    got = to_row(w, 1)
    high = split(keep_high, near_high, far_high, 1, n_rep, deep)
    half_rows = n_row // 2
    back_high = [to_row(x, half_rows + i) for i, x in enumerate(high)]
    w = w + after(got, high)
    step = 8
    while step < n_row:
        w = w + to_row(w, step)
        step *= 2
    got = to_row(w, 2)
    low = split(keep_low, near_low, after(far_low, back_high[:-1]), 0, n_rep, deep)
    w = w + after(got, low)
    returned = [low[0]] + [to_row(low[i], i) for i in range(1, half_rows)] + back_high
    *grads, w = collect(lists, returned, w, to_row(w, 4), per_list, row_blocks, blk)
    node_grad, weight_grad = finish([grads[0]] + [to_rep(grads[j], j) for j in range(1, n_rep)], w)
    return (output, weight_grad, node_grad)


def solution(mesh):
    in_specs = (
        P("row", None),
        P(),
        P(("row", "rep"), None),
        P(("row", "rep"), None, None),
        P(("row", "rep")),
        P(("row", "rep")),
        P(("row", "rep"), None, None),
        P(("row", "rep")),
    )
    out_specs = (P(("row", "rep"), None), P(), P(("row", "rep"), None))
    return jax.shard_map(local, mesh=mesh, in_specs=in_specs, out_specs=out_specs, check_vma=False)
```

```python
import functools

import jax
import jax.numpy as jnp
from jax import lax
from jax.experimental import pallas as pl
from jax.experimental.pallas import tpu as pltpu
from jax.sharding import PartitionSpec as P

BF16 = jnp.bfloat16
F32 = jnp.float32
COL_CHUNK = 16
ROW_TILE = 256
COL_TILE = 512
WHOLE = pl.BlockSpec(memory_space=pltpu.VMEM)
SMEM = pl.BlockSpec(memory_space=pltpu.SMEM)
ANY = pl.BlockSpec(memory_space=pl.ANY)


def params(*parts):
    return pltpu.CompilerParams(vmem_limit_bytes=min(sum(parts) + (6 << 20), 62 << 20))


def shape(dims, dtype):
    return jax.ShapeDtypeStruct(tuple(dims), dtype)


def dot(a, b, dims=((1,), (0,))):
    return lax.dot_general(a, b, (dims, ((), ())), preferred_element_type=F32)


def xor_perm(count, offset):
    return [(i, i ^ offset) for i in range(count)]


def div_rem(x, n):
    if n & (n - 1) == 0:
        return x >> (n.bit_length() - 1), x & (n - 1)
    return lax.div(x, n), lax.rem(x, n)


class Table:
    def __init__(self, slots, cells):
        self.groups = cells // COL_CHUNK
        self.first = 0
        self.second = cells
        self.older = 2 * cells
        self.wide_at = self.older + slots + 1
        self.wide_cell = self.wide_at + self.groups
        self.wide_next = self.wide_cell + slots
        self.size = -(-(self.wide_next + slots) // 128) * 128


def lists_body(rows_ref, fetch_ref, count_ref, out_ref, *, slots, n_rep, n_hi, per_list, quarter):
    r, q = lax.axis_index("row"), lax.axis_index("rep")
    all_cols = n_rep * n_hi * per_list
    chunks = all_cols // COL_CHUNK
    deep = n_hi // 2
    t = Table(slots, n_rep * quarter * all_cols)

    @pl.loop(0, t.older, unroll=16)
    def _(at):
        out_ref[at] = slots

    @pl.loop(0, t.groups, unroll=16)
    def _(at):
        out_ref[t.wide_at + at] = -1

    out_ref[t.older + slots] = slots

    def link(slot, wide):
        row_high, row_low = div_rem(rows_ref[slot], quarter)
        source, c = div_rem(fetch_ref[slot], per_list)
        hi, low = div_rem(source ^ r, n_rep)
        half, hi = div_rem(hi, deep)
        row = (n_rep - 1 - (row_high ^ q)) * quarter + row_low
        col = ((half * n_rep + (low ^ q)) * deep + hi) * per_list + c
        cell = row * all_cols + col
        at = t.wide_at + row * chunks + div_rem(col, COL_CHUNK)[0]
        one, two, begin = out_ref[t.first + cell], out_ref[t.second + cell], out_ref[at]
        out_ref[t.first + cell] = slot
        out_ref[t.second + cell] = one
        out_ref[t.older + slot] = one
        full = two != slots
        out_ref[t.wide_cell + wide] = cell
        out_ref[t.wide_next + wide] = begin
        out_ref[at] = jnp.where(full, wide, begin)
        return wide + full.astype(jnp.int32)

    lax.fori_loop(0, count_ref[0], link, jnp.int32(0))


def slot_lists(block_rows, block_fetch, block_count, n_row, n_rep, per_list, row_blocks):
    slots = block_rows.shape[0]
    body = functools.partial(
        lists_body,
        slots=slots,
        n_rep=n_rep,
        n_hi=n_row // n_rep,
        per_list=per_list,
        quarter=row_blocks // n_rep,
    )
    return pl.pallas_call(
        body,
        out_shape=shape((Table(slots, row_blocks * n_row * per_list).size,), jnp.int32),
        in_specs=[SMEM] * 3,
        out_specs=SMEM,
        compiler_params=pltpu.CompilerParams(vmem_limit_bytes=56 << 20),
        cost_estimate=pl.CostEstimate(flops=3 << 30, bytes_accessed=8 * slots, transcendentals=0),
        name="slot_lists",
    )(block_rows, block_fetch, block_count)


def densify_body(table_ref, held, out_ref, *, all_cols, row_blocks):
    chunk, row_cell = pl.program_id(0), pl.program_id(1)
    slots, blk = held.shape[0], held.shape[1]
    t = Table(slots, row_blocks * all_cols)
    zero = jnp.zeros((blk, blk), BF16)

    def block(slot):
        return jnp.where(slot < slots, held[jnp.minimum(slot, slots - 1)], zero)

    for col in range(COL_CHUNK):
        cell = row_cell * all_cols + chunk * COL_CHUNK + col
        total = block(table_ref[t.first + cell]) + block(table_ref[t.second + cell])
        out_ref[:, col * blk : (col + 1) * blk] = total

    def redo(wide):
        cell = table_ref[t.wide_cell + wide]
        two = table_ref[t.second + cell]
        three = table_ref[t.older + two]
        four = table_ref[t.older + three]
        total = held[table_ref[t.first + cell]].astype(F32) + held[two].astype(F32)
        total = total + (held[three].astype(F32) + block(four).astype(F32))
        col = cell - row_cell * all_cols - chunk * COL_CHUNK
        place = (slice(None), pl.ds(pl.multiple_of(col * blk, blk), blk))
        out_ref[place] = total.astype(BF16)
        five = table_ref[t.older + four]

        @pl.when(five < slots)
        def _():
            def more(carry):
                slot, total = carry
                return table_ref[t.older + slot], total + held[slot].astype(F32)

            _, rest = lax.while_loop(lambda carry: carry[0] < slots, more, (five, total))
            out_ref[place] = rest.astype(BF16)

        return table_ref[t.wide_next + wide]

    begin = table_ref[t.wide_at + row_cell * (all_cols // COL_CHUNK) + chunk]
    lax.while_loop(lambda wide: wide >= 0, redo, begin)


def densify(table, blocks, n_row, per_list, row_blocks):
    slots, blk, _ = blocks.shape
    all_cols = n_row * per_list
    width = COL_CHUNK * blk
    return pl.pallas_call(
        functools.partial(densify_body, all_cols=all_cols, row_blocks=row_blocks),
        out_shape=shape((row_blocks * blk, all_cols * blk), BF16),
        grid_spec=pltpu.PrefetchScalarGridSpec(
            num_scalar_prefetch=1,
            grid=(all_cols // COL_CHUNK, row_blocks),
            in_specs=[WHOLE],
            out_specs=pl.BlockSpec((blk, width), lambda c, i, *_: (i, c)),
        ),
        compiler_params=params(blocks.size * 2, blk * width * 4),
        cost_estimate=pl.CostEstimate(
            flops=slots * blk * blk,
            bytes_accessed=blocks.size * 2 + 2 * all_cols * row_blocks * blk * blk,
            transcendentals=0,
        ),
        name="densify",
    )(table, blocks)


def pack_body(*refs, n_hi, per_list, blk):
    lists = refs[:n_hi]
    features = refs[n_hi]
    outs = refs[n_hi + 1 : 2 * n_hi + 1]
    own_list, sems = refs[2 * n_hi + 1 :]
    r = lax.axis_index("row")
    copies = []
    for hi in range(n_hi):
        for c in range(per_list):
            b = lists[hi][0, r, c]
            own_list[hi * per_list + c] = b
            copy = pltpu.make_async_copy(
                features.at[pl.ds(pl.multiple_of(b * blk, blk), blk)],
                outs[hi].at[pl.ds(c * blk, blk)],
                sems.at[hi * per_list + c],
            )
            copy.start()
            copies.append(copy)
    for copy in copies:
        copy.wait()


def pack(lists, features, per_list, blk):
    n_hi = len(lists)
    return pl.pallas_call(
        functools.partial(pack_body, n_hi=n_hi, per_list=per_list, blk=blk),
        out_shape=[shape((per_list * blk, features.shape[1]), BF16)] * n_hi + [shape((128,), jnp.int32)],
        in_specs=[SMEM] * n_hi + [pl.BlockSpec(memory_space=pltpu.HBM)],
        out_specs=[ANY] * n_hi + [SMEM],
        scratch_shapes=[pltpu.SemaphoreType.DMA((n_hi * per_list,))],
        compiler_params=pltpu.CompilerParams(vmem_limit_bytes=53 << 20),
        name="pack",
    )(*lists, features)


def forward_body(*refs, n_rep):
    pieces = refs[:n_rep]
    adj_ref, send_ref, keep_ref = refs[n_rep:]
    i = pl.program_id(0)
    depth = pieces[0].shape[0] // 2
    total = 0.0
    for half in range(2):
        for j in range(n_rep):
            at = (half * n_rep + j) * depth
            total += dot(adj_ref[:, at : at + depth], pieces[j][half * depth : (half + 1) * depth])

    half = pl.num_programs(0) // 2

    @pl.when(i < half)
    def _():
        send_ref[...] = total.astype(BF16)

    @pl.when(i >= half)
    def _():
        keep_ref[...] = total


def forward(pieces, adj, half_index):
    rows, cols = adj.shape[0] // 2, adj.shape[1]
    features = pieces[0].shape[1]
    tiles = rows // ROW_TILE
    half = tiles // 2
    return pl.pallas_call(
        functools.partial(forward_body, n_rep=len(pieces)),
        grid=(tiles,),
        out_shape=[shape((rows // 2, features), BF16), shape((rows // 2, features), F32)],
        in_specs=[pl.BlockSpec(x.shape, lambda i: (0, 0)) for x in pieces]
        + [pl.BlockSpec((ROW_TILE, cols), lambda i: (i + half_index * tiles, 0))],
        out_specs=[
            pl.BlockSpec((ROW_TILE, features), lambda i: (jnp.minimum(i, half - 1), 0)),
            pl.BlockSpec((ROW_TILE, features), lambda i: (jnp.maximum(i - half, 0), 0)),
        ],
        compiler_params=params(ROW_TILE * cols * 4, cols * features * 4),
        cost_estimate=pl.CostEstimate(
            flops=2 * rows * cols * features, bytes_accessed=adj.size + cols * features * 2, transcendentals=0
        ),
        name="forward",
    )(*pieces, adj)


def middle_body(
    keep_ref, near_ref, far_ref, weight_ref, cot_ref, out_ref, near_out, far_out, wkeep_ref, acc_ref, *, factor
):
    q = lax.axis_index("rep")
    hidden = (keep_ref[...] + near_ref[...].astype(F32) + far_ref[...].astype(F32)).astype(BF16)
    weight = weight_ref[...]
    pre_act = dot(hidden, weight)
    sig = jax.nn.sigmoid(pre_act)
    pre_grad = (cot_ref[...].astype(F32) * (sig * (1.0 + pre_act * (1.0 - sig)))).astype(BF16)
    features, rows = weight.shape[0], hidden.shape[0]
    input_grad = dot(weight, pre_grad, ((1,), (1,))).astype(BF16)
    near_out[:features] = input_grad
    far_out[...] = input_grad
    out_ref[...] = (pre_act * sig).astype(BF16)
    acc_ref[...] = dot(hidden, pre_grad, ((0,), (0,))) * factor
    part = wkeep_ref.shape[0] // 2
    for j in range(4):
        piece = acc_ref[pl.ds(pl.multiple_of((q ^ j) * part, part), part), :]
        if j & 1:
            fold_in(near_out, features, j // 2, piece)
        else:
            wkeep_ref[j // 2 * part : (j // 2 + 1) * part] = piece


def fold_in(ref, base, at, piece):
    part, features = piece.shape
    folds = ref.shape[1] // features
    depth = part // folds
    for i in range(folds):
        ref[base + at * depth : base + (at + 1) * depth, i * features : (i + 1) * features] = piece[
            i * depth : (i + 1) * depth
        ].astype(ref.dtype)


def fold_out(ref, base, at, part, features):
    folds = ref.shape[1] // features
    depth = part // folds
    rows = ref[base + at * depth : base + (at + 1) * depth, :].astype(F32)
    return jnp.concatenate([rows[:, i * features : (i + 1) * features] for i in range(folds)], axis=0)


def middle(keep, near, far, weight, cot, n_rep, factor):
    rows, features = keep.shape
    part = features // n_rep
    extra = part * features // rows
    return pl.pallas_call(
        functools.partial(middle_body, factor=factor),
        out_shape=[
            shape((rows, features), BF16),
            shape((features + 2 * extra, rows), BF16),
            shape((features, rows), BF16),
            shape((2 * part, features), F32),
        ],
        in_specs=[WHOLE] * 5,
        out_specs=[WHOLE] * 4,
        scratch_shapes=[pltpu.VMEM((features, features), F32)],
        compiler_params=params(12 << 20),
        cost_estimate=pl.CostEstimate(
            flops=6 * rows * features * features, bytes_accessed=rows * features * 14, transcendentals=rows * features
        ),
        name="middle",
    )(keep, near, far, weight, cot)


def back_first_body(odd_ref, even_ref, adj_ref, wkeep_ref, out_ref, wsend_out, wkeep_out):
    features, rows = out_ref.shape[0], odd_ref.shape[1]
    out_ref[...] = dot(odd_ref[:features], adj_ref[:rows]) + dot(even_ref[...], adj_ref[rows:])

    @pl.when(pl.program_id(0) == 0)
    def _():
        part = wkeep_out.shape[0]
        mine = (lax.rem(lax.axis_index("row"), 2) ^ lax.div(lax.axis_index("rep"), 2)) == 0
        zero = wkeep_ref[:part] + fold_out(odd_ref, features, 0, *wkeep_out.shape)
        two = wkeep_ref[part:] + fold_out(odd_ref, features, 1, *wkeep_out.shape)
        wkeep_out[...] = jnp.where(mine, zero, two)
        wsend_out[...] = jnp.where(mine, two, zero)


def back_first(odd, even, adj, wkeep):
    rows, cols = adj.shape[0] // 2, adj.shape[1]
    features = wkeep.shape[1]
    whole = lambda x: pl.BlockSpec(x.shape, lambda i: (0, 0))
    part = wkeep.shape[0] // 2
    return pl.pallas_call(
        back_first_body,
        grid=(cols // COL_TILE,),
        out_shape=[shape((features, cols), F32)] + [shape((part, features), F32)] * 2,
        in_specs=[whole(odd), whole(even), pl.BlockSpec((rows, COL_TILE), lambda i: (1, i)), whole(wkeep)],
        out_specs=[pl.BlockSpec((features, COL_TILE), lambda i: (0, i))]
        + [pl.BlockSpec((part, features), lambda i: (0, 0))] * 2,
        compiler_params=params(4 << 20),
        cost_estimate=pl.CostEstimate(
            flops=2 * rows * cols * features, bytes_accessed=adj.size + cols * features * 4, transcendentals=0
        ),
        name="back_first",
    )(odd, even, adj, wkeep)


def back_second_body(odd_ref, even_ref, adj_ref, first_ref, send_ref, keep_ref, acc_ref):
    q = lax.axis_index("rep")
    rows = odd_ref.shape[1]
    acc_ref[...] = first_ref[...] + dot(odd_ref[...], adj_ref[:rows]) + dot(even_ref[...], adj_ref[rows:])
    part = send_ref.shape[0] // 2
    for j in range(4):
        out = send_ref if j & 1 else keep_ref
        at = (3 - j) // 2 * part
        piece = acc_ref[pl.ds(pl.multiple_of((q ^ j) * part, part), part), :]
        out[at : at + part] = piece.astype(out.dtype)


def back_second(odd, even, adj, first, half, n_rep, per_piece):
    rows, cols = adj.shape[0] // 2, adj.shape[1] // 2
    features = first.shape[0]
    width = cols // n_rep // per_piece
    tiles = cols // width
    whole = lambda x: pl.BlockSpec(x.shape, lambda i: (0, 0))
    return pl.pallas_call(
        back_second_body,
        grid=(tiles,),
        out_shape=[shape((features // 2, cols), BF16), shape((features // 2, cols), F32)],
        in_specs=[
            whole(odd),
            whole(even),
            pl.BlockSpec((rows, width), lambda i: (0, i + half * tiles)),
            pl.BlockSpec((features, width), lambda i: (0, i + half * tiles)),
        ],
        out_specs=[
            pl.BlockSpec(
                (features // 2, width), lambda i: (0, (lax.div(i, per_piece) ^ 1) * per_piece + lax.rem(i, per_piece))
            ),
            pl.BlockSpec((features // 2, width), lambda i: (0, i)),
        ],
        scratch_shapes=[pltpu.VMEM((features, width), F32)],
        compiler_params=params(4 << 20),
        cost_estimate=pl.CostEstimate(
            flops=2 * rows * cols * features, bytes_accessed=rows * cols * 2 + cols * features * 7, transcendentals=0
        ),
        name=f"back_second_{half}",
    )(odd, even, adj, first)


def split_body(own_ref, near_ref, far_ref, *refs, n_rep, deep, half):
    q = lax.axis_index("rep")
    w, outs = (None, refs) if half else (refs[0], refs[1:])
    part, width = outs[0].shape
    for i, out in enumerate(outs):
        low, hi = i % n_rep, i // n_rep
        j = low ^ q
        cols = pl.ds(pl.multiple_of((j * deep + hi) * width, width), width)
        far_cols = pl.ds(pl.multiple_of(((j ^ 2) * deep + hi) * width, width), width)
        total = own_ref[part:, cols] + near_ref[part:, cols].astype(F32) + far_ref[:, far_cols].astype(F32)
        out[:part] = total.astype(out.dtype)
    if w is not None:
        fold_in(outs[1], part, 0, w[...])


def split(own, near, far, w, half, n_rep, deep):
    part, cols = far.shape
    count = n_rep * deep
    width = cols // count
    out_shape = [shape((part, width), BF16) for i in range(count)]
    if not half:
        out_shape[0] = shape((part, width), F32)
        out_shape[1] = shape((part + w.size // width, width), BF16)
    extra = [] if half else [w]
    return pl.pallas_call(
        functools.partial(split_body, n_rep=n_rep, deep=deep, half=half),
        out_shape=out_shape,
        in_specs=[WHOLE] * (3 + len(extra)),
        out_specs=[WHOLE] * count,
        compiler_params=params(own.size * 10),
        cost_estimate=pl.CostEstimate(flops=own.size, bytes_accessed=own.size * 5, transcendentals=0),
        name=f"split_{half}",
    )(own, near, far, *extra)


def collect_body(*refs, n_row, n_rep, per_list, quarter, blk):
    lists = refs[:n_rep]
    messages = refs[n_rep : n_rep + n_row]
    w_ref = refs[n_rep + n_row]
    outs = refs[n_rep + n_row + 1 : -3]
    w_out, other_out, acc_ref = refs[-3:]
    q = lax.axis_index("rep")
    acc_ref[...] = jnp.zeros(acc_ref.shape, F32)
    for k in range(n_row):
        j = (k % n_rep) ^ q
        for c in range(per_list):
            at = k // n_rep * per_list + c
            b = lists[0][at]
            for other in range(1, n_rep):
                b = jnp.where(j == other, lists[other][at], b)
            cell = (lax.div(b, quarter) ^ q) * quarter + lax.rem(b, quarter)
            cols = pl.ds(pl.multiple_of(cell * blk, blk), blk)
            acc_ref[:, cols] += messages[k][: acc_ref.shape[0], c * blk : (c + 1) * blk].astype(F32)
    width = outs[0].shape[1]
    part = acc_ref.shape[0]
    w_out[...] = w_ref[...].astype(BF16)
    other_out[...] = fold_out(messages[1], part, 0, *w_ref.shape).astype(BF16)
    for j, out in enumerate(outs):
        out[:part] = acc_ref[:, j * width : (j + 1) * width].astype(out.dtype)
    fold_in(outs[1], part, 0, w_out[...])
    fold_in(outs[1], part, 1, other_out[...])


def collect(lists, messages, w, per_list, row_blocks, blk):
    n_rep = len(lists)
    n_row = len(messages)
    part = messages[0].shape[0]
    quarter = row_blocks // n_rep
    body = functools.partial(
        collect_body, n_row=n_row, n_rep=n_rep, per_list=per_list, quarter=quarter, blk=blk
    )
    return pl.pallas_call(
        body,
        out_shape=[
            shape((part, quarter * blk), F32),
            shape((part + 2 * w.size // (quarter * blk), quarter * blk), BF16),
        ]
        + [shape((part, quarter * blk), BF16)] * (n_rep - 2)
        + [shape(w.shape, BF16)] * 2,
        in_specs=[SMEM] * n_rep + [WHOLE] * (n_row + 1),
        out_specs=[WHOLE] * (n_rep + 2),
        scratch_shapes=[pltpu.VMEM((part, row_blocks * blk), F32)],
        compiler_params=params(4 << 20),
        cost_estimate=pl.CostEstimate(
            flops=part * row_blocks * blk, bytes_accessed=part * row_blocks * blk * 5, transcendentals=0
        ),
        name="collect",
    )(*lists, *messages, w)


def finish_body(*refs, n_rep):
    grads = refs[:n_rep]
    w_ref, other_ref, node_ref, weight_ref, acc_ref = refs[n_rep:]
    q = lax.axis_index("rep")
    part = w_ref.shape[0]
    for j in range(n_rep):
        acc_ref[pl.ds(pl.multiple_of((q ^ j) * part, part), part), :] = grads[j][:part].astype(F32)
    mine = lax.rem(q, 2) + 2 * lax.rem(lax.axis_index("row"), 2)
    near = [fold_out(grads[1], part, at, *w_ref.shape) for at in range(2)]
    for j, piece in enumerate((w_ref[...].astype(F32), near[0], other_ref[...].astype(F32), near[1])):
        weight_ref[pl.ds(pl.multiple_of((mine ^ j) * part, part), part), :] = piece
    node_ref[...] = acc_ref[...].T


def finish(grads, w, other):
    n_rep = len(grads)
    part, rows = grads[0].shape
    features = w.shape[1]
    return pl.pallas_call(
        functools.partial(finish_body, n_rep=n_rep),
        out_shape=[shape((rows, part * n_rep), F32), shape((features, features), F32)],
        in_specs=[WHOLE] * (n_rep + 2),
        out_specs=[WHOLE] * 2,
        scratch_shapes=[pltpu.VMEM((part * n_rep, rows), F32)],
        compiler_params=params(6 << 20),
        cost_estimate=pl.CostEstimate(flops=0, bytes_accessed=rows * part * n_rep * 8, transcendentals=0),
        name="finish",
    )(*grads, w, other)


def local(
    node_features, weight, out_grad, blocks, block_rows, block_fetch, fetch_lists, block_count
):
    n_row = lax.axis_size("row")
    n_rep = lax.axis_size("rep")
    n_hi = n_row // n_rep
    band_rows, features = node_features.shape
    blk = blocks.shape[1]
    row_blocks = band_rows // blk
    per_list = fetch_lists.shape[2]

    def to_rep(x, j):
        return lax.ppermute(x, "rep", xor_perm(n_rep, j))

    def to_row(x, k):
        return lax.ppermute(x, "row", xor_perm(n_row, k))

    def spread(x, hi):
        perm = [
            (r * n_rep + q, (r ^ (hi * n_rep + q)) * n_rep + q) for r in range(n_row) for q in range(n_rep)
        ]
        return lax.ppermute(x, ("row", "rep"), perm)

    def after(x, *done):
        return lax.optimization_barrier((x, *done))[0]

    wanted = [spread(fetch_lists, hi) for hi in range(n_hi)]
    *outgoing, own_list = pack(wanted, node_features, per_list, blk)
    own = [spread(x, hi) for hi, x in enumerate(outgoing)]
    table = slot_lists(
        block_rows, block_fetch, after(block_count, outgoing), n_row, n_rep, per_list, row_blocks
    )
    adj = densify(table, blocks, n_row, per_list, row_blocks)
    deep = n_hi // 2
    own = after(jnp.concatenate(own, axis=0), adj)
    far = to_rep(own, 2)
    pieces = [own, to_rep(own, 1), far, to_rep(far, 1)]

    send3, keep2 = forward(pieces, adj, 0)
    across = (keep2 + to_rep(send3, 1).astype(F32)).astype(BF16)
    arrived = to_rep(across, 2)
    send1, keep0 = forward(pieces, after(adj, across), 1)
    own_list = after(own_list, keep0)
    lists = [own_list] + [to_rep(own_list, j) for j in range(1, n_rep)]
    arrived = after(arrived, keep0, lists)
    factor = float(n_row * band_rows) ** (-0.5)
    output, to_near, grad0, wkeep = middle(keep0, to_rep(send1, 1), arrived, weight, out_grad, n_rep, factor)

    grad2 = to_rep(grad0, 2)
    first, wsend, w = back_first(to_rep(to_near, 1), grad0, adj, wkeep)
    w = w + to_row(wsend, 1)
    grad2 = after(grad2, first, w)
    grad3 = to_rep(grad2, 1)
    got = to_rep(w, 2)
    send_high, keep_high = back_second(grad3, grad2, adj, first, 1, n_rep, deep)
    send_high = after(send_high, got)
    near_high = to_rep(send_high, 1)
    send_low, keep_low = back_second(grad3, grad2, adj, after(first, send_high), 0, n_rep, deep)
    near_low = to_rep(send_low, 1)
    w = w + got
    got = to_row(w, 2)
    part = features // n_rep

    def across_sum(keep, near):
        return (keep[:part] + near[:part].astype(F32)).astype(BF16)

    far_high = to_rep(across_sum(keep_high, after(near_high, send_low, got)), 2)
    across = across_sum(keep_low, near_low)
    far_low = to_rep(across, 2)
    w = w + got
    got = to_row(after(w, across), 4)
    high = split(keep_high, near_high, after(far_high, got), None, 1, n_rep, deep)
    w = w + got
    step = 8
    while step < n_row:
        w = w + to_row(w, step)
        step *= 2
    half_rows = n_row // 2
    back_high = [to_row(x, half_rows + i) for i, x in enumerate(high)]
    low = split(keep_low, near_low, after(far_low, back_high[:2]), w, 0, n_rep, deep)
    returned = [low[0]] + [to_row(low[i], i) for i in range(1, half_rows)] + back_high
    *grads, w, other = collect(lists, returned, w, per_list, row_blocks, blk)
    node_grad, weight_grad = finish([grads[0]] + [to_rep(grads[j], j) for j in range(1, n_rep)], w, other)
    return (output, weight_grad, node_grad)


def solution(mesh):
    in_specs = (
        P("row", None),
        P(),
        P(("row", "rep"), None),
        P(("row", "rep"), None, None),
        P(("row", "rep")),
        P(("row", "rep")),
        P(("row", "rep"), None, None),
        P(("row", "rep")),
    )
    out_specs = (P(("row", "rep"), None), P(), P(("row", "rep"), None))
    return jax.shard_map(local, mesh=mesh, in_specs=in_specs, out_specs=out_specs, check_vma=False)
```

```python
import functools

import jax
import jax.numpy as jnp
from jax import lax
from jax.experimental import pallas as pl
from jax.experimental.pallas import tpu as pltpu
from jax.sharding import PartitionSpec as P

BF16 = jnp.bfloat16
F32 = jnp.float32
COL_CHUNK = 16
LIST_STEP = 4
ROW_TILE = 256
COL_TILE = 512
WHOLE = pl.BlockSpec(memory_space=pltpu.VMEM)
SMEM = pl.BlockSpec(memory_space=pltpu.SMEM)
ANY = pl.BlockSpec(memory_space=pl.ANY)


def params(*parts):
    return pltpu.CompilerParams(vmem_limit_bytes=min(sum(parts) + (6 << 20), 62 << 20))


def shape(dims, dtype):
    return jax.ShapeDtypeStruct(tuple(dims), dtype)


def dot(a, b, dims=((1,), (0,))):
    return lax.dot_general(a, b, (dims, ((), ())), preferred_element_type=F32)


def xor_perm(count, offset):
    return [(i, i ^ offset) for i in range(count)]


def div_rem(x, n):
    if n & (n - 1) == 0:
        return x >> (n.bit_length() - 1), x & (n - 1)
    return lax.div(x, n), lax.rem(x, n)


class Table:
    def __init__(self, slots, cells):
        self.groups = cells // COL_CHUNK
        self.spare = cells
        self.first = 0
        self.second = cells + 1
        self.older = 2 * (cells + 1)
        self.wide_at = self.older + slots + 1
        self.wide_cell = self.wide_at + self.groups
        self.wide_next = self.wide_cell + slots
        self.size = -(-(self.wide_next + slots) // 128) * 128


def lists_body(rows_ref, fetch_ref, count_ref, out_ref, *, slots, n_rep, n_hi, per_list, quarter):
    r, q = lax.axis_index("row"), lax.axis_index("rep")
    all_cols = n_rep * n_hi * per_list
    chunks = all_cols // COL_CHUNK
    deep = n_hi // 2
    t = Table(slots, n_rep * quarter * all_cols)

    @pl.loop(0, t.older, unroll=16)
    def _(at):
        out_ref[at] = slots

    @pl.loop(0, t.groups, unroll=16)
    def _(at):
        out_ref[t.wide_at + at] = -1

    out_ref[t.older + slots] = slots

    live = count_ref[0]

    def place(slot):
        row_high, row_low = div_rem(rows_ref[slot], quarter)
        source, c = div_rem(fetch_ref[slot], per_list)
        hi, low = div_rem(source ^ r, n_rep)
        half, hi = div_rem(hi, deep)
        row = (n_rep - 1 - (row_high ^ q)) * quarter + row_low
        col = ((half * n_rep + (low ^ q)) * deep + hi) * per_list + c
        cell = jnp.where(slot < live, row * all_cols + col, t.spare)
        return cell, t.wide_at + row * chunks + div_rem(col, COL_CHUNK)[0]

    def link(slot, cell, at, wide):
        one, two, begin = out_ref[t.first + cell], out_ref[t.second + cell], out_ref[at]
        out_ref[t.first + cell] = slot
        out_ref[t.second + cell] = one
        out_ref[t.older + slot] = one
        full = (two != slots) & (slot < live)
        out_ref[t.wide_cell + wide] = cell
        out_ref[t.wide_next + wide] = begin
        out_ref[at] = jnp.where(full, wide, begin)
        return wide + full.astype(jnp.int32)

    def link_group(group, wide):
        begin = group * LIST_STEP
        places = [(begin + i, *place(begin + i)) for i in range(LIST_STEP)]
        for slot, cell, at in places:
            wide = link(slot, cell, at, wide)
        return wide

    lax.fori_loop(0, lax.div(live + LIST_STEP - 1, LIST_STEP), link_group, jnp.int32(0))


def slot_lists(block_rows, block_fetch, block_count, n_row, n_rep, per_list, row_blocks):
    slots = block_rows.shape[0]
    body = functools.partial(
        lists_body,
        slots=slots,
        n_rep=n_rep,
        n_hi=n_row // n_rep,
        per_list=per_list,
        quarter=row_blocks // n_rep,
    )
    return pl.pallas_call(
        body,
        out_shape=shape((Table(slots, row_blocks * n_row * per_list).size,), jnp.int32),
        in_specs=[SMEM] * 3,
        out_specs=SMEM,
        compiler_params=pltpu.CompilerParams(vmem_limit_bytes=56 << 20),
        cost_estimate=pl.CostEstimate(flops=3 << 30, bytes_accessed=8 * slots, transcendentals=0),
        name="slot_lists",
    )(block_rows, block_fetch, block_count)


def densify_body(table_ref, held, out_ref, *, all_cols, row_blocks):
    chunk, row_cell = pl.program_id(0), pl.program_id(1)
    slots, blk = held.shape[0], held.shape[1]
    t = Table(slots, row_blocks * all_cols)
    zero = jnp.zeros((blk, blk), BF16)

    def block(slot):
        return jnp.where(slot < slots, held[jnp.minimum(slot, slots - 1)], zero)

    for col in range(COL_CHUNK):
        cell = row_cell * all_cols + chunk * COL_CHUNK + col
        total = block(table_ref[t.first + cell]) + block(table_ref[t.second + cell])
        out_ref[:, col * blk : (col + 1) * blk] = total

    def redo(wide):
        cell = table_ref[t.wide_cell + wide]
        two = table_ref[t.second + cell]
        three = table_ref[t.older + two]
        four = table_ref[t.older + three]
        total = held[table_ref[t.first + cell]].astype(F32) + held[two].astype(F32)
        total = total + (held[three].astype(F32) + block(four).astype(F32))
        col = cell - row_cell * all_cols - chunk * COL_CHUNK
        place = (slice(None), pl.ds(pl.multiple_of(col * blk, blk), blk))
        out_ref[place] = total.astype(BF16)
        five = table_ref[t.older + four]

        @pl.when(five < slots)
        def _():
            def more(carry):
                slot, total = carry
                return table_ref[t.older + slot], total + held[slot].astype(F32)

            _, rest = lax.while_loop(lambda carry: carry[0] < slots, more, (five, total))
            out_ref[place] = rest.astype(BF16)

        return table_ref[t.wide_next + wide]

    begin = table_ref[t.wide_at + row_cell * (all_cols // COL_CHUNK) + chunk]
    lax.while_loop(lambda wide: wide >= 0, redo, begin)


def densify(table, blocks, n_row, per_list, row_blocks):
    slots, blk, _ = blocks.shape
    all_cols = n_row * per_list
    width = COL_CHUNK * blk
    return pl.pallas_call(
        functools.partial(densify_body, all_cols=all_cols, row_blocks=row_blocks),
        out_shape=shape((row_blocks * blk, all_cols * blk), BF16),
        grid_spec=pltpu.PrefetchScalarGridSpec(
            num_scalar_prefetch=1,
            grid=(all_cols // COL_CHUNK, row_blocks),
            in_specs=[WHOLE],
            out_specs=pl.BlockSpec((blk, width), lambda c, i, *_: (i, c)),
        ),
        compiler_params=params(blocks.size * 2, blk * width * 4),
        cost_estimate=pl.CostEstimate(
            flops=slots * blk * blk,
            bytes_accessed=blocks.size * 2 + 2 * all_cols * row_blocks * blk * blk,
            transcendentals=0,
        ),
        name="densify",
    )(table, blocks)


def pack_body(*refs, n_hi, per_list, blk):
    lists = refs[:n_hi]
    features = refs[n_hi]
    outs = refs[n_hi + 1 : 2 * n_hi + 1]
    own_list, sems = refs[2 * n_hi + 1 :]
    r = lax.axis_index("row")
    copies = []
    for hi in range(n_hi):
        for c in range(per_list):
            b = lists[hi][0, r, c]
            own_list[hi * per_list + c] = b
            copy = pltpu.make_async_copy(
                features.at[pl.ds(pl.multiple_of(b * blk, blk), blk)],
                outs[hi].at[pl.ds(c * blk, blk)],
                sems.at[hi * per_list + c],
            )
            copy.start()
            copies.append(copy)
    for copy in copies:
        copy.wait()


def pack(lists, features, per_list, blk):
    n_hi = len(lists)
    return pl.pallas_call(
        functools.partial(pack_body, n_hi=n_hi, per_list=per_list, blk=blk),
        out_shape=[shape((per_list * blk, features.shape[1]), BF16)] * n_hi + [shape((128,), jnp.int32)],
        in_specs=[SMEM] * n_hi + [pl.BlockSpec(memory_space=pltpu.HBM)],
        out_specs=[ANY] * n_hi + [SMEM],
        scratch_shapes=[pltpu.SemaphoreType.DMA((n_hi * per_list,))],
        compiler_params=pltpu.CompilerParams(vmem_limit_bytes=53 << 20),
        name="pack",
    )(*lists, features)


def forward_body(*refs, n_rep):
    pieces = refs[:n_rep]
    adj_ref, send_ref, keep_ref = refs[n_rep:]
    i = pl.program_id(0)
    depth = pieces[0].shape[0] // 2
    total = 0.0
    for half in range(2):
        for j in range(n_rep):
            at = (half * n_rep + j) * depth
            total += dot(adj_ref[:, at : at + depth], pieces[j][half * depth : (half + 1) * depth])

    half = pl.num_programs(0) // 2

    @pl.when(i < half)
    def _():
        send_ref[...] = total.astype(BF16)

    @pl.when(i >= half)
    def _():
        keep_ref[...] = total


def forward(pieces, adj, half_index):
    rows, cols = adj.shape[0] // 2, adj.shape[1]
    features = pieces[0].shape[1]
    tiles = rows // ROW_TILE
    half = tiles // 2
    return pl.pallas_call(
        functools.partial(forward_body, n_rep=len(pieces)),
        grid=(tiles,),
        out_shape=[shape((rows // 2, features), BF16), shape((rows // 2, features), F32)],
        in_specs=[pl.BlockSpec(x.shape, lambda i: (0, 0)) for x in pieces]
        + [pl.BlockSpec((ROW_TILE, cols), lambda i: (i + half_index * tiles, 0))],
        out_specs=[
            pl.BlockSpec((ROW_TILE, features), lambda i: (jnp.minimum(i, half - 1), 0)),
            pl.BlockSpec((ROW_TILE, features), lambda i: (jnp.maximum(i - half, 0), 0)),
        ],
        compiler_params=params(ROW_TILE * cols * 4, cols * features * 4),
        cost_estimate=pl.CostEstimate(
            flops=2 * rows * cols * features, bytes_accessed=adj.size + cols * features * 2, transcendentals=0
        ),
        name="forward",
    )(*pieces, adj)


def middle_body(
    keep_ref, near_ref, far_ref, weight_ref, cot_ref, out_ref, near_out, far_out, wkeep_ref, acc_ref, *, factor
):
    q = lax.axis_index("rep")
    hidden = (keep_ref[...] + near_ref[...].astype(F32) + far_ref[...].astype(F32)).astype(BF16)
    weight = weight_ref[...]
    pre_act = dot(hidden, weight)
    sig = jax.nn.sigmoid(pre_act)
    pre_grad = (cot_ref[...].astype(F32) * (sig * (1.0 + pre_act * (1.0 - sig)))).astype(BF16)
    features, rows = weight.shape[0], hidden.shape[0]
    input_grad = dot(weight, pre_grad, ((1,), (1,))).astype(BF16)
    near_out[:features] = input_grad
    far_out[...] = input_grad
    out_ref[...] = (pre_act * sig).astype(BF16)
    acc_ref[...] = dot(hidden, pre_grad, ((0,), (0,))) * factor
    part = wkeep_ref.shape[0] // 2
    for j in range(4):
        piece = acc_ref[pl.ds(pl.multiple_of((q ^ j) * part, part), part), :]
        if j & 1:
            fold_in(near_out, features, j // 2, piece)
        else:
            wkeep_ref[j // 2 * part : (j // 2 + 1) * part] = piece


def fold_in(ref, base, at, piece):
    part, features = piece.shape
    folds = ref.shape[1] // features
    depth = part // folds
    for i in range(folds):
        ref[base + at * depth : base + (at + 1) * depth, i * features : (i + 1) * features] = piece[
            i * depth : (i + 1) * depth
        ].astype(ref.dtype)


def fold_out(ref, base, at, part, features):
    folds = ref.shape[1] // features
    depth = part // folds
    rows = ref[base + at * depth : base + (at + 1) * depth, :].astype(F32)
    return jnp.concatenate([rows[:, i * features : (i + 1) * features] for i in range(folds)], axis=0)


def middle(keep, near, far, weight, cot, n_rep, factor):
    rows, features = keep.shape
    part = features // n_rep
    extra = part * features // rows
    return pl.pallas_call(
        functools.partial(middle_body, factor=factor),
        out_shape=[
            shape((rows, features), BF16),
            shape((features + 2 * extra, rows), BF16),
            shape((features, rows), BF16),
            shape((2 * part, features), F32),
        ],
        in_specs=[WHOLE] * 5,
        out_specs=[WHOLE] * 4,
        scratch_shapes=[pltpu.VMEM((features, features), F32)],
        compiler_params=params(12 << 20),
        cost_estimate=pl.CostEstimate(
            flops=6 * rows * features * features, bytes_accessed=rows * features * 14, transcendentals=rows * features
        ),
        name="middle",
    )(keep, near, far, weight, cot)


def back_first_body(odd_ref, even_ref, adj_ref, wkeep_ref, out_ref, wsend_out, wkeep_out):
    features, rows = out_ref.shape[0], odd_ref.shape[1]
    out_ref[...] = dot(odd_ref[:features], adj_ref[:rows]) + dot(even_ref[...], adj_ref[rows:])

    @pl.when(pl.program_id(0) == 0)
    def _():
        part = wkeep_out.shape[0]
        mine = (lax.rem(lax.axis_index("row"), 2) ^ lax.div(lax.axis_index("rep"), 2)) == 0
        zero = wkeep_ref[:part] + fold_out(odd_ref, features, 0, *wkeep_out.shape)
        two = wkeep_ref[part:] + fold_out(odd_ref, features, 1, *wkeep_out.shape)
        wkeep_out[...] = jnp.where(mine, zero, two)
        wsend_out[...] = jnp.where(mine, two, zero)


def back_first(odd, even, adj, wkeep):
    rows, cols = adj.shape[0] // 2, adj.shape[1]
    features = wkeep.shape[1]
    whole = lambda x: pl.BlockSpec(x.shape, lambda i: (0, 0))
    part = wkeep.shape[0] // 2
    return pl.pallas_call(
        back_first_body,
        grid=(cols // COL_TILE,),
        out_shape=[shape((features, cols), F32)] + [shape((part, features), F32)] * 2,
        in_specs=[whole(odd), whole(even), pl.BlockSpec((rows, COL_TILE), lambda i: (1, i)), whole(wkeep)],
        out_specs=[pl.BlockSpec((features, COL_TILE), lambda i: (0, i))]
        + [pl.BlockSpec((part, features), lambda i: (0, 0))] * 2,
        compiler_params=params(4 << 20),
        cost_estimate=pl.CostEstimate(
            flops=2 * rows * cols * features, bytes_accessed=adj.size + cols * features * 4, transcendentals=0
        ),
        name="back_first",
    )(odd, even, adj, wkeep)


def back_second_body(odd_ref, even_ref, adj_ref, first_ref, send_ref, keep_ref, acc_ref):
    q = lax.axis_index("rep")
    rows = odd_ref.shape[1]
    acc_ref[...] = first_ref[...] + dot(odd_ref[...], adj_ref[:rows]) + dot(even_ref[...], adj_ref[rows:])
    part = send_ref.shape[0] // 2
    for j in range(4):
        out = send_ref if j & 1 else keep_ref
        at = (3 - j) // 2 * part
        piece = acc_ref[pl.ds(pl.multiple_of((q ^ j) * part, part), part), :]
        out[at : at + part] = piece.astype(out.dtype)


def back_second(odd, even, adj, first, half, n_rep, per_piece):
    rows, cols = adj.shape[0] // 2, adj.shape[1] // 2
    features = first.shape[0]
    width = cols // n_rep // per_piece
    tiles = cols // width
    whole = lambda x: pl.BlockSpec(x.shape, lambda i: (0, 0))
    return pl.pallas_call(
        back_second_body,
        grid=(tiles,),
        out_shape=[shape((features // 2, cols), BF16), shape((features // 2, cols), F32)],
        in_specs=[
            whole(odd),
            whole(even),
            pl.BlockSpec((rows, width), lambda i: (0, i + half * tiles)),
            pl.BlockSpec((features, width), lambda i: (0, i + half * tiles)),
        ],
        out_specs=[
            pl.BlockSpec(
                (features // 2, width), lambda i: (0, (lax.div(i, per_piece) ^ 1) * per_piece + lax.rem(i, per_piece))
            ),
            pl.BlockSpec((features // 2, width), lambda i: (0, i)),
        ],
        scratch_shapes=[pltpu.VMEM((features, width), F32)],
        compiler_params=params(4 << 20),
        cost_estimate=pl.CostEstimate(
            flops=2 * rows * cols * features, bytes_accessed=rows * cols * 2 + cols * features * 7, transcendentals=0
        ),
        name=f"back_second_{half}",
    )(odd, even, adj, first)


def split_body(*refs, n_rep, deep):
    halves, out_ref = (refs[:3], refs[3:6]), refs[6]
    r, q = lax.axis_index("row"), lax.axis_index("rep")
    _, part, width = out_ref.shape
    for half, (own_ref, near_ref, far_ref) in enumerate(halves):
        for i in range(n_rep * deep):
            low, hi = i % n_rep, i // n_rep
            j = low ^ q
            cols = pl.ds(pl.multiple_of((j * deep + hi) * width, width), width)
            far_cols = pl.ds(pl.multiple_of(((j ^ 2) * deep + hi) * width, width), width)
            total = own_ref[part:, cols] + near_ref[part:, cols].astype(F32) + far_ref[:, far_cols].astype(F32)
            out_ref[r ^ (half * n_rep * deep + i)] = total.astype(BF16)


def split(low, high, n_row, n_rep):
    part, cols = low[2].shape
    width = 2 * cols // n_row
    return pl.pallas_call(
        functools.partial(split_body, n_rep=n_rep, deep=n_row // n_rep // 2),
        out_shape=shape((n_row, part, width), BF16),
        in_specs=[WHOLE] * 6,
        out_specs=WHOLE,
        compiler_params=params(cols * part * 40),
        cost_estimate=pl.CostEstimate(flops=4 * part * cols, bytes_accessed=part * cols * 20, transcendentals=0),
        name="split",
    )(*low, *high)


def collect_body(*refs, n_row, n_rep, per_list, quarter, blk):
    lists = refs[:n_rep]
    messages, w_ref, other_ref = refs[n_rep : n_rep + 3]
    outs, acc_ref = refs[n_rep + 3 : -1], refs[-1]
    r, q = lax.axis_index("row"), lax.axis_index("rep")
    acc_ref[...] = jnp.zeros(acc_ref.shape, F32)
    for k in range(n_row):
        j = (k % n_rep) ^ q
        for c in range(per_list):
            at = k // n_rep * per_list + c
            b = lists[0][at]
            for other in range(1, n_rep):
                b = jnp.where(j == other, lists[other][at], b)
            cell = (lax.div(b, quarter) ^ q) * quarter + lax.rem(b, quarter)
            cols = pl.ds(pl.multiple_of(cell * blk, blk), blk)
            acc_ref[:, cols] += messages[r ^ k, :, c * blk : (c + 1) * blk].astype(F32)
    width = outs[0].shape[1]
    part = acc_ref.shape[0]
    for j, out in enumerate(outs):
        out[:part] = acc_ref[:, j * width : (j + 1) * width].astype(out.dtype)
    fold_in(outs[1], part, 0, w_ref[...])
    fold_in(outs[1], part, 1, other_ref[...])


def collect(lists, messages, w, other, per_list, row_blocks, blk):
    n_rep = len(lists)
    n_row, part, _ = messages.shape
    quarter = row_blocks // n_rep
    body = functools.partial(
        collect_body, n_row=n_row, n_rep=n_rep, per_list=per_list, quarter=quarter, blk=blk
    )
    return pl.pallas_call(
        body,
        out_shape=[
            shape((part, quarter * blk), F32),
            shape((part + 2 * w.size // (quarter * blk), quarter * blk), BF16),
        ]
        + [shape((part, quarter * blk), BF16)] * (n_rep - 2),
        in_specs=[SMEM] * n_rep + [WHOLE] * 3,
        out_specs=[WHOLE] * n_rep,
        scratch_shapes=[pltpu.VMEM((part, row_blocks * blk), F32)],
        compiler_params=params(4 << 20),
        cost_estimate=pl.CostEstimate(
            flops=part * row_blocks * blk, bytes_accessed=part * row_blocks * blk * 5, transcendentals=0
        ),
        name="collect",
    )(*lists, messages, w, other)


def finish_body(*refs, n_rep):
    grads = refs[:n_rep]
    w_ref, other_ref, node_ref, weight_ref, acc_ref = refs[n_rep:]
    q = lax.axis_index("rep")
    part = w_ref.shape[0]
    for j in range(n_rep):
        acc_ref[pl.ds(pl.multiple_of((q ^ j) * part, part), part), :] = grads[j][:part].astype(F32)
    mine = lax.rem(q, 2) + 2 * lax.rem(lax.axis_index("row"), 2)
    near = [fold_out(grads[1], part, at, *w_ref.shape) for at in range(2)]
    for j, piece in enumerate((w_ref[...].astype(F32), near[0], other_ref[...].astype(F32), near[1])):
        weight_ref[pl.ds(pl.multiple_of((mine ^ j) * part, part), part), :] = piece
    node_ref[...] = acc_ref[...].T


def finish(grads, w, other):
    n_rep = len(grads)
    part, rows = grads[0].shape
    features = w.shape[1]
    return pl.pallas_call(
        functools.partial(finish_body, n_rep=n_rep),
        out_shape=[shape((rows, part * n_rep), F32), shape((features, features), F32)],
        in_specs=[WHOLE] * (n_rep + 2),
        out_specs=[WHOLE] * 2,
        scratch_shapes=[pltpu.VMEM((part * n_rep, rows), F32)],
        compiler_params=params(6 << 20),
        cost_estimate=pl.CostEstimate(flops=0, bytes_accessed=rows * part * n_rep * 8, transcendentals=0),
        name="finish",
    )(*grads, w, other)


def local(
    node_features, weight, out_grad, blocks, block_rows, block_fetch, fetch_lists, block_count
):
    n_row = lax.axis_size("row")
    n_rep = lax.axis_size("rep")
    n_hi = n_row // n_rep
    band_rows, features = node_features.shape
    blk = blocks.shape[1]
    row_blocks = band_rows // blk
    per_list = fetch_lists.shape[2]

    def to_rep(x, j):
        return lax.ppermute(x, "rep", xor_perm(n_rep, j))

    def to_row(x, k):
        return lax.ppermute(x, "row", xor_perm(n_row, k))

    def spread(x, hi):
        perm = [
            (r * n_rep + q, (r ^ (hi * n_rep + q)) * n_rep + q) for r in range(n_row) for q in range(n_rep)
        ]
        return lax.ppermute(x, ("row", "rep"), perm)

    def after(x, *done):
        return lax.optimization_barrier((x, *done))[0]

    wanted = [spread(fetch_lists, hi) for hi in range(n_hi)]
    *outgoing, own_list = pack(wanted, node_features, per_list, blk)
    own = [spread(x, hi) for hi, x in enumerate(outgoing)]
    table = slot_lists(
        block_rows, block_fetch, after(block_count, outgoing), n_row, n_rep, per_list, row_blocks
    )
    deep = n_hi // 2
    own = after(jnp.concatenate(own, axis=0), table)
    far = to_rep(own, 2)
    near = to_rep(own, 1)
    adj = densify(after(table, near), blocks, n_row, per_list, row_blocks)
    pieces = [own, near, far, to_rep(after(far, adj), 1)]

    send3, keep2 = forward(pieces, adj, 0)
    across = (keep2 + to_rep(send3, 1).astype(F32)).astype(BF16)
    arrived = to_rep(across, 2)
    send1, keep0 = forward(pieces, after(adj, across), 1)
    own_list = after(own_list, keep0)
    lists = [own_list] + [to_rep(own_list, j) for j in range(1, n_rep)]
    arrived = after(arrived, keep0, lists)
    factor = float(n_row * band_rows) ** (-0.5)
    output, to_near, grad0, wkeep = middle(keep0, to_rep(send1, 1), arrived, weight, out_grad, n_rep, factor)

    grad2 = to_rep(grad0, 2)
    first, wsend, w = back_first(to_rep(to_near, 1), grad0, adj, wkeep)
    w = w + to_row(wsend, 1)
    grad2 = after(grad2, first, w)
    grad3 = to_rep(grad2, 1)
    got = to_rep(w, 2)
    send_high, keep_high = back_second(grad3, grad2, adj, first, 1, n_rep, deep)
    send_high = after(send_high, got)
    w = w + got
    got = to_row(w, 2)
    near_high = to_rep(send_high, 1)
    send_low, keep_low = back_second(grad3, grad2, adj, after(first, send_high), 0, n_rep, deep)
    near_low = to_rep(after(send_low, near_high, got), 1)
    part = features // n_rep

    def across_sum(keep, near):
        return (keep[:part] + near[:part].astype(F32)).astype(BF16)

    across_high = across_sum(keep_high, after(near_high, send_low))
    across_low = across_sum(keep_low, near_low)
    far_high = to_rep(across_high, 2)
    far_low = to_rep(across_low, 2)
    w = w + got
    w = w + to_row(after(w, across_high, across_low), 4)
    step = 8
    while step < n_row:
        w = w + to_row(w, step)
        step *= 2
    w = w.astype(BF16)
    other = to_row(w, 1)
    messages = split((keep_low, near_low, far_low), (keep_high, near_high, after(far_high, w)), n_row, n_rep)
    returned = lax.all_to_all(messages, "row", split_axis=0, concat_axis=0, tiled=True)
    grads = collect(lists, returned, w, other, per_list, row_blocks, blk)
    node_grad, weight_grad = finish([grads[0]] + [to_rep(grads[j], j) for j in range(1, n_rep)], w, other)
    return (output, weight_grad, node_grad)


def solution(mesh):
    in_specs = (
        P("row", None),
        P(),
        P(("row", "rep"), None),
        P(("row", "rep"), None, None),
        P(("row", "rep")),
        P(("row", "rep")),
        P(("row", "rep"), None, None),
        P(("row", "rep")),
    )
    out_specs = (P(("row", "rep"), None), P(), P(("row", "rep"), None))
    return jax.shard_map(local, mesh=mesh, in_specs=in_specs, out_specs=out_specs, check_vma=False)
```

```python
import functools

import jax
import jax.numpy as jnp
from jax import lax
from jax.experimental import pallas as pl
from jax.experimental.pallas import tpu as pltpu
from jax.sharding import PartitionSpec as P

BF16 = jnp.bfloat16
F32 = jnp.float32
COL_CHUNK = 16
LIST_STEP = 4
ROW_TILE = 256
COL_TILE = 512
WHOLE = pl.BlockSpec(memory_space=pltpu.VMEM)
SMEM = pl.BlockSpec(memory_space=pltpu.SMEM)
ANY = pl.BlockSpec(memory_space=pl.ANY)


def params(*parts):
    return pltpu.CompilerParams(vmem_limit_bytes=min(sum(parts) + (6 << 20), 62 << 20))


def shape(dims, dtype):
    return jax.ShapeDtypeStruct(tuple(dims), dtype)


def dot(a, b, dims=((1,), (0,))):
    return lax.dot_general(a, b, (dims, ((), ())), preferred_element_type=F32)


def xor_perm(count, offset):
    return [(i, i ^ offset) for i in range(count)]


def div_rem(x, n):
    if n & (n - 1) == 0:
        return x >> (n.bit_length() - 1), x & (n - 1)
    return lax.div(x, n), lax.rem(x, n)


class Table:
    def __init__(self, slots, cells):
        self.groups = cells // COL_CHUNK
        self.spare = cells
        self.first = 0
        self.second = cells + 1
        self.older = 2 * (cells + 1)
        self.wide_at = self.older + slots + 1
        self.wide_cell = self.wide_at + self.groups
        self.wide_next = self.wide_cell + slots
        self.size = -(-(self.wide_next + slots) // 128) * 128


def lists_body(rows_ref, fetch_ref, count_ref, out_ref, *, slots, n_rep, n_hi, per_list, quarter):
    r, q = lax.axis_index("row"), lax.axis_index("rep")
    all_cols = n_rep * n_hi * per_list
    chunks = all_cols // COL_CHUNK
    deep = n_hi // 2
    t = Table(slots, n_rep * quarter * all_cols)

    @pl.loop(0, t.older, unroll=16)
    def _(at):
        out_ref[at] = slots

    @pl.loop(0, t.groups, unroll=16)
    def _(at):
        out_ref[t.wide_at + at] = -1

    out_ref[t.older + slots] = slots

    live = count_ref[0]

    def place(slot):
        row_high, row_low = div_rem(rows_ref[slot], quarter)
        source, c = div_rem(fetch_ref[slot], per_list)
        hi, low = div_rem(source ^ r, n_rep)
        half, hi = div_rem(hi, deep)
        row = (n_rep - 1 - (row_high ^ q)) * quarter + row_low
        col = ((half * n_rep + (low ^ q)) * deep + hi) * per_list + c
        cell = jnp.where(slot < live, row * all_cols + col, t.spare)
        return cell, t.wide_at + row * chunks + div_rem(col, COL_CHUNK)[0]

    def link(slot, cell, at, wide):
        one, two, begin = out_ref[t.first + cell], out_ref[t.second + cell], out_ref[at]
        out_ref[t.first + cell] = slot
        out_ref[t.second + cell] = one
        out_ref[t.older + slot] = one
        full = (two != slots) & (slot < live)
        out_ref[t.wide_cell + wide] = cell
        out_ref[t.wide_next + wide] = begin
        out_ref[at] = jnp.where(full, wide, begin)
        return wide + full.astype(jnp.int32)

    def link_group(group, wide):
        begin = group * LIST_STEP
        places = [(begin + i, *place(begin + i)) for i in range(LIST_STEP)]
        for slot, cell, at in places:
            wide = link(slot, cell, at, wide)
        return wide

    lax.fori_loop(0, lax.div(live + LIST_STEP - 1, LIST_STEP), link_group, jnp.int32(0))


def slot_lists(block_rows, block_fetch, block_count, n_row, n_rep, per_list, row_blocks):
    slots = block_rows.shape[0]
    body = functools.partial(
        lists_body,
        slots=slots,
        n_rep=n_rep,
        n_hi=n_row // n_rep,
        per_list=per_list,
        quarter=row_blocks // n_rep,
    )
    return pl.pallas_call(
        body,
        out_shape=shape((Table(slots, row_blocks * n_row * per_list).size,), jnp.int32),
        in_specs=[SMEM] * 3,
        out_specs=SMEM,
        compiler_params=pltpu.CompilerParams(vmem_limit_bytes=56 << 20),
        cost_estimate=pl.CostEstimate(flops=3 << 30, bytes_accessed=8 * slots, transcendentals=0),
        name="slot_lists",
    )(block_rows, block_fetch, block_count)


def densify_body(table_ref, held, out_ref, *, all_cols, row_blocks):
    chunk, row_cell = pl.program_id(0), pl.program_id(1)
    slots, blk = held.shape[0], held.shape[1]
    t = Table(slots, row_blocks * all_cols)
    zero = jnp.zeros((blk, blk), BF16)

    def block(slot):
        return jnp.where(slot < slots, held[jnp.minimum(slot, slots - 1)], zero)

    for col in range(COL_CHUNK):
        cell = row_cell * all_cols + chunk * COL_CHUNK + col
        total = block(table_ref[t.first + cell]) + block(table_ref[t.second + cell])
        out_ref[:, col * blk : (col + 1) * blk] = total

    def redo(wide):
        cell = table_ref[t.wide_cell + wide]
        two = table_ref[t.second + cell]
        three = table_ref[t.older + two]
        four = table_ref[t.older + three]
        total = held[table_ref[t.first + cell]].astype(F32) + held[two].astype(F32)
        total = total + (held[three].astype(F32) + block(four).astype(F32))
        col = cell - row_cell * all_cols - chunk * COL_CHUNK
        place = (slice(None), pl.ds(pl.multiple_of(col * blk, blk), blk))
        out_ref[place] = total.astype(BF16)
        five = table_ref[t.older + four]

        @pl.when(five < slots)
        def _():
            def more(carry):
                slot, total = carry
                return table_ref[t.older + slot], total + held[slot].astype(F32)

            _, rest = lax.while_loop(lambda carry: carry[0] < slots, more, (five, total))
            out_ref[place] = rest.astype(BF16)

        return table_ref[t.wide_next + wide]

    begin = table_ref[t.wide_at + row_cell * (all_cols // COL_CHUNK) + chunk]
    lax.while_loop(lambda wide: wide >= 0, redo, begin)


def densify(table, blocks, n_row, per_list, row_blocks):
    slots, blk, _ = blocks.shape
    all_cols = n_row * per_list
    width = COL_CHUNK * blk
    return pl.pallas_call(
        functools.partial(densify_body, all_cols=all_cols, row_blocks=row_blocks),
        out_shape=shape((row_blocks * blk, all_cols * blk), BF16),
        grid_spec=pltpu.PrefetchScalarGridSpec(
            num_scalar_prefetch=1,
            grid=(all_cols // COL_CHUNK, row_blocks),
            in_specs=[WHOLE],
            out_specs=pl.BlockSpec((blk, width), lambda c, i, *_: (i, c)),
        ),
        compiler_params=params(blocks.size * 2, blk * width * 4),
        cost_estimate=pl.CostEstimate(
            flops=slots * blk * blk,
            bytes_accessed=blocks.size * 2 + 2 * all_cols * row_blocks * blk * blk,
            transcendentals=0,
        ),
        name="densify",
    )(table, blocks)


def pack_body(*refs, n_hi, per_list, blk):
    lists = refs[:n_hi]
    features = refs[n_hi]
    outs = refs[n_hi + 1 : 2 * n_hi + 1]
    own_list, sems = refs[2 * n_hi + 1 :]
    r = lax.axis_index("row")
    copies = []
    for hi in range(n_hi):
        for c in range(per_list):
            b = lists[hi][0, r, c]
            own_list[hi * per_list + c] = b
            copy = pltpu.make_async_copy(
                features.at[pl.ds(pl.multiple_of(b * blk, blk), blk)],
                outs[hi].at[pl.ds(c * blk, blk)],
                sems.at[hi * per_list + c],
            )
            copy.start()
            copies.append(copy)
    for copy in copies:
        copy.wait()


def pack(lists, features, per_list, blk):
    n_hi = len(lists)
    return pl.pallas_call(
        functools.partial(pack_body, n_hi=n_hi, per_list=per_list, blk=blk),
        out_shape=[shape((per_list * blk, features.shape[1]), BF16)] * n_hi + [shape((128,), jnp.int32)],
        in_specs=[SMEM] * n_hi + [pl.BlockSpec(memory_space=pltpu.HBM)],
        out_specs=[ANY] * n_hi + [SMEM],
        scratch_shapes=[pltpu.SemaphoreType.DMA((n_hi * per_list,))],
        compiler_params=pltpu.CompilerParams(vmem_limit_bytes=53 << 20),
        name="pack",
    )(*lists, features)


def forward_body(*refs, n_rep):
    pieces = refs[:n_rep]
    adj_ref, send_ref, keep_ref = refs[n_rep:]
    i = pl.program_id(0)
    depth = pieces[0].shape[0] // 2
    total = 0.0
    for half in range(2):
        for j in range(n_rep):
            at = (half * n_rep + j) * depth
            total += dot(adj_ref[:, at : at + depth], pieces[j][half * depth : (half + 1) * depth])

    half = pl.num_programs(0) // 2

    @pl.when(i < half)
    def _():
        send_ref[...] = total.astype(BF16)

    @pl.when(i >= half)
    def _():
        keep_ref[...] = total


def forward(pieces, adj, half_index):
    rows, cols = adj.shape[0] // 2, adj.shape[1]
    features = pieces[0].shape[1]
    tiles = rows // ROW_TILE
    half = tiles // 2
    return pl.pallas_call(
        functools.partial(forward_body, n_rep=len(pieces)),
        grid=(tiles,),
        out_shape=[shape((rows // 2, features), BF16), shape((rows // 2, features), F32)],
        in_specs=[pl.BlockSpec(x.shape, lambda i: (0, 0)) for x in pieces]
        + [pl.BlockSpec((ROW_TILE, cols), lambda i: (i + half_index * tiles, 0))],
        out_specs=[
            pl.BlockSpec((ROW_TILE, features), lambda i: (jnp.minimum(i, half - 1), 0)),
            pl.BlockSpec((ROW_TILE, features), lambda i: (jnp.maximum(i - half, 0), 0)),
        ],
        compiler_params=params(ROW_TILE * cols * 4, cols * features * 4),
        cost_estimate=pl.CostEstimate(
            flops=2 * rows * cols * features, bytes_accessed=adj.size + cols * features * 2, transcendentals=0
        ),
        name="forward",
    )(*pieces, adj)


def middle_body(
    keep_ref, near_ref, far_ref, weight_ref, cot_ref, out_ref, near_out, far_out, wkeep_ref, acc_ref, *, factor
):
    q = lax.axis_index("rep")
    hidden = (keep_ref[...] + near_ref[...].astype(F32) + far_ref[...].astype(F32)).astype(BF16)
    weight = weight_ref[...]
    pre_act = dot(hidden, weight)
    sig = jax.nn.sigmoid(pre_act)
    pre_grad = (cot_ref[...].astype(F32) * (sig * (1.0 + pre_act * (1.0 - sig)))).astype(BF16)
    features, rows = weight.shape[0], hidden.shape[0]
    input_grad = dot(weight, pre_grad, ((1,), (1,))).astype(BF16)
    near_out[:features] = input_grad
    far_out[...] = input_grad
    out_ref[...] = (pre_act * sig).astype(BF16)
    acc_ref[...] = dot(hidden, pre_grad, ((0,), (0,))) * factor
    part = wkeep_ref.shape[0] // 2
    for j in range(4):
        piece = acc_ref[pl.ds(pl.multiple_of((q ^ j) * part, part), part), :]
        if j & 1:
            fold_in(near_out, features, j // 2, piece)
        else:
            wkeep_ref[j // 2 * part : (j // 2 + 1) * part] = piece


def fold_in(ref, base, at, piece):
    part, features = piece.shape
    folds = ref.shape[1] // features
    depth = part // folds
    for i in range(folds):
        ref[base + at * depth : base + (at + 1) * depth, i * features : (i + 1) * features] = piece[
            i * depth : (i + 1) * depth
        ].astype(ref.dtype)


def fold_out(ref, base, at, part, features):
    folds = ref.shape[1] // features
    depth = part // folds
    rows = ref[base + at * depth : base + (at + 1) * depth, :].astype(F32)
    return jnp.concatenate([rows[:, i * features : (i + 1) * features] for i in range(folds)], axis=0)


def middle(keep, near, far, weight, cot, n_rep, factor):
    rows, features = keep.shape
    part = features // n_rep
    extra = part * features // rows
    return pl.pallas_call(
        functools.partial(middle_body, factor=factor),
        out_shape=[
            shape((rows, features), BF16),
            shape((features + 2 * extra, rows), BF16),
            shape((features, rows), BF16),
            shape((2 * part, features), F32),
        ],
        in_specs=[WHOLE] * 5,
        out_specs=[WHOLE] * 4,
        scratch_shapes=[pltpu.VMEM((features, features), F32)],
        compiler_params=params(12 << 20),
        cost_estimate=pl.CostEstimate(
            flops=6 * rows * features * features, bytes_accessed=rows * features * 14, transcendentals=rows * features
        ),
        name="middle",
    )(keep, near, far, weight, cot)


def back_first_body(odd_ref, even_ref, adj_ref, wkeep_ref, out_ref, w_out):
    features, rows = out_ref.shape[0], odd_ref.shape[1]
    out_ref[...] = dot(odd_ref[:features], adj_ref[:rows]) + dot(even_ref[...], adj_ref[rows:])

    @pl.when(pl.program_id(0) == 0)
    def _():
        part = w_out.shape[0] // 2
        for at in range(2):
            rows_here = slice(at * part, (at + 1) * part)
            w_out[rows_here] = wkeep_ref[rows_here] + fold_out(odd_ref, features, at, part, features)


def back_first(odd, even, adj, wkeep):
    rows, cols = adj.shape[0] // 2, adj.shape[1]
    features = wkeep.shape[1]
    whole = lambda x: pl.BlockSpec(x.shape, lambda i: (0, 0))
    return pl.pallas_call(
        back_first_body,
        grid=(cols // COL_TILE,),
        out_shape=[shape((features, cols), F32), shape(wkeep.shape, F32)],
        in_specs=[whole(odd), whole(even), pl.BlockSpec((rows, COL_TILE), lambda i: (1, i)), whole(wkeep)],
        out_specs=[pl.BlockSpec((features, COL_TILE), lambda i: (0, i)), whole(wkeep)],
        compiler_params=params(4 << 20),
        cost_estimate=pl.CostEstimate(
            flops=2 * rows * cols * features, bytes_accessed=adj.size + cols * features * 4, transcendentals=0
        ),
        name="back_first",
    )(odd, even, adj, wkeep)


def back_second_body(odd_ref, even_ref, adj_ref, first_ref, send_ref, keep_ref, acc_ref):
    q = lax.axis_index("rep")
    rows = odd_ref.shape[1]
    acc_ref[...] = first_ref[...] + dot(odd_ref[...], adj_ref[:rows]) + dot(even_ref[...], adj_ref[rows:])
    part = send_ref.shape[0] // 2
    for j in range(4):
        out = send_ref if j & 1 else keep_ref
        at = (3 - j) // 2 * part
        piece = acc_ref[pl.ds(pl.multiple_of((q ^ j) * part, part), part), :]
        out[at : at + part] = piece.astype(out.dtype)


def back_second(odd, even, adj, first, half, n_rep, per_piece):
    rows, cols = adj.shape[0] // 2, adj.shape[1] // 2
    features = first.shape[0]
    width = cols // n_rep // per_piece
    tiles = cols // width
    whole = lambda x: pl.BlockSpec(x.shape, lambda i: (0, 0))
    return pl.pallas_call(
        back_second_body,
        grid=(tiles,),
        out_shape=[shape((features // 2, cols), BF16), shape((features // 2, cols), F32)],
        in_specs=[
            whole(odd),
            whole(even),
            pl.BlockSpec((rows, width), lambda i: (0, i + half * tiles)),
            pl.BlockSpec((features, width), lambda i: (0, i + half * tiles)),
        ],
        out_specs=[
            pl.BlockSpec(
                (features // 2, width), lambda i: (0, (lax.div(i, per_piece) ^ 1) * per_piece + lax.rem(i, per_piece))
            ),
            pl.BlockSpec((features // 2, width), lambda i: (0, i)),
        ],
        scratch_shapes=[pltpu.VMEM((features, width), F32)],
        compiler_params=params(4 << 20),
        cost_estimate=pl.CostEstimate(
            flops=2 * rows * cols * features, bytes_accessed=rows * cols * 2 + cols * features * 7, transcendentals=0
        ),
        name=f"back_second_{half}",
    )(odd, even, adj, first)


def split_body(*refs, n_rep, deep):
    halves, out_ref = (refs[:3], refs[3:6]), refs[6]
    r, q = lax.axis_index("row"), lax.axis_index("rep")
    _, part, width = out_ref.shape
    for half, (own_ref, near_ref, far_ref) in enumerate(halves):
        for i in range(n_rep * deep):
            low, hi = i % n_rep, i // n_rep
            j = low ^ q
            cols = pl.ds(pl.multiple_of((j * deep + hi) * width, width), width)
            far_cols = pl.ds(pl.multiple_of(((j ^ 2) * deep + hi) * width, width), width)
            total = own_ref[part:, cols] + near_ref[part:, cols].astype(F32) + far_ref[:, far_cols].astype(F32)
            out_ref[r ^ (half * n_rep * deep + i)] = total.astype(BF16)


def split(low, high, n_row, n_rep):
    part, cols = low[2].shape
    width = 2 * cols // n_row
    return pl.pallas_call(
        functools.partial(split_body, n_rep=n_rep, deep=n_row // n_rep // 2),
        out_shape=shape((n_row, part, width), BF16),
        in_specs=[WHOLE] * 6,
        out_specs=WHOLE,
        compiler_params=params(cols * part * 40),
        cost_estimate=pl.CostEstimate(flops=4 * part * cols, bytes_accessed=part * cols * 20, transcendentals=0),
        name="split",
    )(*low, *high)


def collect_body(*refs, n_row, n_rep, per_list, quarter, blk):
    lists = refs[:n_rep]
    messages, w_ref = refs[n_rep : n_rep + 2]
    outs, acc_ref = refs[n_rep + 2 : -1], refs[-1]
    r, q = lax.axis_index("row"), lax.axis_index("rep")
    acc_ref[...] = jnp.zeros(acc_ref.shape, F32)
    for k in range(n_row):
        j = (k % n_rep) ^ q
        for c in range(per_list):
            at = k // n_rep * per_list + c
            b = lists[0][at]
            for other in range(1, n_rep):
                b = jnp.where(j == other, lists[other][at], b)
            cell = (lax.div(b, quarter) ^ q) * quarter + lax.rem(b, quarter)
            cols = pl.ds(pl.multiple_of(cell * blk, blk), blk)
            acc_ref[:, cols] += messages[r ^ k, :, c * blk : (c + 1) * blk].astype(F32)
    width = outs[0].shape[1]
    part = acc_ref.shape[0]
    for j, out in enumerate(outs):
        out[:part] = acc_ref[:, j * width : (j + 1) * width].astype(out.dtype)
        if j:
            fold_in(out, part, 0, w_ref[...])


def collect(lists, messages, w, per_list, row_blocks, blk):
    n_rep = len(lists)
    n_row, part, _ = messages.shape
    quarter = row_blocks // n_rep
    body = functools.partial(
        collect_body, n_row=n_row, n_rep=n_rep, per_list=per_list, quarter=quarter, blk=blk
    )
    return pl.pallas_call(
        body,
        out_shape=[shape((part, quarter * blk), F32)]
        + [shape((part + w.size // (quarter * blk), quarter * blk), BF16)] * (n_rep - 1),
        in_specs=[SMEM] * n_rep + [WHOLE] * 2,
        out_specs=[WHOLE] * n_rep,
        scratch_shapes=[pltpu.VMEM((part, row_blocks * blk), F32)],
        compiler_params=params(4 << 20),
        cost_estimate=pl.CostEstimate(
            flops=part * row_blocks * blk, bytes_accessed=part * row_blocks * blk * 5, transcendentals=0
        ),
        name="collect",
    )(*lists, messages, w)


def finish_body(*refs, n_rep):
    grads = refs[:n_rep]
    w_ref, node_ref, weight_ref, acc_ref = refs[n_rep:]
    q = lax.axis_index("rep")
    part = w_ref.shape[0]
    for j in range(n_rep):
        rows = pl.ds(pl.multiple_of((q ^ j) * part, part), part)
        acc_ref[rows, :] = grads[j][:part].astype(F32)
        weight_ref[rows, :] = fold_out(grads[j], part, 0, *w_ref.shape) if j else w_ref[...].astype(F32)
    node_ref[...] = acc_ref[...].T


def finish(grads, w):
    n_rep = len(grads)
    part, rows = grads[0].shape
    features = w.shape[1]
    return pl.pallas_call(
        functools.partial(finish_body, n_rep=n_rep),
        out_shape=[shape((rows, part * n_rep), F32), shape((features, features), F32)],
        in_specs=[WHOLE] * (n_rep + 1),
        out_specs=[WHOLE] * 2,
        scratch_shapes=[pltpu.VMEM((part * n_rep, rows), F32)],
        compiler_params=params(6 << 20),
        cost_estimate=pl.CostEstimate(flops=0, bytes_accessed=rows * part * n_rep * 8, transcendentals=0),
        name="finish",
    )(*grads, w)


def local(
    node_features, weight, out_grad, blocks, block_rows, block_fetch, fetch_lists, block_count
):
    n_row = lax.axis_size("row")
    n_rep = lax.axis_size("rep")
    n_hi = n_row // n_rep
    band_rows, features = node_features.shape
    blk = blocks.shape[1]
    row_blocks = band_rows // blk
    per_list = fetch_lists.shape[2]

    def to_rep(x, j):
        return lax.ppermute(x, "rep", xor_perm(n_rep, j))

    def to_row(x, k):
        return lax.ppermute(x, "row", xor_perm(n_row, k))

    def spread(x, hi):
        perm = [
            (r * n_rep + q, (r ^ (hi * n_rep + q)) * n_rep + q) for r in range(n_row) for q in range(n_rep)
        ]
        return lax.ppermute(x, ("row", "rep"), perm)

    def after(x, *done):
        return lax.optimization_barrier((x, *done))[0]

    wanted = [spread(fetch_lists, hi) for hi in range(n_hi)]
    *outgoing, own_list = pack(wanted, node_features, per_list, blk)
    own = [spread(x, hi) for hi, x in enumerate(outgoing)]
    table = slot_lists(
        block_rows, block_fetch, after(block_count, outgoing), n_row, n_rep, per_list, row_blocks
    )
    deep = n_hi // 2
    own = after(jnp.concatenate(own, axis=0), table)
    far = to_rep(own, 2)
    near = to_rep(own, 1)
    adj = densify(after(table, near), blocks, n_row, per_list, row_blocks)
    pieces = [own, near, far, to_rep(after(far, adj), 1)]

    send3, keep2 = forward(pieces, adj, 0)
    across = (keep2 + to_rep(send3, 1).astype(F32)).astype(BF16)
    arrived = to_rep(across, 2)
    send1, keep0 = forward(pieces, after(adj, across), 1)
    own_list = after(own_list, keep0)
    lists = [own_list] + [to_rep(own_list, j) for j in range(1, n_rep)]
    arrived = after(arrived, keep0, lists)
    factor = float(n_row * band_rows) ** (-0.5)
    output, to_near, grad0, wkeep = middle(keep0, to_rep(send1, 1), arrived, weight, out_grad, n_rep, factor)

    grad2 = to_rep(grad0, 2)
    first, w = back_first(to_rep(to_near, 1), grad0, adj, wkeep)
    grad2 = after(grad2, first)
    grad3 = to_rep(grad2, 1)
    send_high, keep_high = back_second(grad3, grad2, adj, first, 1, n_rep, deep)
    near_high = to_rep(send_high, 1)
    send_low, keep_low = back_second(grad3, grad2, adj, after(first, send_high), 0, n_rep, deep)
    near_low = to_rep(after(send_low, near_high), 1)
    part = features // n_rep

    def across_sum(keep, near):
        return (keep[:part] + near[:part].astype(F32)).astype(BF16)

    across_high = across_sum(keep_high, after(near_high, send_low))
    across_low = across_sum(keep_low, near_low)
    far_high = to_rep(across_high, 2)
    far_low = to_rep(across_low, 2)

    got = to_row(after(w, far_high), 1)
    messages = split((keep_low, near_low, far_low), (keep_high, near_high, far_high), n_row, n_rep)
    returned = lax.all_to_all(messages, "row", split_axis=0, concat_axis=0, tiled=True)
    w2 = after(w[part:] + got[part:], messages)
    w = w[:part] + got[:part] + to_rep(w2, 2)
    step = 2
    while step < n_row:
        w = w + to_row(w, step)
        step *= 2
    w = w.astype(BF16)
    grads = collect(lists, after(returned, w), w, per_list, row_blocks, blk)
    node_grad, weight_grad = finish([grads[0]] + [to_rep(grads[j], j) for j in range(1, n_rep)], w)
    return (output, weight_grad, node_grad)


def solution(mesh):
    in_specs = (
        P("row", None),
        P(),
        P(("row", "rep"), None),
        P(("row", "rep"), None, None),
        P(("row", "rep")),
        P(("row", "rep")),
        P(("row", "rep"), None, None),
        P(("row", "rep")),
    )
    out_specs = (P(("row", "rep"), None), P(), P(("row", "rep"), None))
    return jax.shard_map(local, mesh=mesh, in_specs=in_specs, out_specs=out_specs, check_vma=False)
```

```python
import functools

import jax
import jax.numpy as jnp
from jax import lax
from jax.experimental import pallas as pl
from jax.experimental.pallas import tpu as pltpu
from jax.sharding import PartitionSpec as P

BF16 = jnp.bfloat16
F32 = jnp.float32
COL_CHUNK = 16
LIST_STEP = 4
ROW_TILE = 256
COL_TILE = 512
WHOLE = pl.BlockSpec(memory_space=pltpu.VMEM)
SMEM = pl.BlockSpec(memory_space=pltpu.SMEM)
ANY = pl.BlockSpec(memory_space=pl.ANY)


def params(*parts):
    return pltpu.CompilerParams(vmem_limit_bytes=min(sum(parts) + (6 << 20), 62 << 20))


def shape(dims, dtype):
    return jax.ShapeDtypeStruct(tuple(dims), dtype)


def dot(a, b, dims=((1,), (0,))):
    return lax.dot_general(a, b, (dims, ((), ())), preferred_element_type=F32)


def xor_perm(count, offset):
    return [(i, i ^ offset) for i in range(count)]


def div_rem(x, n):
    if n & (n - 1) == 0:
        return x >> (n.bit_length() - 1), x & (n - 1)
    return lax.div(x, n), lax.rem(x, n)


class Table:
    def __init__(self, slots, cells):
        self.groups = cells // COL_CHUNK
        self.spare = cells
        self.first = 0
        self.second = cells + 1
        self.older = 2 * (cells + 1)
        self.wide_at = self.older + slots + 1
        self.wide_cell = self.wide_at + self.groups
        self.wide_next = self.wide_cell + slots
        self.size = -(-(self.wide_next + slots) // 128) * 128


def lists_body(rows_ref, fetch_ref, count_ref, out_ref, *, slots, n_rep, n_hi, per_list, quarter):
    r, q = lax.axis_index("row"), lax.axis_index("rep")
    all_cols = n_rep * n_hi * per_list
    chunks = all_cols // COL_CHUNK
    deep = n_hi // 2
    t = Table(slots, n_rep * quarter * all_cols)

    @pl.loop(0, t.older, unroll=16)
    def _(at):
        out_ref[at] = slots

    @pl.loop(0, t.groups, unroll=16)
    def _(at):
        out_ref[t.wide_at + at] = -1

    out_ref[t.older + slots] = slots

    live = count_ref[0]

    def place(slot):
        row_high, row_low = div_rem(rows_ref[slot], quarter)
        source, c = div_rem(fetch_ref[slot], per_list)
        hi, low = div_rem(source ^ r, n_rep)
        half, hi = div_rem(hi, deep)
        row = (n_rep - 1 - (row_high ^ q)) * quarter + row_low
        col = ((half * n_rep + (low ^ q)) * deep + hi) * per_list + c
        cell = jnp.where(slot < live, row * all_cols + col, t.spare)
        return cell, t.wide_at + row * chunks + div_rem(col, COL_CHUNK)[0]

    def link(slot, cell, at, wide):
        one, two, begin = out_ref[t.first + cell], out_ref[t.second + cell], out_ref[at]
        out_ref[t.first + cell] = slot
        out_ref[t.second + cell] = one
        out_ref[t.older + slot] = one
        full = (two != slots) & (slot < live)
        out_ref[t.wide_cell + wide] = cell
        out_ref[t.wide_next + wide] = begin
        out_ref[at] = jnp.where(full, wide, begin)
        return wide + full.astype(jnp.int32)

    def link_group(group, wide):
        begin = group * LIST_STEP
        places = [(begin + i, *place(begin + i)) for i in range(LIST_STEP)]
        for slot, cell, at in places:
            wide = link(slot, cell, at, wide)
        return wide

    lax.fori_loop(0, lax.div(live + LIST_STEP - 1, LIST_STEP), link_group, jnp.int32(0))


def slot_lists(block_rows, block_fetch, block_count, n_row, n_rep, per_list, row_blocks):
    slots = block_rows.shape[0]
    body = functools.partial(
        lists_body,
        slots=slots,
        n_rep=n_rep,
        n_hi=n_row // n_rep,
        per_list=per_list,
        quarter=row_blocks // n_rep,
    )
    return pl.pallas_call(
        body,
        out_shape=shape((Table(slots, row_blocks * n_row * per_list).size,), jnp.int32),
        in_specs=[SMEM] * 3,
        out_specs=SMEM,
        compiler_params=pltpu.CompilerParams(vmem_limit_bytes=56 << 20),
        cost_estimate=pl.CostEstimate(flops=3 << 30, bytes_accessed=8 * slots, transcendentals=0),
        name="slot_lists",
    )(block_rows, block_fetch, block_count)


def densify_body(table_ref, held, out_ref, *, all_cols, row_blocks):
    chunk, row_cell = pl.program_id(0), pl.program_id(1)
    slots, blk = held.shape[0], held.shape[1]
    t = Table(slots, row_blocks * all_cols)
    zero = jnp.zeros((blk, blk), BF16)

    def block(slot):
        return jnp.where(slot < slots, held[jnp.minimum(slot, slots - 1)], zero)

    for col in range(COL_CHUNK):
        cell = row_cell * all_cols + chunk * COL_CHUNK + col
        total = block(table_ref[t.first + cell]) + block(table_ref[t.second + cell])
        out_ref[:, col * blk : (col + 1) * blk] = total

    def redo(wide):
        cell = table_ref[t.wide_cell + wide]
        two = table_ref[t.second + cell]
        three = table_ref[t.older + two]
        four = table_ref[t.older + three]
        total = held[table_ref[t.first + cell]].astype(F32) + held[two].astype(F32)
        total = total + (held[three].astype(F32) + block(four).astype(F32))
        col = cell - row_cell * all_cols - chunk * COL_CHUNK
        place = (slice(None), pl.ds(pl.multiple_of(col * blk, blk), blk))
        out_ref[place] = total.astype(BF16)
        five = table_ref[t.older + four]

        @pl.when(five < slots)
        def _():
            def more(carry):
                slot, total = carry
                return table_ref[t.older + slot], total + held[slot].astype(F32)

            _, rest = lax.while_loop(lambda carry: carry[0] < slots, more, (five, total))
            out_ref[place] = rest.astype(BF16)

        return table_ref[t.wide_next + wide]

    begin = table_ref[t.wide_at + row_cell * (all_cols // COL_CHUNK) + chunk]
    lax.while_loop(lambda wide: wide >= 0, redo, begin)


def densify(table, blocks, n_row, per_list, row_blocks):
    slots, blk, _ = blocks.shape
    all_cols = n_row * per_list
    width = COL_CHUNK * blk
    return pl.pallas_call(
        functools.partial(densify_body, all_cols=all_cols, row_blocks=row_blocks),
        out_shape=shape((row_blocks * blk, all_cols * blk), BF16),
        grid_spec=pltpu.PrefetchScalarGridSpec(
            num_scalar_prefetch=1,
            grid=(all_cols // COL_CHUNK, row_blocks),
            in_specs=[WHOLE],
            out_specs=pl.BlockSpec((blk, width), lambda c, i, *_: (i, c)),
        ),
        compiler_params=params(blocks.size * 2, blk * width * 4),
        cost_estimate=pl.CostEstimate(
            flops=slots * blk * blk,
            bytes_accessed=blocks.size * 2 + 2 * all_cols * row_blocks * blk * blk,
            transcendentals=0,
        ),
        name="densify",
    )(table, blocks)


def pack_body(*refs, n_hi, per_list, blk):
    lists = refs[:n_hi]
    features = refs[n_hi]
    outs = refs[n_hi + 1 : 2 * n_hi + 1]
    own_list, sems = refs[2 * n_hi + 1 :]
    r = lax.axis_index("row")
    copies = []
    for hi in range(n_hi):
        for c in range(per_list):
            b = lists[hi][0, r, c]
            own_list[hi * per_list + c] = b
            copy = pltpu.make_async_copy(
                features.at[pl.ds(pl.multiple_of(b * blk, blk), blk)],
                outs[hi].at[pl.ds(c * blk, blk)],
                sems.at[hi * per_list + c],
            )
            copy.start()
            copies.append(copy)
    for copy in copies:
        copy.wait()


def pack(lists, features, per_list, blk):
    n_hi = len(lists)
    return pl.pallas_call(
        functools.partial(pack_body, n_hi=n_hi, per_list=per_list, blk=blk),
        out_shape=[shape((per_list * blk, features.shape[1]), BF16)] * n_hi + [shape((128,), jnp.int32)],
        in_specs=[SMEM] * n_hi + [pl.BlockSpec(memory_space=pltpu.HBM)],
        out_specs=[ANY] * n_hi + [SMEM],
        scratch_shapes=[pltpu.SemaphoreType.DMA((n_hi * per_list,))],
        compiler_params=pltpu.CompilerParams(vmem_limit_bytes=53 << 20),
        name="pack",
    )(*lists, features)


def forward_body(*refs, n_rep):
    pieces = refs[:n_rep]
    adj_ref, send_ref, keep_ref = refs[n_rep:]
    i = pl.program_id(0)
    depth = pieces[0].shape[0] // 2
    total = 0.0
    for half in range(2):
        for j in range(n_rep):
            at = (half * n_rep + j) * depth
            total += dot(adj_ref[:, at : at + depth], pieces[j][half * depth : (half + 1) * depth])

    half = pl.num_programs(0) // 2

    @pl.when(i < half)
    def _():
        send_ref[...] = total.astype(BF16)

    @pl.when(i >= half)
    def _():
        keep_ref[...] = total


def forward(pieces, adj, half_index):
    rows, cols = adj.shape[0] // 2, adj.shape[1]
    features = pieces[0].shape[1]
    tiles = rows // ROW_TILE
    half = tiles // 2
    return pl.pallas_call(
        functools.partial(forward_body, n_rep=len(pieces)),
        grid=(tiles,),
        out_shape=[shape((rows // 2, features), BF16), shape((rows // 2, features), F32)],
        in_specs=[pl.BlockSpec(x.shape, lambda i: (0, 0)) for x in pieces]
        + [pl.BlockSpec((ROW_TILE, cols), lambda i: (i + half_index * tiles, 0))],
        out_specs=[
            pl.BlockSpec((ROW_TILE, features), lambda i: (jnp.minimum(i, half - 1), 0)),
            pl.BlockSpec((ROW_TILE, features), lambda i: (jnp.maximum(i - half, 0), 0)),
        ],
        compiler_params=params(ROW_TILE * cols * 4, cols * features * 4),
        cost_estimate=pl.CostEstimate(
            flops=2 * rows * cols * features, bytes_accessed=adj.size + cols * features * 2, transcendentals=0
        ),
        name="forward",
    )(*pieces, adj)


def middle_body(
    keep_ref, near_ref, far_ref, weight_ref, cot_ref, out_ref, near_out, far_out, wkeep_ref, acc_ref, *, factor
):
    q = lax.axis_index("rep")
    hidden = (keep_ref[...] + near_ref[...].astype(F32) + far_ref[...].astype(F32)).astype(BF16)
    weight = weight_ref[...]
    pre_act = dot(hidden, weight)
    sig = jax.nn.sigmoid(pre_act)
    pre_grad = (cot_ref[...].astype(F32) * (sig * (1.0 + pre_act * (1.0 - sig)))).astype(BF16)
    features, rows = weight.shape[0], hidden.shape[0]
    input_grad = dot(weight, pre_grad, ((1,), (1,))).astype(BF16)
    near_out[:features] = input_grad
    far_out[...] = input_grad
    out_ref[...] = (pre_act * sig).astype(BF16)
    acc_ref[...] = dot(hidden, pre_grad, ((0,), (0,))) * factor
    part = wkeep_ref.shape[0] // 2
    for j in range(4):
        piece = acc_ref[pl.ds(pl.multiple_of((q ^ j) * part, part), part), :]
        if j & 1:
            fold_in(near_out, features, j // 2, piece)
        else:
            wkeep_ref[j // 2 * part : (j // 2 + 1) * part] = piece


def fold_in(ref, base, at, piece):
    part, features = piece.shape
    folds = ref.shape[1] // features
    depth = part // folds
    for i in range(folds):
        ref[base + at * depth : base + (at + 1) * depth, i * features : (i + 1) * features] = piece[
            i * depth : (i + 1) * depth
        ].astype(ref.dtype)


def fold_out(ref, base, at, part, features):
    folds = ref.shape[1] // features
    depth = part // folds
    rows = ref[base + at * depth : base + (at + 1) * depth, :].astype(F32)
    return jnp.concatenate([rows[:, i * features : (i + 1) * features] for i in range(folds)], axis=0)


def middle(keep, near, far, weight, cot, n_rep, factor):
    rows, features = keep.shape
    part = features // n_rep
    extra = part * features // rows
    return pl.pallas_call(
        functools.partial(middle_body, factor=factor),
        out_shape=[
            shape((rows, features), BF16),
            shape((features + 2 * extra, rows), BF16),
            shape((features, rows), BF16),
            shape((2 * part, features), F32),
        ],
        in_specs=[WHOLE] * 5,
        out_specs=[WHOLE] * 4,
        scratch_shapes=[pltpu.VMEM((features, features), F32)],
        compiler_params=params(12 << 20),
        cost_estimate=pl.CostEstimate(
            flops=6 * rows * features * features, bytes_accessed=rows * features * 14, transcendentals=rows * features
        ),
        name="middle",
    )(keep, near, far, weight, cot)


def back_first_body(odd_ref, even_ref, adj_ref, wkeep_ref, out_ref, w_out):
    features, rows = out_ref.shape[0], odd_ref.shape[1]
    out_ref[...] = dot(odd_ref[:features], adj_ref[:rows]) + dot(even_ref[...], adj_ref[rows:])

    @pl.when(pl.program_id(0) == 0)
    def _():
        part = w_out.shape[0] // 2
        for at in range(2):
            rows_here = slice(at * part, (at + 1) * part)
            w_out[rows_here] = wkeep_ref[rows_here] + fold_out(odd_ref, features, at, part, features)


def back_first(odd, even, adj, wkeep):
    rows, cols = adj.shape[0] // 2, adj.shape[1]
    features = wkeep.shape[1]
    whole = lambda x: pl.BlockSpec(x.shape, lambda i: (0, 0))
    return pl.pallas_call(
        back_first_body,
        grid=(cols // COL_TILE,),
        out_shape=[shape((features, cols), F32), shape(wkeep.shape, F32)],
        in_specs=[whole(odd), whole(even), pl.BlockSpec((rows, COL_TILE), lambda i: (1, i)), whole(wkeep)],
        out_specs=[pl.BlockSpec((features, COL_TILE), lambda i: (0, i)), whole(wkeep)],
        compiler_params=params(4 << 20),
        cost_estimate=pl.CostEstimate(
            flops=2 * rows * cols * features, bytes_accessed=adj.size + cols * features * 4, transcendentals=0
        ),
        name="back_first",
    )(odd, even, adj, wkeep)


def back_second_body(odd_ref, even_ref, adj_ref, first_ref, send_ref, keep_ref, acc_ref):
    q = lax.axis_index("rep")
    rows = odd_ref.shape[1]
    acc_ref[...] = first_ref[...] + dot(odd_ref[...], adj_ref[:rows]) + dot(even_ref[...], adj_ref[rows:])
    part = send_ref.shape[0] // 2
    for j in range(4):
        out = send_ref if j & 1 else keep_ref
        at = (3 - j) // 2 * part
        piece = acc_ref[pl.ds(pl.multiple_of((q ^ j) * part, part), part), :]
        out[at : at + part] = piece.astype(out.dtype)


def back_second(odd, even, adj, first, half, n_rep, per_piece):
    rows, cols = adj.shape[0] // 2, adj.shape[1] // 2
    features = first.shape[0]
    width = cols // n_rep // per_piece
    tiles = cols // width
    whole = lambda x: pl.BlockSpec(x.shape, lambda i: (0, 0))
    return pl.pallas_call(
        back_second_body,
        grid=(tiles,),
        out_shape=[shape((features // 2, cols), BF16), shape((features // 2, cols), F32)],
        in_specs=[
            whole(odd),
            whole(even),
            pl.BlockSpec((rows, width), lambda i: (0, i + half * tiles)),
            pl.BlockSpec((features, width), lambda i: (0, i + half * tiles)),
        ],
        out_specs=[
            pl.BlockSpec(
                (features // 2, width), lambda i: (0, (lax.div(i, per_piece) ^ 1) * per_piece + lax.rem(i, per_piece))
            ),
            pl.BlockSpec((features // 2, width), lambda i: (0, i)),
        ],
        scratch_shapes=[pltpu.VMEM((features, width), F32)],
        compiler_params=params(4 << 20),
        cost_estimate=pl.CostEstimate(
            flops=2 * rows * cols * features, bytes_accessed=rows * cols * 2 + cols * features * 7, transcendentals=0
        ),
        name=f"back_second_{half}",
    )(odd, even, adj, first)


def across_body(low_ref, low_near, high_ref, high_near, out_ref):
    part, cols = out_ref.shape[0], low_ref.shape[1]
    for half, (keep, near) in enumerate(((low_ref, low_near), (high_ref, high_near))):
        out_ref[:, half * cols : (half + 1) * cols] = (keep[:part] + near[:part].astype(F32)).astype(BF16)


def across_sum(keep_low, near_low, keep_high, near_high):
    rows, cols = keep_low.shape
    return pl.pallas_call(
        across_body,
        out_shape=shape((rows // 2, 2 * cols), BF16),
        in_specs=[WHOLE] * 4,
        out_specs=WHOLE,
        compiler_params=params(rows * cols * 14),
        cost_estimate=pl.CostEstimate(flops=rows * cols, bytes_accessed=rows * cols * 8, transcendentals=0),
        name="across_sum",
    )(keep_low, near_low, keep_high, near_high)


def split_body(low_ref, low_near, high_ref, high_near, far_ref, out_ref, *, n_rep, deep):
    r, q = lax.axis_index("row"), lax.axis_index("rep")
    _, part, width = out_ref.shape
    per_half = n_rep * deep
    for half, (own, near) in enumerate(((low_ref, low_near), (high_ref, high_near))):
        for i in range(per_half):
            low, hi = i % n_rep, i // n_rep
            j = low ^ q
            cols = pl.ds(pl.multiple_of((j * deep + hi) * width, width), width)
            far_cols = pl.ds(pl.multiple_of((half * per_half + (j ^ 2) * deep + hi) * width, width), width)
            total = own[part:, cols] + near[part:, cols].astype(F32) + far_ref[:, far_cols].astype(F32)
            out_ref[r ^ (half * per_half + i)] = total.astype(BF16)


def split(keep_low, near_low, keep_high, near_high, far, n_row, n_rep):
    part, cols = far.shape
    return pl.pallas_call(
        functools.partial(split_body, n_rep=n_rep, deep=n_row // n_rep // 2),
        out_shape=shape((n_row, part, cols // n_row), BF16),
        in_specs=[WHOLE] * 5,
        out_specs=WHOLE,
        compiler_params=params(cols * part * 20),
        cost_estimate=pl.CostEstimate(flops=2 * part * cols, bytes_accessed=part * cols * 10, transcendentals=0),
        name="split",
    )(keep_low, near_low, keep_high, near_high, far)


def collect_body(*refs, n_row, n_rep, per_list, quarter, blk):
    lists = refs[:n_rep]
    messages, w_ref = refs[n_rep : n_rep + 2]
    outs, acc_ref = refs[n_rep + 2 : -1], refs[-1]
    r, q = lax.axis_index("row"), lax.axis_index("rep")
    acc_ref[...] = jnp.zeros(acc_ref.shape, F32)
    for k in range(n_row):
        j = (k % n_rep) ^ q
        for c in range(per_list):
            at = k // n_rep * per_list + c
            b = lists[0][at]
            for other in range(1, n_rep):
                b = jnp.where(j == other, lists[other][at], b)
            cell = (lax.div(b, quarter) ^ q) * quarter + lax.rem(b, quarter)
            cols = pl.ds(pl.multiple_of(cell * blk, blk), blk)
            acc_ref[:, cols] += messages[r ^ k, :, c * blk : (c + 1) * blk].astype(F32)
    width = outs[0].shape[1]
    part = acc_ref.shape[0]
    for j, out in enumerate(outs):
        out[:part] = acc_ref[:, j * width : (j + 1) * width].astype(out.dtype)
        if j:
            fold_in(out, part, 0, w_ref[...])


def collect(lists, messages, w, per_list, row_blocks, blk):
    n_rep = len(lists)
    n_row, part, _ = messages.shape
    quarter = row_blocks // n_rep
    body = functools.partial(
        collect_body, n_row=n_row, n_rep=n_rep, per_list=per_list, quarter=quarter, blk=blk
    )
    return pl.pallas_call(
        body,
        out_shape=[shape((part, quarter * blk), F32)]
        + [shape((part + w.size // (quarter * blk), quarter * blk), BF16)] * (n_rep - 1),
        in_specs=[SMEM] * n_rep + [WHOLE] * 2,
        out_specs=[WHOLE] * n_rep,
        scratch_shapes=[pltpu.VMEM((part, row_blocks * blk), F32)],
        compiler_params=params(4 << 20),
        cost_estimate=pl.CostEstimate(
            flops=part * row_blocks * blk, bytes_accessed=part * row_blocks * blk * 5, transcendentals=0
        ),
        name="collect",
    )(*lists, messages, w)


def finish_body(*refs, n_rep):
    grads = refs[:n_rep]
    w_ref, node_ref, weight_ref, acc_ref = refs[n_rep:]
    q = lax.axis_index("rep")
    part = w_ref.shape[0]
    for j in range(n_rep):
        rows = pl.ds(pl.multiple_of((q ^ j) * part, part), part)
        acc_ref[rows, :] = grads[j][:part].astype(F32)
        weight_ref[rows, :] = fold_out(grads[j], part, 0, *w_ref.shape) if j else w_ref[...].astype(F32)
    node_ref[...] = acc_ref[...].T


def finish(grads, w):
    n_rep = len(grads)
    part, rows = grads[0].shape
    features = w.shape[1]
    return pl.pallas_call(
        functools.partial(finish_body, n_rep=n_rep),
        out_shape=[shape((rows, part * n_rep), F32), shape((features, features), F32)],
        in_specs=[WHOLE] * (n_rep + 1),
        out_specs=[WHOLE] * 2,
        scratch_shapes=[pltpu.VMEM((part * n_rep, rows), F32)],
        compiler_params=params(6 << 20),
        cost_estimate=pl.CostEstimate(flops=0, bytes_accessed=rows * part * n_rep * 8, transcendentals=0),
        name="finish",
    )(*grads, w)


def local(
    node_features, weight, out_grad, blocks, block_rows, block_fetch, fetch_lists, block_count
):
    n_row = lax.axis_size("row")
    n_rep = lax.axis_size("rep")
    n_hi = n_row // n_rep
    band_rows, features = node_features.shape
    blk = blocks.shape[1]
    row_blocks = band_rows // blk
    per_list = fetch_lists.shape[2]

    def to_rep(x, j):
        return lax.ppermute(x, "rep", xor_perm(n_rep, j))

    def to_row(x, k):
        return lax.ppermute(x, "row", xor_perm(n_row, k))

    def spread(x, hi):
        perm = [
            (r * n_rep + q, (r ^ (hi * n_rep + q)) * n_rep + q) for r in range(n_row) for q in range(n_rep)
        ]
        return lax.ppermute(x, ("row", "rep"), perm)

    def after(x, *done):
        return lax.optimization_barrier((x, *done))[0]

    wanted = [spread(fetch_lists, hi) for hi in range(n_hi)]
    *outgoing, own_list = pack(wanted, node_features, per_list, blk)
    own = [spread(x, hi) for hi, x in enumerate(outgoing)]
    table = slot_lists(
        block_rows, block_fetch, after(block_count, outgoing), n_row, n_rep, per_list, row_blocks
    )
    deep = n_hi // 2
    own = after(jnp.concatenate(own, axis=0), table)
    far = to_rep(own, 2)
    near = to_rep(own, 1)
    adj = densify(after(table, near), blocks, n_row, per_list, row_blocks)
    pieces = [own, near, far, to_rep(after(far, adj), 1)]

    send3, keep2 = forward(pieces, adj, 0)
    across = (keep2 + to_rep(send3, 1).astype(F32)).astype(BF16)
    arrived = to_rep(across, 2)
    send1, keep0 = forward(pieces, after(adj, across), 1)
    own_list = after(own_list, keep0)
    lists = [own_list] + [to_rep(own_list, j) for j in range(1, n_rep)]
    arrived = after(arrived, keep0, lists)
    factor = float(n_row * band_rows) ** (-0.5)
    output, to_near, grad0, wkeep = middle(keep0, to_rep(send1, 1), arrived, weight, out_grad, n_rep, factor)

    grad2 = to_rep(grad0, 2)
    first, w = back_first(to_rep(to_near, 1), grad0, adj, wkeep)
    w = w + to_row(w, 1)
    grad2 = after(grad2, first, w)
    grad3 = to_rep(grad2, 1)
    part = features // n_rep
    got = to_rep(w[part:], 2)
    send_high, keep_high = back_second(grad3, grad2, adj, first, 1, n_rep, deep)
    send_high = after(send_high, got)
    near_high = to_rep(send_high, 1)
    send_low, keep_low = back_second(grad3, grad2, adj, after(first, send_high), 0, n_rep, deep)
    near_low = to_rep(after(send_low, near_high), 1)
    across = across_sum(keep_low, near_low, keep_high, near_high)
    far = to_rep(across, 2)
    w = after(w[:part], across) + got
    step = 2
    while step < n_row:
        w = w + to_row(w, step)
        step *= 2
    messages = split(keep_low, near_low, keep_high, near_high, after(far, w), n_row, n_rep)
    returned = lax.all_to_all(messages, "row", split_axis=0, concat_axis=0, tiled=True)
    w = w.astype(BF16)
    grads = collect(lists, returned, w, per_list, row_blocks, blk)
    node_grad, weight_grad = finish([grads[0]] + [to_rep(grads[j], j) for j in range(1, n_rep)], w)
    return (output, weight_grad, node_grad)


def solution(mesh):
    in_specs = (
        P("row", None),
        P(),
        P(("row", "rep"), None),
        P(("row", "rep"), None, None),
        P(("row", "rep")),
        P(("row", "rep")),
        P(("row", "rep"), None, None),
        P(("row", "rep")),
    )
    out_specs = (P(("row", "rep"), None), P(), P(("row", "rep"), None))
    return jax.shard_map(local, mesh=mesh, in_specs=in_specs, out_specs=out_specs, check_vma=False)
```

```python
import functools

import jax
import jax.numpy as jnp
from jax import lax
from jax.experimental import pallas as pl
from jax.experimental.pallas import tpu as pltpu
from jax.sharding import PartitionSpec as P

BF16 = jnp.bfloat16
F32 = jnp.float32
COL_CHUNK = 16
LIST_STEP = 4
ROW_TILE = 256
COL_TILE = 512
WHOLE = pl.BlockSpec(memory_space=pltpu.VMEM)
SMEM = pl.BlockSpec(memory_space=pltpu.SMEM)
ANY = pl.BlockSpec(memory_space=pl.ANY)


def params(*parts):
    return pltpu.CompilerParams(vmem_limit_bytes=min(sum(parts) + (6 << 20), 62 << 20))


def shape(dims, dtype):
    return jax.ShapeDtypeStruct(tuple(dims), dtype)


def dot(a, b, dims=((1,), (0,))):
    return lax.dot_general(a, b, (dims, ((), ())), preferred_element_type=F32)


def xor_perm(count, offset):
    return [(i, i ^ offset) for i in range(count)]


def div_rem(x, n):
    if n & (n - 1) == 0:
        return x >> (n.bit_length() - 1), x & (n - 1)
    return lax.div(x, n), lax.rem(x, n)


def turned(low):
    return ((low & 1) << 1) | (low >> 1)


class Table:
    def __init__(self, slots, cells):
        self.groups = cells // COL_CHUNK
        self.spare = cells
        self.first = 0
        self.second = cells + 1
        self.older = 2 * (cells + 1)
        self.wide_at = self.older + slots + 1
        self.wide_cell = self.wide_at + self.groups
        self.wide_next = self.wide_cell + slots
        self.size = -(-(self.wide_next + slots) // 128) * 128


def lists_body(rows_ref, fetch_ref, count_ref, out_ref, *, slots, n_rep, n_hi, per_list, quarter):
    r, q = lax.axis_index("row"), lax.axis_index("rep")
    all_cols = n_rep * n_hi * per_list
    chunks = all_cols // COL_CHUNK
    deep = n_hi // 2
    t = Table(slots, n_rep * quarter * all_cols)

    @pl.loop(0, t.older, unroll=16)
    def _(at):
        out_ref[at] = slots

    @pl.loop(0, t.groups, unroll=16)
    def _(at):
        out_ref[t.wide_at + at] = -1

    out_ref[t.older + slots] = slots

    live = count_ref[0]

    def place(slot):
        row_high, row_low = div_rem(rows_ref[slot], quarter)
        source, c = div_rem(fetch_ref[slot], per_list)
        hi, low = div_rem(source ^ r, n_rep)
        half, hi = div_rem(hi, deep)
        row = (n_rep - 1 - (row_high ^ q)) * quarter + row_low
        col = ((half * n_rep + (turned(low) ^ q)) * deep + hi) * per_list + c
        cell = jnp.where(slot < live, row * all_cols + col, t.spare)
        return cell, t.wide_at + row * chunks + div_rem(col, COL_CHUNK)[0]

    def link(slot, cell, at, wide):
        one, two, begin = out_ref[t.first + cell], out_ref[t.second + cell], out_ref[at]
        out_ref[t.first + cell] = slot
        out_ref[t.second + cell] = one
        out_ref[t.older + slot] = one
        full = (two != slots) & (slot < live)
        out_ref[t.wide_cell + wide] = cell
        out_ref[t.wide_next + wide] = begin
        out_ref[at] = jnp.where(full, wide, begin)
        return wide + full.astype(jnp.int32)

    def link_group(group, wide):
        begin = group * LIST_STEP
        places = [(begin + i, *place(begin + i)) for i in range(LIST_STEP)]
        for slot, cell, at in places:
            wide = link(slot, cell, at, wide)
        return wide

    lax.fori_loop(0, lax.div(live + LIST_STEP - 1, LIST_STEP), link_group, jnp.int32(0))


def slot_lists(block_rows, block_fetch, block_count, n_row, n_rep, per_list, row_blocks):
    slots = block_rows.shape[0]
    body = functools.partial(
        lists_body,
        slots=slots,
        n_rep=n_rep,
        n_hi=n_row // n_rep,
        per_list=per_list,
        quarter=row_blocks // n_rep,
    )
    return pl.pallas_call(
        body,
        out_shape=shape((Table(slots, row_blocks * n_row * per_list).size,), jnp.int32),
        in_specs=[SMEM] * 3,
        out_specs=SMEM,
        compiler_params=pltpu.CompilerParams(vmem_limit_bytes=56 << 20),
        cost_estimate=pl.CostEstimate(flops=3 << 30, bytes_accessed=8 * slots, transcendentals=0),
        name="slot_lists",
    )(block_rows, block_fetch, block_count)


def densify_body(table_ref, held, out_ref, *, all_cols, row_blocks):
    chunk, row_cell = pl.program_id(0), pl.program_id(1)
    slots, blk = held.shape[0], held.shape[1]
    t = Table(slots, row_blocks * all_cols)
    zero = jnp.zeros((blk, blk), BF16)

    def block(slot):
        return jnp.where(slot < slots, held[jnp.minimum(slot, slots - 1)], zero)

    for col in range(COL_CHUNK):
        cell = row_cell * all_cols + chunk * COL_CHUNK + col
        total = block(table_ref[t.first + cell]) + block(table_ref[t.second + cell])
        out_ref[:, col * blk : (col + 1) * blk] = total

    def redo(wide):
        cell = table_ref[t.wide_cell + wide]
        two = table_ref[t.second + cell]
        three = table_ref[t.older + two]
        four = table_ref[t.older + three]
        total = held[table_ref[t.first + cell]].astype(F32) + held[two].astype(F32)
        total = total + (held[three].astype(F32) + block(four).astype(F32))
        col = cell - row_cell * all_cols - chunk * COL_CHUNK
        place = (slice(None), pl.ds(pl.multiple_of(col * blk, blk), blk))
        out_ref[place] = total.astype(BF16)
        five = table_ref[t.older + four]

        @pl.when(five < slots)
        def _():
            def more(carry):
                slot, total = carry
                return table_ref[t.older + slot], total + held[slot].astype(F32)

            _, rest = lax.while_loop(lambda carry: carry[0] < slots, more, (five, total))
            out_ref[place] = rest.astype(BF16)

        return table_ref[t.wide_next + wide]

    begin = table_ref[t.wide_at + row_cell * (all_cols // COL_CHUNK) + chunk]
    lax.while_loop(lambda wide: wide >= 0, redo, begin)


def densify(table, blocks, n_row, per_list, row_blocks):
    slots, blk, _ = blocks.shape
    all_cols = n_row * per_list
    width = COL_CHUNK * blk
    return pl.pallas_call(
        functools.partial(densify_body, all_cols=all_cols, row_blocks=row_blocks),
        out_shape=shape((row_blocks * blk, all_cols * blk), BF16),
        grid_spec=pltpu.PrefetchScalarGridSpec(
            num_scalar_prefetch=1,
            grid=(all_cols // COL_CHUNK, row_blocks),
            in_specs=[WHOLE],
            out_specs=pl.BlockSpec((blk, width), lambda c, i, *_: (i, c)),
        ),
        compiler_params=params(blocks.size * 2, blk * width * 4),
        cost_estimate=pl.CostEstimate(
            flops=slots * blk * blk,
            bytes_accessed=blocks.size * 2 + 2 * all_cols * row_blocks * blk * blk,
            transcendentals=0,
        ),
        name="densify",
    )(table, blocks)


def pack_body(*refs, n_hi, per_list, blk):
    lists = refs[:n_hi]
    features = refs[n_hi]
    outs = refs[n_hi + 1 : 2 * n_hi + 1]
    own_list, sems = refs[2 * n_hi + 1 :]
    r = lax.axis_index("row")
    copies = []
    for hi in range(n_hi):
        for c in range(per_list):
            b = lists[hi][0, r, c]
            own_list[hi * per_list + c] = b
            copy = pltpu.make_async_copy(
                features.at[pl.ds(pl.multiple_of(b * blk, blk), blk)],
                outs[hi].at[pl.ds(c * blk, blk)],
                sems.at[hi * per_list + c],
            )
            copy.start()
            copies.append(copy)
    for copy in copies:
        copy.wait()


def pack(lists, features, per_list, blk):
    n_hi = len(lists)
    return pl.pallas_call(
        functools.partial(pack_body, n_hi=n_hi, per_list=per_list, blk=blk),
        out_shape=[shape((per_list * blk, features.shape[1]), BF16)] * n_hi + [shape((128,), jnp.int32)],
        in_specs=[SMEM] * n_hi + [pl.BlockSpec(memory_space=pltpu.HBM)],
        out_specs=[ANY] * n_hi + [SMEM],
        scratch_shapes=[pltpu.SemaphoreType.DMA((n_hi * per_list,))],
        compiler_params=pltpu.CompilerParams(vmem_limit_bytes=53 << 20),
        name="pack",
    )(*lists, features)


def forward_body(*refs, n_rep):
    pieces = refs[: 2 * n_rep]
    adj_ref, send_ref, keep_ref = refs[2 * n_rep :]
    i = pl.program_id(0)
    depth = pieces[0].shape[0]
    total = 0.0
    for n, piece in enumerate(pieces):
        total += dot(adj_ref[:, n * depth : (n + 1) * depth], piece[...])

    half = pl.num_programs(0) // 2

    @pl.when(i < half)
    def _():
        send_ref[...] = total.astype(BF16)

    @pl.when(i >= half)
    def _():
        keep_ref[...] = total


def forward(pieces, adj, half_index):
    rows, cols = adj.shape[0] // 2, adj.shape[1]
    features = pieces[0].shape[1]
    tiles = rows // ROW_TILE
    half = tiles // 2
    return pl.pallas_call(
        functools.partial(forward_body, n_rep=len(pieces) // 2),
        grid=(tiles,),
        out_shape=[shape((rows // 2, features), BF16), shape((rows // 2, features), F32)],
        in_specs=[pl.BlockSpec(x.shape, lambda i: (0, 0)) for x in pieces]
        + [pl.BlockSpec((ROW_TILE, cols), lambda i: (i + half_index * tiles, 0))],
        out_specs=[
            pl.BlockSpec((ROW_TILE, features), lambda i: (jnp.minimum(i, half - 1), 0)),
            pl.BlockSpec((ROW_TILE, features), lambda i: (jnp.maximum(i - half, 0), 0)),
        ],
        compiler_params=params(ROW_TILE * cols * 4, cols * features * 4),
        cost_estimate=pl.CostEstimate(
            flops=2 * rows * cols * features, bytes_accessed=adj.size + cols * features * 2, transcendentals=0
        ),
        name="forward",
    )(*pieces, adj)


def middle_body(
    keep_ref, near_ref, far_ref, weight_ref, cot_ref, out_ref, near_out, far_out, wkeep_ref, acc_ref, *, factor
):
    q = lax.axis_index("rep")
    hidden = (keep_ref[...] + near_ref[...].astype(F32) + far_ref[...].astype(F32)).astype(BF16)
    weight = weight_ref[...]
    pre_act = dot(hidden, weight)
    sig = jax.nn.sigmoid(pre_act)
    pre_grad = (cot_ref[...].astype(F32) * (sig * (1.0 + pre_act * (1.0 - sig)))).astype(BF16)
    features, rows = weight.shape[0], hidden.shape[0]
    input_grad = dot(weight, pre_grad, ((1,), (1,))).astype(BF16)
    near_out[:features] = input_grad
    far_out[...] = input_grad
    out_ref[...] = (pre_act * sig).astype(BF16)
    acc_ref[...] = dot(hidden, pre_grad, ((0,), (0,))) * factor
    part = wkeep_ref.shape[0] // 2
    for j in range(4):
        piece = acc_ref[pl.ds(pl.multiple_of((q ^ j) * part, part), part), :]
        if j & 1:
            fold_in(near_out, features, j // 2, piece)
        else:
            wkeep_ref[j // 2 * part : (j // 2 + 1) * part] = piece


def fold_in(ref, base, at, piece):
    part, features = piece.shape
    folds = ref.shape[1] // features
    depth = part // folds
    for i in range(folds):
        ref[base + at * depth : base + (at + 1) * depth, i * features : (i + 1) * features] = piece[
            i * depth : (i + 1) * depth
        ].astype(ref.dtype)


def fold_out(ref, base, at, part, features):
    folds = ref.shape[1] // features
    depth = part // folds
    rows = ref[base + at * depth : base + (at + 1) * depth, :].astype(F32)
    return jnp.concatenate([rows[:, i * features : (i + 1) * features] for i in range(folds)], axis=0)


def middle(keep, near, far, weight, cot, n_rep, factor):
    rows, features = keep.shape
    part = features // n_rep
    extra = part * features // rows
    return pl.pallas_call(
        functools.partial(middle_body, factor=factor),
        out_shape=[
            shape((rows, features), BF16),
            shape((features + 2 * extra, rows), BF16),
            shape((features, rows), BF16),
            shape((2 * part, features), F32),
        ],
        in_specs=[WHOLE] * 5,
        out_specs=[WHOLE] * 4,
        scratch_shapes=[pltpu.VMEM((features, features), F32)],
        compiler_params=params(12 << 20),
        cost_estimate=pl.CostEstimate(
            flops=6 * rows * features * features, bytes_accessed=rows * features * 14, transcendentals=rows * features
        ),
        name="middle",
    )(keep, near, far, weight, cot)


def back_first_body(odd_ref, even_ref, adj_ref, wkeep_ref, out_ref, w_out):
    features, rows = out_ref.shape[0], odd_ref.shape[1]
    out_ref[...] = dot(odd_ref[:features], adj_ref[:rows]) + dot(even_ref[...], adj_ref[rows:])

    @pl.when(pl.program_id(0) == 0)
    def _():
        part = w_out.shape[0] // 2
        for at in range(2):
            rows_here = slice(at * part, (at + 1) * part)
            w_out[rows_here] = wkeep_ref[rows_here] + fold_out(odd_ref, features, at, part, features)


def back_first(odd, even, adj, wkeep):
    rows, cols = adj.shape[0] // 2, adj.shape[1]
    features = wkeep.shape[1]
    whole = lambda x: pl.BlockSpec(x.shape, lambda i: (0, 0))
    return pl.pallas_call(
        back_first_body,
        grid=(cols // COL_TILE,),
        out_shape=[shape((features, cols), F32), shape(wkeep.shape, F32)],
        in_specs=[whole(odd), whole(even), pl.BlockSpec((rows, COL_TILE), lambda i: (1, i)), whole(wkeep)],
        out_specs=[pl.BlockSpec((features, COL_TILE), lambda i: (0, i)), whole(wkeep)],
        compiler_params=params(4 << 20),
        cost_estimate=pl.CostEstimate(
            flops=2 * rows * cols * features, bytes_accessed=adj.size + cols * features * 4, transcendentals=0
        ),
        name="back_first",
    )(odd, even, adj, wkeep)


def back_second_body(odd_ref, even_ref, adj_ref, first_ref, send_ref, keep_ref, acc_ref):
    q = lax.axis_index("rep")
    rows = odd_ref.shape[1]
    acc_ref[...] = first_ref[...] + dot(odd_ref[...], adj_ref[:rows]) + dot(even_ref[...], adj_ref[rows:])
    part = send_ref.shape[0] // 2
    for j in range(4):
        out = send_ref if j & 1 else keep_ref
        at = (3 - j) // 2 * part
        piece = acc_ref[pl.ds(pl.multiple_of((q ^ j) * part, part), part), :]
        out[at : at + part] = piece.astype(out.dtype)


def back_second(odd, even, adj, first, half, n_rep, per_piece):
    rows, cols = adj.shape[0] // 2, adj.shape[1] // 2
    features = first.shape[0]
    width = cols // n_rep // per_piece
    tiles = cols // width
    whole = lambda x: pl.BlockSpec(x.shape, lambda i: (0, 0))
    return pl.pallas_call(
        back_second_body,
        grid=(tiles,),
        out_shape=[shape((features // 2, cols), BF16), shape((features // 2, cols), F32)],
        in_specs=[
            whole(odd),
            whole(even),
            pl.BlockSpec((rows, width), lambda i: (0, i + half * tiles)),
            pl.BlockSpec((features, width), lambda i: (0, i + half * tiles)),
        ],
        out_specs=[
            pl.BlockSpec(
                (features // 2, width), lambda i: (0, (lax.div(i, per_piece) ^ 1) * per_piece + lax.rem(i, per_piece))
            ),
            pl.BlockSpec((features // 2, width), lambda i: (0, i)),
        ],
        scratch_shapes=[pltpu.VMEM((features, width), F32)],
        compiler_params=params(4 << 20),
        cost_estimate=pl.CostEstimate(
            flops=2 * rows * cols * features, bytes_accessed=rows * cols * 2 + cols * features * 7, transcendentals=0
        ),
        name=f"back_second_{half}",
    )(odd, even, adj, first)


def across_body(low_ref, low_near, high_ref, high_near, out_ref):
    part, cols = out_ref.shape[0], low_ref.shape[1]
    for half, (keep, near) in enumerate(((low_ref, low_near), (high_ref, high_near))):
        out_ref[:, half * cols : (half + 1) * cols] = (keep[:part] + near[:part].astype(F32)).astype(BF16)


def across_sum(keep_low, near_low, keep_high, near_high):
    rows, cols = keep_low.shape
    return pl.pallas_call(
        across_body,
        out_shape=shape((rows // 2, 2 * cols), BF16),
        in_specs=[WHOLE] * 4,
        out_specs=WHOLE,
        compiler_params=params(rows * cols * 14),
        cost_estimate=pl.CostEstimate(flops=rows * cols, bytes_accessed=rows * cols * 8, transcendentals=0),
        name="across_sum",
    )(keep_low, near_low, keep_high, near_high)


def split_body(low_ref, low_near, high_ref, high_near, far_ref, out_ref, *, n_rep, deep):
    r, q = lax.axis_index("row"), lax.axis_index("rep")
    _, part, width = out_ref.shape
    per_half = n_rep * deep
    for half, (own, near) in enumerate(((low_ref, low_near), (high_ref, high_near))):
        for i in range(per_half):
            low, hi = i % n_rep, i // n_rep
            j = turned(low) ^ q
            cols = pl.ds(pl.multiple_of((j * deep + hi) * width, width), width)
            far_cols = pl.ds(pl.multiple_of((half * per_half + (j ^ 2) * deep + hi) * width, width), width)
            total = own[part:, cols] + near[part:, cols].astype(F32) + far_ref[:, far_cols].astype(F32)
            out_ref[r ^ (half * per_half + i)] = total.astype(BF16)


def split(keep_low, near_low, keep_high, near_high, far, n_row, n_rep):
    part, cols = far.shape
    return pl.pallas_call(
        functools.partial(split_body, n_rep=n_rep, deep=n_row // n_rep // 2),
        out_shape=shape((n_row, part, cols // n_row), BF16),
        in_specs=[WHOLE] * 5,
        out_specs=WHOLE,
        compiler_params=params(cols * part * 20),
        cost_estimate=pl.CostEstimate(flops=2 * part * cols, bytes_accessed=part * cols * 10, transcendentals=0),
        name="split",
    )(keep_low, near_low, keep_high, near_high, far)


def collect_body(*refs, n_row, n_rep, per_list, quarter, blk):
    lists = refs[:n_rep]
    messages, w_ref = refs[n_rep : n_rep + 2]
    outs, acc_ref = refs[n_rep + 2 : -1], refs[-1]
    r, q = lax.axis_index("row"), lax.axis_index("rep")
    acc_ref[...] = jnp.zeros(acc_ref.shape, F32)
    for k in range(n_row):
        j = turned(k % n_rep) ^ q
        for c in range(per_list):
            at = k // n_rep * per_list + c
            b = lists[0][at]
            for other in range(1, n_rep):
                b = jnp.where(j == other, lists[other][at], b)
            cell = (lax.div(b, quarter) ^ q) * quarter + lax.rem(b, quarter)
            cols = pl.ds(pl.multiple_of(cell * blk, blk), blk)
            acc_ref[:, cols] += messages[r ^ k, :, c * blk : (c + 1) * blk].astype(F32)
    width = outs[0].shape[1]
    part = acc_ref.shape[0]
    for j, out in enumerate(outs):
        out[:part] = acc_ref[:, j * width : (j + 1) * width].astype(out.dtype)
        if j:
            fold_in(out, part, 0, w_ref[...])


def collect(lists, messages, w, per_list, row_blocks, blk):
    n_rep = len(lists)
    n_row, part, _ = messages.shape
    quarter = row_blocks // n_rep
    body = functools.partial(
        collect_body, n_row=n_row, n_rep=n_rep, per_list=per_list, quarter=quarter, blk=blk
    )
    return pl.pallas_call(
        body,
        out_shape=[shape((part, quarter * blk), F32)]
        + [shape((part + w.size // (quarter * blk), quarter * blk), BF16)] * (n_rep - 1),
        in_specs=[SMEM] * n_rep + [WHOLE] * 2,
        out_specs=[WHOLE] * n_rep,
        scratch_shapes=[pltpu.VMEM((part, row_blocks * blk), F32)],
        compiler_params=params(4 << 20),
        cost_estimate=pl.CostEstimate(
            flops=part * row_blocks * blk, bytes_accessed=part * row_blocks * blk * 5, transcendentals=0
        ),
        name="collect",
    )(*lists, messages, w)


def finish_body(*refs, n_rep):
    grads = refs[:n_rep]
    w_ref, node_ref, weight_ref, acc_ref = refs[n_rep:]
    q = lax.axis_index("rep")
    part = w_ref.shape[0]
    for j in range(n_rep):
        rows = pl.ds(pl.multiple_of((q ^ j) * part, part), part)
        acc_ref[rows, :] = grads[j][:part].astype(F32)
        weight_ref[rows, :] = fold_out(grads[j], part, 0, *w_ref.shape) if j else w_ref[...].astype(F32)
    node_ref[...] = acc_ref[...].T


def finish(grads, w):
    n_rep = len(grads)
    part, rows = grads[0].shape
    features = w.shape[1]
    return pl.pallas_call(
        functools.partial(finish_body, n_rep=n_rep),
        out_shape=[shape((rows, part * n_rep), F32), shape((features, features), F32)],
        in_specs=[WHOLE] * (n_rep + 1),
        out_specs=[WHOLE] * 2,
        scratch_shapes=[pltpu.VMEM((part * n_rep, rows), F32)],
        compiler_params=params(6 << 20),
        cost_estimate=pl.CostEstimate(flops=0, bytes_accessed=rows * part * n_rep * 8, transcendentals=0),
        name="finish",
    )(*grads, w)


def local(
    node_features, weight, out_grad, blocks, block_rows, block_fetch, fetch_lists, block_count
):
    n_row = lax.axis_size("row")
    n_rep = lax.axis_size("rep")
    n_hi = n_row // n_rep
    band_rows, features = node_features.shape
    blk = blocks.shape[1]
    row_blocks = band_rows // blk
    per_list = fetch_lists.shape[2]

    def to_rep(x, j):
        return lax.ppermute(x, "rep", xor_perm(n_rep, j))

    def to_row(x, k):
        return lax.ppermute(x, "row", xor_perm(n_row, k))

    def spread(x, hi):
        perm = [
            (r * n_rep + q, (r ^ (hi * n_rep + turned(q))) * n_rep + q) for r in range(n_row) for q in range(n_rep)
        ]
        return lax.ppermute(x, ("row", "rep"), perm)

    def after(x, *done):
        return lax.optimization_barrier((x, *done))[0]

    wanted = [spread(fetch_lists, hi) for hi in range(n_hi)]
    *outgoing, own_list = pack(wanted, node_features, per_list, blk)
    own = [spread(x, hi) for hi, x in enumerate(outgoing)]
    deep = n_hi // 2
    low, high = [jnp.concatenate(own[half * deep : (half + 1) * deep], axis=0) for half in range(2)]
    low_far, low_near = to_rep(low, 2), to_rep(low, 1)
    table = slot_lists(
        block_rows, block_fetch, after(block_count, low_near), n_row, n_rep, per_list, row_blocks
    )
    high = after(high, low_far, table)
    high_far, high_near = to_rep(high, 2), to_rep(high, 1)
    adj = densify(after(table, high_near), blocks, n_row, per_list, row_blocks)
    low_diag = to_rep(after(low_far, high_near), 1)
    high_diag = to_rep(after(high_far, adj), 1)
    pieces = [low, low_near, low_far, low_diag, high, high_near, high_far, high_diag]

    send3, keep2 = forward(pieces, adj, 0)
    across = (keep2 + to_rep(send3, 1).astype(F32)).astype(BF16)
    arrived = to_rep(across, 2)
    send1, keep0 = forward(pieces, after(adj, across), 1)
    own_list = after(own_list, keep0)
    lists = [own_list] + [to_rep(own_list, j) for j in range(1, n_rep)]
    arrived = after(arrived, keep0, lists)
    factor = float(n_row * band_rows) ** (-0.5)
    output, to_near, grad0, wkeep = middle(keep0, to_rep(send1, 1), arrived, weight, out_grad, n_rep, factor)

    grad2 = to_rep(grad0, 2)
    first, w = back_first(to_rep(to_near, 1), grad0, adj, wkeep)
    w = w + to_row(w, 1)
    grad2 = after(grad2, first, w)
    grad3 = to_rep(grad2, 1)
    part = features // n_rep
    got = to_rep(w[part:], 2)
    send_high, keep_high = back_second(grad3, grad2, adj, first, 1, n_rep, deep)
    send_high = after(send_high, got)
    w = w[:part] + got
    got = to_row(w, 2)
    near_high = to_rep(send_high, 1)
    send_low, keep_low = back_second(grad3, grad2, adj, after(first, send_high), 0, n_rep, deep)
    near_low = to_rep(after(send_low, near_high, got), 1)
    across = across_sum(keep_low, near_low, keep_high, near_high)
    far = to_rep(across, 2)
    w = after(w, across) + got
    step = 4
    while step < n_row:
        w = w + to_row(w, step)
        step *= 2
    messages = split(keep_low, near_low, keep_high, near_high, after(far, w), n_row, n_rep)
    returned = lax.all_to_all(messages, "row", split_axis=0, concat_axis=0, tiled=True)
    w = w.astype(BF16)
    grads = collect(lists, returned, w, per_list, row_blocks, blk)
    node_grad, weight_grad = finish([grads[0]] + [to_rep(grads[j], j) for j in range(1, n_rep)], w)
    return (output, weight_grad, node_grad)


def solution(mesh):
    in_specs = (
        P("row", None),
        P(),
        P(("row", "rep"), None),
        P(("row", "rep"), None, None),
        P(("row", "rep")),
        P(("row", "rep")),
        P(("row", "rep"), None, None),
        P(("row", "rep")),
    )
    out_specs = (P(("row", "rep"), None), P(), P(("row", "rep"), None))
    return jax.shard_map(local, mesh=mesh, in_specs=in_specs, out_specs=out_specs, check_vma=False)
```

```python
import functools

import jax
import jax.numpy as jnp
from jax import lax
from jax.experimental import pallas as pl
from jax.experimental.pallas import tpu as pltpu
from jax.sharding import PartitionSpec as P

BF16 = jnp.bfloat16
F32 = jnp.float32
COL_CHUNK = 16
ROW_TILE = 256
COL_TILE = 512
WHOLE = pl.BlockSpec(memory_space=pltpu.VMEM)
SMEM = pl.BlockSpec(memory_space=pltpu.SMEM)
ANY = pl.BlockSpec(memory_space=pl.ANY)


def params(*parts):
    return pltpu.CompilerParams(vmem_limit_bytes=min(sum(parts) + (6 << 20), 62 << 20))


def shape(dims, dtype):
    return jax.ShapeDtypeStruct(tuple(dims), dtype)


def dot(a, b, dims=((1,), (0,))):
    return lax.dot_general(a, b, (dims, ((), ())), preferred_element_type=F32)


def xor_perm(count, offset):
    return [(i, i ^ offset) for i in range(count)]


def div_rem(x, n):
    if n & (n - 1) == 0:
        return x >> (n.bit_length() - 1), x & (n - 1)
    return lax.div(x, n), lax.rem(x, n)


def turned(low):
    return ((low & 1) << 1) | (low >> 1)


def lists_body(slots_ref, count_ref, out_ref, *, n_rep, n_hi, per_list, quarter):
    r, q = lax.axis_index("row"), lax.axis_index("rep")
    all_cols = n_rep * n_hi * per_list
    cells = n_rep * quarter * all_cols
    slots = slots_ref.shape[1]
    row_high, row_low = div_rem(slots_ref[0:1, :], quarter)
    source, c = div_rem(slots_ref[1:2, :], per_list)
    hi, low = div_rem(source ^ r, n_rep)
    half, hi = div_rem(hi, n_hi // 2)
    row = (n_rep - 1 - (row_high ^ q)) * quarter + row_low
    col = ((half * n_rep + (turned(low) ^ q)) * (n_hi // 2) + hi) * per_list + c
    across = lax.broadcasted_iota(jnp.int32, (1, slots), 1)
    cell = jnp.where(across < count_ref[0], row * all_cols + col, cells)
    down = lax.broadcasted_iota(jnp.int32, (slots, slots), 0)
    side = lax.broadcasted_iota(jnp.int32, (slots, slots), 1)
    cell_down = jnp.sum(jnp.where(down == side, jnp.broadcast_to(cell, (slots, slots)), 0), axis=1, keepdims=True)
    before = jnp.where((cell_down == cell) & (down < side), down, -1)
    out_ref[4:5, :slots] = jnp.max(before, axis=0, keepdims=True)
    width = 256
    for begin in range(0, cells, width):
        here = lax.broadcasted_iota(jnp.int32, (slots, width), 1) + begin
        slot = lax.broadcasted_iota(jnp.int32, (slots, width), 0)
        slot = jnp.where(cell_down == here, slot, -1)
        for depth in range(4):
            last = jnp.max(slot, axis=0, keepdims=True)
            out_ref[depth : depth + 1, begin : begin + width] = last
            slot = jnp.where(slot < last, slot, -1)


def slot_lists(block_rows, block_fetch, block_count, n_row, n_rep, per_list, row_blocks):
    cells = row_blocks * n_row * per_list
    body = functools.partial(
        lists_body, n_rep=n_rep, n_hi=n_row // n_rep, per_list=per_list, quarter=row_blocks // n_rep
    )
    return pl.pallas_call(
        body,
        out_shape=shape((8, cells), jnp.int32),
        in_specs=[WHOLE, SMEM],
        out_specs=WHOLE,
        compiler_params=params(8 << 20),
        cost_estimate=pl.CostEstimate(flops=3 << 30, bytes_accessed=32 * cells, transcendentals=0),
        name="slot_lists",
    )(jnp.stack([block_rows, block_fetch]), block_count)


def densify_body(table_ref, held, out_ref, *, all_cols):
    chunk, row_cell = pl.program_id(0), pl.program_id(1)
    blk = held.shape[1]
    base = row_cell * all_cols + chunk * COL_CHUNK
    zero = jnp.zeros((blk, blk), BF16)

    def block(slot):
        return jnp.where(slot >= 0, held[jnp.maximum(slot, 0)], zero)

    widest = jnp.int32(-1)
    for col in range(COL_CHUNK):
        cell = base + col
        out_ref[:, col * blk : (col + 1) * blk] = block(table_ref[0, cell]) + block(table_ref[1, cell])
        widest = jnp.maximum(widest, table_ref[2, cell])

    @pl.when(widest >= 0)
    def _():
        @pl.loop(0, COL_CHUNK)
        def _(col):
            cell = base + col
            one, two, three, four = (table_ref[depth, cell] for depth in range(4))

            @pl.when(three >= 0)
            def _():
                total = held[one].astype(F32) + held[two].astype(F32)
                total = total + (held[three].astype(F32) + block(four).astype(F32))
                place = (slice(None), pl.ds(pl.multiple_of(col * blk, blk), blk))
                out_ref[place] = total.astype(BF16)
                five = jnp.where(four >= 0, table_ref[4, jnp.maximum(four, 0)], -1)

                @pl.when(five >= 0)
                def _():
                    def more(carry):
                        slot, total = carry
                        return table_ref[4, slot], total + held[slot].astype(F32)

                    _, rest = lax.while_loop(lambda carry: carry[0] >= 0, more, (five, total))
                    out_ref[place] = rest.astype(BF16)


def densify(table, blocks, n_row, per_list, row_blocks):
    slots, blk, _ = blocks.shape
    all_cols = n_row * per_list
    width = COL_CHUNK * blk
    return pl.pallas_call(
        functools.partial(densify_body, all_cols=all_cols),
        out_shape=shape((row_blocks * blk, all_cols * blk), BF16),
        grid_spec=pltpu.PrefetchScalarGridSpec(
            num_scalar_prefetch=1,
            grid=(all_cols // COL_CHUNK, row_blocks),
            in_specs=[WHOLE],
            out_specs=pl.BlockSpec((blk, width), lambda c, i, *_: (i, c)),
        ),
        compiler_params=params(blocks.size * 2, blk * width * 4),
        cost_estimate=pl.CostEstimate(
            flops=slots * blk * blk,
            bytes_accessed=blocks.size * 2 + 2 * all_cols * row_blocks * blk * blk,
            transcendentals=0,
        ),
        name="densify",
    )(table, blocks)


def pack_body(*refs, n_hi, per_list, blk):
    lists = refs[:n_hi]
    features = refs[n_hi]
    outs = refs[n_hi + 1 : 2 * n_hi + 1]
    own_list, sems = refs[2 * n_hi + 1 :]
    r = lax.axis_index("row")
    copies = []
    for hi in range(n_hi):
        for c in range(per_list):
            b = lists[hi][0, r, c]
            own_list[hi * per_list + c] = b
            copy = pltpu.make_async_copy(
                features.at[pl.ds(pl.multiple_of(b * blk, blk), blk)],
                outs[hi].at[pl.ds(c * blk, blk)],
                sems.at[hi * per_list + c],
            )
            copy.start()
            copies.append(copy)
    for copy in copies:
        copy.wait()


def pack(lists, features, per_list, blk):
    n_hi = len(lists)
    return pl.pallas_call(
        functools.partial(pack_body, n_hi=n_hi, per_list=per_list, blk=blk),
        out_shape=[shape((per_list * blk, features.shape[1]), BF16)] * n_hi + [shape((128,), jnp.int32)],
        in_specs=[SMEM] * n_hi + [pl.BlockSpec(memory_space=pltpu.HBM)],
        out_specs=[ANY] * n_hi + [SMEM],
        scratch_shapes=[pltpu.SemaphoreType.DMA((n_hi * per_list,))],
        compiler_params=pltpu.CompilerParams(vmem_limit_bytes=53 << 20),
        name="pack",
    )(*lists, features)


def forward_body(*refs, n_rep):
    pieces = refs[: 2 * n_rep]
    adj_ref, send_ref, keep_ref = refs[2 * n_rep :]
    i = pl.program_id(0)
    depth = pieces[0].shape[0]
    total = 0.0
    for n, piece in enumerate(pieces):
        total += dot(adj_ref[:, n * depth : (n + 1) * depth], piece[...])

    half = pl.num_programs(0) // 2

    @pl.when(i < half)
    def _():
        send_ref[...] = total.astype(BF16)

    @pl.when(i >= half)
    def _():
        keep_ref[...] = total


def forward(pieces, adj, half_index):
    rows, cols = adj.shape[0] // 2, adj.shape[1]
    features = pieces[0].shape[1]
    tiles = rows // ROW_TILE
    half = tiles // 2
    return pl.pallas_call(
        functools.partial(forward_body, n_rep=len(pieces) // 2),
        grid=(tiles,),
        out_shape=[shape((rows // 2, features), BF16), shape((rows // 2, features), F32)],
        in_specs=[pl.BlockSpec(x.shape, lambda i: (0, 0)) for x in pieces]
        + [pl.BlockSpec((ROW_TILE, cols), lambda i: (i + half_index * tiles, 0))],
        out_specs=[
            pl.BlockSpec((ROW_TILE, features), lambda i: (jnp.minimum(i, half - 1), 0)),
            pl.BlockSpec((ROW_TILE, features), lambda i: (jnp.maximum(i - half, 0), 0)),
        ],
        compiler_params=params(ROW_TILE * cols * 4, cols * features * 4),
        cost_estimate=pl.CostEstimate(
            flops=2 * rows * cols * features, bytes_accessed=adj.size + cols * features * 2, transcendentals=0
        ),
        name="forward",
    )(*pieces, adj)


def middle_body(
    keep_ref, near_ref, far_ref, weight_ref, cot_ref, out_ref, near_out, far_out, wkeep_ref, acc_ref, *, factor
):
    q = lax.axis_index("rep")
    hidden = (keep_ref[...] + near_ref[...].astype(F32) + far_ref[...].astype(F32)).astype(BF16)
    weight = weight_ref[...]
    pre_act = dot(hidden, weight)
    sig = jax.nn.sigmoid(pre_act)
    pre_grad = (cot_ref[...].astype(F32) * (sig * (1.0 + pre_act * (1.0 - sig)))).astype(BF16)
    features, rows = weight.shape[0], hidden.shape[0]
    input_grad = dot(weight, pre_grad, ((1,), (1,))).astype(BF16)
    near_out[:features] = input_grad
    far_out[...] = input_grad
    out_ref[...] = (pre_act * sig).astype(BF16)
    acc_ref[...] = dot(hidden, pre_grad, ((0,), (0,))) * factor
    part = wkeep_ref.shape[0] // 2
    for j in range(4):
        piece = acc_ref[pl.ds(pl.multiple_of((q ^ j) * part, part), part), :]
        if j & 1:
            fold_in(near_out, features, j // 2, piece)
        else:
            wkeep_ref[j // 2 * part : (j // 2 + 1) * part] = piece


def fold_in(ref, base, at, piece):
    part, features = piece.shape
    folds = ref.shape[1] // features
    depth = part // folds
    for i in range(folds):
        ref[base + at * depth : base + (at + 1) * depth, i * features : (i + 1) * features] = piece[
            i * depth : (i + 1) * depth
        ].astype(ref.dtype)


def fold_out(ref, base, at, part, features):
    folds = ref.shape[1] // features
    depth = part // folds
    rows = ref[base + at * depth : base + (at + 1) * depth, :].astype(F32)
    return jnp.concatenate([rows[:, i * features : (i + 1) * features] for i in range(folds)], axis=0)


def middle(keep, near, far, weight, cot, n_rep, factor):
    rows, features = keep.shape
    part = features // n_rep
    extra = part * features // rows
    return pl.pallas_call(
        functools.partial(middle_body, factor=factor),
        out_shape=[
            shape((rows, features), BF16),
            shape((features + 2 * extra, rows), BF16),
            shape((features, rows), BF16),
            shape((2 * part, features), F32),
        ],
        in_specs=[WHOLE] * 5,
        out_specs=[WHOLE] * 4,
        scratch_shapes=[pltpu.VMEM((features, features), F32)],
        compiler_params=params(12 << 20),
        cost_estimate=pl.CostEstimate(
            flops=6 * rows * features * features, bytes_accessed=rows * features * 14, transcendentals=rows * features
        ),
        name="middle",
    )(keep, near, far, weight, cot)


def back_first_body(odd_ref, even_ref, adj_ref, wkeep_ref, out_ref, w_out):
    features, rows = out_ref.shape[0], odd_ref.shape[1]
    out_ref[...] = dot(odd_ref[:features], adj_ref[:rows]) + dot(even_ref[...], adj_ref[rows:])

    @pl.when(pl.program_id(0) == 0)
    def _():
        part = w_out.shape[0] // 2
        for at in range(2):
            rows_here = slice(at * part, (at + 1) * part)
            w_out[rows_here] = wkeep_ref[rows_here] + fold_out(odd_ref, features, at, part, features)


def back_first(odd, even, adj, wkeep):
    rows, cols = adj.shape[0] // 2, adj.shape[1]
    features = wkeep.shape[1]
    whole = lambda x: pl.BlockSpec(x.shape, lambda i: (0, 0))
    return pl.pallas_call(
        back_first_body,
        grid=(cols // COL_TILE,),
        out_shape=[shape((features, cols), F32), shape(wkeep.shape, F32)],
        in_specs=[whole(odd), whole(even), pl.BlockSpec((rows, COL_TILE), lambda i: (1, i)), whole(wkeep)],
        out_specs=[pl.BlockSpec((features, COL_TILE), lambda i: (0, i)), whole(wkeep)],
        compiler_params=params(4 << 20),
        cost_estimate=pl.CostEstimate(
            flops=2 * rows * cols * features, bytes_accessed=adj.size + cols * features * 4, transcendentals=0
        ),
        name="back_first",
    )(odd, even, adj, wkeep)


def back_second_body(odd_ref, even_ref, adj_ref, first_ref, send_ref, keep_ref, acc_ref):
    q = lax.axis_index("rep")
    rows = odd_ref.shape[1]
    acc_ref[...] = first_ref[...] + dot(odd_ref[...], adj_ref[:rows]) + dot(even_ref[...], adj_ref[rows:])
    part = send_ref.shape[0] // 2
    for j in range(4):
        out = send_ref if j & 1 else keep_ref
        at = (3 - j) // 2 * part
        piece = acc_ref[pl.ds(pl.multiple_of((q ^ j) * part, part), part), :]
        out[at : at + part] = piece.astype(out.dtype)


def back_second(odd, even, adj, first, half, n_rep, per_piece):
    rows, cols = adj.shape[0] // 2, adj.shape[1] // 2
    features = first.shape[0]
    width = cols // n_rep // per_piece
    tiles = cols // width
    whole = lambda x: pl.BlockSpec(x.shape, lambda i: (0, 0))
    return pl.pallas_call(
        back_second_body,
        grid=(tiles,),
        out_shape=[shape((features // 2, cols), BF16), shape((features // 2, cols), F32)],
        in_specs=[
            whole(odd),
            whole(even),
            pl.BlockSpec((rows, width), lambda i: (0, i + half * tiles)),
            pl.BlockSpec((features, width), lambda i: (0, i + half * tiles)),
        ],
        out_specs=[
            pl.BlockSpec(
                (features // 2, width), lambda i: (0, (lax.div(i, per_piece) ^ 1) * per_piece + lax.rem(i, per_piece))
            ),
            pl.BlockSpec((features // 2, width), lambda i: (0, i)),
        ],
        scratch_shapes=[pltpu.VMEM((features, width), F32)],
        compiler_params=params(4 << 20),
        cost_estimate=pl.CostEstimate(
            flops=2 * rows * cols * features, bytes_accessed=rows * cols * 2 + cols * features * 7, transcendentals=0
        ),
        name=f"back_second_{half}",
    )(odd, even, adj, first)


def across_body(low_ref, low_near, high_ref, high_near, out_ref):
    part, cols = out_ref.shape[0], low_ref.shape[1]
    for half, (keep, near) in enumerate(((low_ref, low_near), (high_ref, high_near))):
        out_ref[:, half * cols : (half + 1) * cols] = (keep[:part] + near[:part].astype(F32)).astype(BF16)


def across_sum(keep_low, near_low, keep_high, near_high):
    rows, cols = keep_low.shape
    return pl.pallas_call(
        across_body,
        out_shape=shape((rows // 2, 2 * cols), BF16),
        in_specs=[WHOLE] * 4,
        out_specs=WHOLE,
        compiler_params=params(rows * cols * 14),
        cost_estimate=pl.CostEstimate(flops=rows * cols, bytes_accessed=rows * cols * 8, transcendentals=0),
        name="across_sum",
    )(keep_low, near_low, keep_high, near_high)


def split_body(low_ref, low_near, high_ref, high_near, far_ref, w_ref, out_ref, *, n_rep, deep):
    r, q = lax.axis_index("row"), lax.axis_index("rep")
    part, width = far_ref.shape[0], out_ref.shape[2]
    depth = w_ref.shape[0] // 2
    w = w_ref[pl.ds(pl.multiple_of((r & 1) * depth, depth), depth), :].astype(BF16)
    per_half = n_rep * deep
    for half, (own, near) in enumerate(((low_ref, low_near), (high_ref, high_near))):
        for i in range(per_half):
            low, hi = i % n_rep, i // n_rep
            j = turned(low) ^ q
            cols = pl.ds(pl.multiple_of((j * deep + hi) * width, width), width)
            far_cols = pl.ds(pl.multiple_of((half * per_half + (j ^ 2) * deep + hi) * width, width), width)
            total = own[part:, cols] + near[part:, cols].astype(F32) + far_ref[:, far_cols].astype(F32)
            out_ref[r ^ (half * per_half + i), :part] = total.astype(BF16)
            out_ref[r ^ (half * per_half + i), part:] = w


def split(keep_low, near_low, keep_high, near_high, far, w, n_row, n_rep):
    part, cols = far.shape
    return pl.pallas_call(
        functools.partial(split_body, n_rep=n_rep, deep=n_row // n_rep // 2),
        out_shape=shape((n_row, part + w.shape[0] // 2, cols // n_row), BF16),
        in_specs=[WHOLE] * 6,
        out_specs=WHOLE,
        compiler_params=params(cols * part * 20),
        cost_estimate=pl.CostEstimate(flops=2 * part * cols, bytes_accessed=part * cols * 10, transcendentals=0),
        name="split",
    )(keep_low, near_low, keep_high, near_high, far, w)


def collect_body(*refs, n_row, n_rep, per_list, quarter, blk):
    lists = refs[:n_rep]
    messages = refs[n_rep]
    outs, w_out, acc_ref = refs[n_rep + 1 : -2], refs[-2], refs[-1]
    r, q = lax.axis_index("row"), lax.axis_index("rep")
    acc_ref[...] = jnp.zeros(acc_ref.shape, F32)
    for k in range(n_row):
        j = turned(k % n_rep) ^ q
        for c in range(per_list):
            at = k // n_rep * per_list + c
            b = lists[0][at]
            for other in range(1, n_rep):
                b = jnp.where(j == other, lists[other][at], b)
            cell = (lax.div(b, quarter) ^ q) * quarter + lax.rem(b, quarter)
            cols = pl.ds(pl.multiple_of(cell * blk, blk), blk)
            acc_ref[:, cols] += messages[r ^ k, : acc_ref.shape[0], c * blk : (c + 1) * blk].astype(F32)
    width = outs[0].shape[1]
    part, depth = acc_ref.shape[0], w_out.shape[0] // 2
    for parity in range(2):
        total = messages[parity, part:].astype(F32)
        for other in range(parity + 2, n_row, 2):
            total += messages[other, part:].astype(F32)
        w_out[parity * depth : (parity + 1) * depth] = total.astype(BF16)
    for j, out in enumerate(outs):
        out[:part] = acc_ref[:, j * width : (j + 1) * width].astype(out.dtype)
        if j:
            fold_in(out, part, 0, w_out[...])


def collect(lists, messages, part, per_list, row_blocks, blk):
    n_rep = len(lists)
    n_row, rows, features = messages.shape
    depth = 2 * (rows - part)
    quarter = row_blocks // n_rep
    body = functools.partial(
        collect_body, n_row=n_row, n_rep=n_rep, per_list=per_list, quarter=quarter, blk=blk
    )
    return pl.pallas_call(
        body,
        out_shape=[shape((part, quarter * blk), F32)]
        + [shape((part + depth * features // (quarter * blk), quarter * blk), BF16)] * (n_rep - 1)
        + [shape((depth, features), BF16)],
        in_specs=[SMEM] * n_rep + [WHOLE],
        out_specs=[WHOLE] * (n_rep + 1),
        scratch_shapes=[pltpu.VMEM((part, row_blocks * blk), F32)],
        compiler_params=params(4 << 20),
        cost_estimate=pl.CostEstimate(
            flops=part * row_blocks * blk, bytes_accessed=part * row_blocks * blk * 5, transcendentals=0
        ),
        name="collect",
    )(*lists, messages)


def finish_body(*refs, n_rep):
    grads = refs[:n_rep]
    w_ref, node_ref, weight_ref, acc_ref = refs[n_rep:]
    q = lax.axis_index("rep")
    part = w_ref.shape[0]
    for j in range(n_rep):
        rows = pl.ds(pl.multiple_of((q ^ j) * part, part), part)
        acc_ref[rows, :] = grads[j][:part].astype(F32)
        weight_ref[rows, :] = fold_out(grads[j], part, 0, *w_ref.shape) if j else w_ref[...].astype(F32)
    node_ref[...] = acc_ref[...].T


def finish(grads, w):
    n_rep = len(grads)
    part, rows = grads[0].shape
    features = w.shape[1]
    return pl.pallas_call(
        functools.partial(finish_body, n_rep=n_rep),
        out_shape=[shape((rows, part * n_rep), F32), shape((features, features), F32)],
        in_specs=[WHOLE] * (n_rep + 1),
        out_specs=[WHOLE] * 2,
        scratch_shapes=[pltpu.VMEM((part * n_rep, rows), F32)],
        compiler_params=params(6 << 20),
        cost_estimate=pl.CostEstimate(flops=0, bytes_accessed=rows * part * n_rep * 8, transcendentals=0),
        name="finish",
    )(*grads, w)


def local(
    node_features, weight, out_grad, blocks, block_rows, block_fetch, fetch_lists, block_count
):
    n_row = lax.axis_size("row")
    n_rep = lax.axis_size("rep")
    n_hi = n_row // n_rep
    band_rows, features = node_features.shape
    blk = blocks.shape[1]
    row_blocks = band_rows // blk
    per_list = fetch_lists.shape[2]

    def to_rep(x, j):
        return lax.ppermute(x, "rep", xor_perm(n_rep, j))

    def to_row(x, k):
        return lax.ppermute(x, "row", xor_perm(n_row, k))

    def spread(x, hi):
        perm = [
            (r * n_rep + q, (r ^ (hi * n_rep + turned(q))) * n_rep + q) for r in range(n_row) for q in range(n_rep)
        ]
        return lax.ppermute(x, ("row", "rep"), perm)

    def after(x, *done):
        return lax.optimization_barrier((x, *done))[0]

    wanted = [spread(fetch_lists, hi) for hi in range(n_hi)]
    *outgoing, own_list = pack(wanted, node_features, per_list, blk)
    own = [spread(x, hi) for hi, x in enumerate(outgoing)]
    deep = n_hi // 2
    low, high = [jnp.concatenate(own[half * deep : (half + 1) * deep], axis=0) for half in range(2)]
    low_far, low_near = to_rep(low, 2), to_rep(low, 1)
    table = slot_lists(
        block_rows, block_fetch, after(block_count, low_near), n_row, n_rep, per_list, row_blocks
    )
    high = after(high, low_far, table)
    high_far, high_near = to_rep(high, 2), to_rep(high, 1)
    adj = densify(after(table, high_near), blocks, n_row, per_list, row_blocks)
    low_diag = to_rep(after(low_far, high_near), 1)
    high_diag = to_rep(after(high_far, adj), 1)
    pieces = [low, low_near, low_far, low_diag, high, high_near, high_far, high_diag]

    send3, keep2 = forward(pieces, adj, 0)
    across = (keep2 + to_rep(send3, 1).astype(F32)).astype(BF16)
    arrived = to_rep(across, 2)
    send1, keep0 = forward(pieces, after(adj, across), 1)
    own_list = after(own_list, keep0)
    lists = [own_list] + [to_rep(own_list, j) for j in range(1, n_rep)]
    arrived = after(arrived, keep0, lists)
    factor = float(n_row * band_rows) ** (-0.5)
    output, to_near, grad0, wkeep = middle(keep0, to_rep(send1, 1), arrived, weight, out_grad, n_rep, factor)

    grad2 = to_rep(grad0, 2)
    first, w = back_first(to_rep(to_near, 1), grad0, adj, wkeep)
    part = features // n_rep
    grad2 = after(grad2, first)
    grad3 = to_rep(grad2, 1)
    got = to_rep(after(w, grad2)[part:], 2)
    send_high, keep_high = back_second(grad3, grad2, adj, first, 1, n_rep, deep)
    near_high = to_rep(send_high, 1)
    send_low, keep_low = back_second(grad3, grad2, adj, after(first, send_high), 0, n_rep, deep)
    near_low = to_rep(after(send_low, near_high, got), 1)
    across = across_sum(keep_low, near_low, keep_high, near_high)
    far = to_rep(across, 2)
    w = after(w[:part], across) + got
    w = w + to_row(w, 1)
    messages = split(keep_low, near_low, keep_high, near_high, far, w, n_row, n_rep)
    returned = lax.all_to_all(messages, "row", split_axis=0, concat_axis=0, tiled=True)
    *grads, w = collect(lists, returned, part, per_list, row_blocks, blk)
    node_grad, weight_grad = finish([grads[0]] + [to_rep(grads[j], j) for j in range(1, n_rep)], w)
    return (output, weight_grad, node_grad)


def solution(mesh):
    in_specs = (
        P("row", None),
        P(),
        P(("row", "rep"), None),
        P(("row", "rep"), None, None),
        P(("row", "rep")),
        P(("row", "rep")),
        P(("row", "rep"), None, None),
        P(("row", "rep")),
    )
    out_specs = (P(("row", "rep"), None), P(), P(("row", "rep"), None))
    return jax.shard_map(local, mesh=mesh, in_specs=in_specs, out_specs=out_specs, check_vma=False)
```

```python
import functools

import jax
import jax.numpy as jnp
from jax import lax
from jax.experimental import pallas as pl
from jax.experimental.pallas import tpu as pltpu
from jax.sharding import PartitionSpec as P

BF16 = jnp.bfloat16
F32 = jnp.float32
COL_CHUNK = 16
ROW_TILE = 256
COL_TILE = 512
WHOLE = pl.BlockSpec(memory_space=pltpu.VMEM)
SMEM = pl.BlockSpec(memory_space=pltpu.SMEM)
ANY = pl.BlockSpec(memory_space=pl.ANY)


def params(*parts):
    return pltpu.CompilerParams(vmem_limit_bytes=min(sum(parts) + (6 << 20), 62 << 20))


def shape(dims, dtype):
    return jax.ShapeDtypeStruct(tuple(dims), dtype)


def dot(a, b, dims=((1,), (0,))):
    return lax.dot_general(a, b, (dims, ((), ())), preferred_element_type=F32)


def xor_perm(count, offset):
    return [(i, i ^ offset) for i in range(count)]


def div_rem(x, n):
    if n & (n - 1) == 0:
        return x >> (n.bit_length() - 1), x & (n - 1)
    return lax.div(x, n), lax.rem(x, n)


def lists_body(slots_ref, count_ref, out_ref, *, n_rep, n_hi, per_list, quarter):
    r, q = lax.axis_index("row"), lax.axis_index("rep")
    all_cols = n_rep * n_hi * per_list
    cells = n_rep * quarter * all_cols
    slots = slots_ref.shape[1]
    row_high, row_low = div_rem(slots_ref[0:1, :], quarter)
    source, c = div_rem(slots_ref[1:2, :], per_list)
    hi, low = div_rem(source ^ r, n_rep)
    half, hi = div_rem(hi, n_hi // 2)
    row = (n_rep - 1 - (row_high ^ q)) * quarter + row_low
    col = ((half * n_rep + (low ^ q)) * (n_hi // 2) + hi) * per_list + c
    across = lax.broadcasted_iota(jnp.int32, (1, slots), 1)
    cell = jnp.where(across < count_ref[0], row * all_cols + col, cells)
    down = lax.broadcasted_iota(jnp.int32, (slots, slots), 0)
    side = lax.broadcasted_iota(jnp.int32, (slots, slots), 1)
    cell_down = jnp.sum(jnp.where(down == side, jnp.broadcast_to(cell, (slots, slots)), 0), axis=1, keepdims=True)
    before = jnp.where((cell_down == cell) & (down < side), down, -1)
    out_ref[4:5, :slots] = jnp.max(before, axis=0, keepdims=True)
    width = 256
    for begin in range(0, cells, width):
        here = lax.broadcasted_iota(jnp.int32, (slots, width), 1) + begin
        slot = lax.broadcasted_iota(jnp.int32, (slots, width), 0)
        slot = jnp.where(cell_down == here, slot, -1)
        for depth in range(4):
            last = jnp.max(slot, axis=0, keepdims=True)
            out_ref[depth : depth + 1, begin : begin + width] = last
            slot = jnp.where(slot < last, slot, -1)


def slot_lists(block_rows, block_fetch, block_count, n_row, n_rep, per_list, row_blocks):
    cells = row_blocks * n_row * per_list
    body = functools.partial(
        lists_body, n_rep=n_rep, n_hi=n_row // n_rep, per_list=per_list, quarter=row_blocks // n_rep
    )
    return pl.pallas_call(
        body,
        out_shape=shape((8, cells), jnp.int32),
        in_specs=[WHOLE, SMEM],
        out_specs=WHOLE,
        compiler_params=params(8 << 20),
        cost_estimate=pl.CostEstimate(flops=3 << 30, bytes_accessed=32 * cells, transcendentals=0),
        name="slot_lists",
    )(jnp.stack([block_rows, block_fetch]), block_count)


def densify_body(table_ref, held, out_ref, *, all_cols):
    chunk, row_cell = pl.program_id(0), pl.program_id(1)
    blk = held.shape[1]
    base = row_cell * all_cols + chunk * COL_CHUNK
    zero = jnp.zeros((blk, blk), BF16)

    def block(slot):
        return jnp.where(slot >= 0, held[jnp.maximum(slot, 0)], zero)

    widest = jnp.int32(-1)
    for col in range(COL_CHUNK):
        cell = base + col
        out_ref[:, col * blk : (col + 1) * blk] = block(table_ref[0, cell]) + block(table_ref[1, cell])
        widest = jnp.maximum(widest, table_ref[2, cell])

    @pl.when(widest >= 0)
    def _():
        @pl.loop(0, COL_CHUNK)
        def _(col):
            cell = base + col
            three = table_ref[2, cell]

            @pl.when(three >= 0)
            def _():
                one, two, four = table_ref[0, cell], table_ref[1, cell], table_ref[3, cell]
                total = held[one].astype(F32) + held[two].astype(F32)
                total = total + (held[three].astype(F32) + block(four).astype(F32))
                place = (slice(None), pl.ds(pl.multiple_of(col * blk, blk), blk))
                out_ref[place] = total.astype(BF16)
                five = jnp.where(four >= 0, table_ref[4, jnp.maximum(four, 0)], -1)

                @pl.when(five >= 0)
                def _():
                    def more(carry):
                        slot, total = carry
                        return table_ref[4, slot], total + held[slot].astype(F32)

                    _, rest = lax.while_loop(lambda carry: carry[0] >= 0, more, (five, total))
                    out_ref[place] = rest.astype(BF16)


def densify(table, blocks, n_row, per_list, row_blocks):
    slots, blk, _ = blocks.shape
    all_cols = n_row * per_list
    width = COL_CHUNK * blk
    return pl.pallas_call(
        functools.partial(densify_body, all_cols=all_cols),
        out_shape=shape((row_blocks * blk, all_cols * blk), BF16),
        grid_spec=pltpu.PrefetchScalarGridSpec(
            num_scalar_prefetch=1,
            grid=(all_cols // COL_CHUNK, row_blocks),
            in_specs=[WHOLE],
            out_specs=pl.BlockSpec((blk, width), lambda c, i, *_: (i, c)),
        ),
        compiler_params=params(blocks.size * 2, blk * width * 4),
        cost_estimate=pl.CostEstimate(
            flops=slots * blk * blk,
            bytes_accessed=blocks.size * 2 + 2 * all_cols * row_blocks * blk * blk,
            transcendentals=0,
        ),
        name="densify",
    )(table, blocks)


def pack_body(*refs, n_hi, per_list, blk):
    lists = refs[:n_hi]
    features = refs[n_hi]
    outs = refs[n_hi + 1 : 2 * n_hi + 1]
    own_list, sems = refs[2 * n_hi + 1 :]
    r = lax.axis_index("row")
    copies = []
    for hi in range(n_hi):
        for c in range(per_list):
            b = lists[hi][0, r, c]
            own_list[hi * per_list + c] = b
            copy = pltpu.make_async_copy(
                features.at[pl.ds(pl.multiple_of(b * blk, blk), blk)],
                outs[hi].at[pl.ds(c * blk, blk)],
                sems.at[hi * per_list + c],
            )
            copy.start()
            copies.append(copy)
    for copy in copies:
        copy.wait()


def pack(lists, features, per_list, blk):
    n_hi = len(lists)
    return pl.pallas_call(
        functools.partial(pack_body, n_hi=n_hi, per_list=per_list, blk=blk),
        out_shape=[shape((per_list * blk, features.shape[1]), BF16)] * n_hi + [shape((128,), jnp.int32)],
        in_specs=[SMEM] * n_hi + [pl.BlockSpec(memory_space=pltpu.HBM)],
        out_specs=[ANY] * n_hi + [SMEM],
        scratch_shapes=[pltpu.SemaphoreType.DMA((n_hi * per_list,))],
        compiler_params=pltpu.CompilerParams(vmem_limit_bytes=53 << 20),
        name="pack",
    )(*lists, features)


def forward_body(*refs, n_rep):
    pieces = refs[:n_rep]
    adj_ref, send_ref, keep_ref = refs[n_rep:]
    i = pl.program_id(0)
    depth = pieces[0].shape[0] // 2
    total = 0.0
    for half in range(2):
        for j in range(n_rep):
            at = (half * n_rep + j) * depth
            total += dot(adj_ref[:, at : at + depth], pieces[j][half * depth : (half + 1) * depth])

    half = pl.num_programs(0) // 2

    @pl.when(i < half)
    def _():
        send_ref[...] = total.astype(BF16)

    @pl.when(i >= half)
    def _():
        keep_ref[...] = total


def forward(pieces, adj, half_index):
    rows, cols = adj.shape[0] // 2, adj.shape[1]
    features = pieces[0].shape[1]
    tiles = rows // ROW_TILE
    half = tiles // 2
    return pl.pallas_call(
        functools.partial(forward_body, n_rep=len(pieces)),
        grid=(tiles,),
        out_shape=[shape((rows // 2, features), BF16), shape((rows // 2, features), F32)],
        in_specs=[pl.BlockSpec(x.shape, lambda i: (0, 0)) for x in pieces]
        + [pl.BlockSpec((ROW_TILE, cols), lambda i: (i + half_index * tiles, 0))],
        out_specs=[
            pl.BlockSpec((ROW_TILE, features), lambda i: (jnp.minimum(i, half - 1), 0)),
            pl.BlockSpec((ROW_TILE, features), lambda i: (jnp.maximum(i - half, 0), 0)),
        ],
        compiler_params=params(ROW_TILE * cols * 4, cols * features * 4),
        cost_estimate=pl.CostEstimate(
            flops=2 * rows * cols * features, bytes_accessed=adj.size + cols * features * 2, transcendentals=0
        ),
        name="forward",
    )(*pieces, adj)


def middle_body(
    keep_ref, near_ref, far_ref, weight_ref, cot_ref, out_ref, near_out, far_out, wkeep_ref, acc_ref, *, factor
):
    q = lax.axis_index("rep")
    hidden = (keep_ref[...] + near_ref[...].astype(F32) + far_ref[...].astype(F32)).astype(BF16)
    weight = weight_ref[...]
    pre_act = dot(hidden, weight)
    sig = jax.nn.sigmoid(pre_act)
    pre_grad = (cot_ref[...].astype(F32) * (sig * (1.0 + pre_act * (1.0 - sig)))).astype(BF16)
    features, rows = weight.shape[0], hidden.shape[0]
    input_grad = dot(weight, pre_grad, ((1,), (1,))).astype(BF16)
    near_out[:features] = input_grad
    far_out[...] = input_grad
    out_ref[...] = (pre_act * sig).astype(BF16)
    acc_ref[...] = dot(hidden, pre_grad, ((0,), (0,))) * factor
    part = wkeep_ref.shape[0] // 2
    for j in range(4):
        piece = acc_ref[pl.ds(pl.multiple_of((q ^ j) * part, part), part), :]
        if j & 1:
            fold_in(near_out, features, j // 2, piece)
        else:
            wkeep_ref[j // 2 * part : (j // 2 + 1) * part] = piece


def fold_in(ref, base, at, piece):
    part, features = piece.shape
    folds = ref.shape[1] // features
    depth = part // folds
    for i in range(folds):
        ref[base + at * depth : base + (at + 1) * depth, i * features : (i + 1) * features] = piece[
            i * depth : (i + 1) * depth
        ].astype(ref.dtype)


def fold_out(ref, base, at, part, features):
    folds = ref.shape[1] // features
    depth = part // folds
    rows = ref[base + at * depth : base + (at + 1) * depth, :].astype(F32)
    return jnp.concatenate([rows[:, i * features : (i + 1) * features] for i in range(folds)], axis=0)


def middle(keep, near, far, weight, cot, n_rep, factor):
    rows, features = keep.shape
    part = features // n_rep
    extra = part * features // rows
    return pl.pallas_call(
        functools.partial(middle_body, factor=factor),
        out_shape=[
            shape((rows, features), BF16),
            shape((features + 2 * extra, rows), BF16),
            shape((features, rows), BF16),
            shape((2 * part, features), F32),
        ],
        in_specs=[WHOLE] * 5,
        out_specs=[WHOLE] * 4,
        scratch_shapes=[pltpu.VMEM((features, features), F32)],
        compiler_params=params(12 << 20),
        cost_estimate=pl.CostEstimate(
            flops=6 * rows * features * features, bytes_accessed=rows * features * 14, transcendentals=rows * features
        ),
        name="middle",
    )(keep, near, far, weight, cot)


def back_first_body(odd_ref, even_ref, adj_ref, wkeep_ref, out_ref, w_out):
    features, rows = out_ref.shape[0], odd_ref.shape[1]
    out_ref[...] = dot(odd_ref[:features], adj_ref[:rows]) + dot(even_ref[...], adj_ref[rows:])

    @pl.when(pl.program_id(0) == 0)
    def _():
        part = w_out.shape[0] // 2
        for at in range(2):
            rows_here = slice(at * part, (at + 1) * part)
            w_out[rows_here] = wkeep_ref[rows_here] + fold_out(odd_ref, features, at, part, features)


def back_first(odd, even, adj, wkeep):
    rows, cols = adj.shape[0] // 2, adj.shape[1]
    features = wkeep.shape[1]
    whole = lambda x: pl.BlockSpec(x.shape, lambda i: (0, 0))
    return pl.pallas_call(
        back_first_body,
        grid=(cols // COL_TILE,),
        out_shape=[shape((features, cols), F32), shape(wkeep.shape, F32)],
        in_specs=[whole(odd), whole(even), pl.BlockSpec((rows, COL_TILE), lambda i: (1, i)), whole(wkeep)],
        out_specs=[pl.BlockSpec((features, COL_TILE), lambda i: (0, i)), whole(wkeep)],
        compiler_params=params(4 << 20),
        cost_estimate=pl.CostEstimate(
            flops=2 * rows * cols * features, bytes_accessed=adj.size + cols * features * 4, transcendentals=0
        ),
        name="back_first",
    )(odd, even, adj, wkeep)


def back_second_body(odd_ref, even_ref, adj_ref, first_ref, send_ref, keep_ref, acc_ref):
    q = lax.axis_index("rep")
    rows = odd_ref.shape[1]
    acc_ref[...] = first_ref[...] + dot(odd_ref[...], adj_ref[:rows]) + dot(even_ref[...], adj_ref[rows:])
    part = send_ref.shape[0] // 2
    for j in range(4):
        out = send_ref if j & 1 else keep_ref
        at = (3 - j) // 2 * part
        piece = acc_ref[pl.ds(pl.multiple_of((q ^ j) * part, part), part), :]
        out[at : at + part] = piece.astype(out.dtype)


def back_second(odd, even, adj, first, half, n_rep, per_piece):
    rows, cols = adj.shape[0] // 2, adj.shape[1] // 2
    features = first.shape[0]
    width = cols // n_rep // per_piece
    tiles = cols // width
    whole = lambda x: pl.BlockSpec(x.shape, lambda i: (0, 0))
    return pl.pallas_call(
        back_second_body,
        grid=(tiles,),
        out_shape=[shape((features // 2, cols), BF16), shape((features // 2, cols), F32)],
        in_specs=[
            whole(odd),
            whole(even),
            pl.BlockSpec((rows, width), lambda i: (0, i + half * tiles)),
            pl.BlockSpec((features, width), lambda i: (0, i + half * tiles)),
        ],
        out_specs=[
            pl.BlockSpec(
                (features // 2, width), lambda i: (0, (lax.div(i, per_piece) ^ 1) * per_piece + lax.rem(i, per_piece))
            ),
            pl.BlockSpec((features // 2, width), lambda i: (0, i)),
        ],
        scratch_shapes=[pltpu.VMEM((features, width), F32)],
        compiler_params=params(4 << 20),
        cost_estimate=pl.CostEstimate(
            flops=2 * rows * cols * features, bytes_accessed=rows * cols * 2 + cols * features * 7, transcendentals=0
        ),
        name=f"back_second_{half}",
    )(odd, even, adj, first)


def across_body(low_ref, low_near, high_ref, high_near, out_ref):
    part, cols = out_ref.shape[0], low_ref.shape[1]
    for half, (keep, near) in enumerate(((low_ref, low_near), (high_ref, high_near))):
        out_ref[:, half * cols : (half + 1) * cols] = (keep[:part] + near[:part].astype(F32)).astype(BF16)


def across_sum(keep_low, near_low, keep_high, near_high):
    rows, cols = keep_low.shape
    return pl.pallas_call(
        across_body,
        out_shape=shape((rows // 2, 2 * cols), BF16),
        in_specs=[WHOLE] * 4,
        out_specs=WHOLE,
        compiler_params=params(rows * cols * 14),
        cost_estimate=pl.CostEstimate(flops=rows * cols, bytes_accessed=rows * cols * 8, transcendentals=0),
        name="across_sum",
    )(keep_low, near_low, keep_high, near_high)


def split_body(low_ref, low_near, high_ref, high_near, far_ref, w_ref, out_ref, *, n_rep, deep):
    r, q = lax.axis_index("row"), lax.axis_index("rep")
    part, width = far_ref.shape[0], out_ref.shape[2]
    depth = w_ref.shape[0] // 2
    w = w_ref[pl.ds(pl.multiple_of((r & 1) * depth, depth), depth), :].astype(BF16)
    per_half = n_rep * deep
    for half, (own, near) in enumerate(((low_ref, low_near), (high_ref, high_near))):
        for i in range(per_half):
            low, hi = i % n_rep, i // n_rep
            j = low ^ q
            cols = pl.ds(pl.multiple_of((j * deep + hi) * width, width), width)
            far_cols = pl.ds(pl.multiple_of((half * per_half + (j ^ 2) * deep + hi) * width, width), width)
            total = own[part:, cols] + near[part:, cols].astype(F32) + far_ref[:, far_cols].astype(F32)
            out_ref[r ^ (half * per_half + i), :part] = total.astype(BF16)
            out_ref[r ^ (half * per_half + i), part:] = w


def split(keep_low, near_low, keep_high, near_high, far, w, n_row, n_rep):
    part, cols = far.shape
    return pl.pallas_call(
        functools.partial(split_body, n_rep=n_rep, deep=n_row // n_rep // 2),
        out_shape=shape((n_row, part + w.shape[0] // 2, cols // n_row), BF16),
        in_specs=[WHOLE] * 6,
        out_specs=WHOLE,
        compiler_params=params(cols * part * 20),
        cost_estimate=pl.CostEstimate(flops=2 * part * cols, bytes_accessed=part * cols * 10, transcendentals=0),
        name="split",
    )(keep_low, near_low, keep_high, near_high, far, w)


def collect_body(*refs, n_row, n_rep, per_list, quarter, blk):
    lists = refs[:n_rep]
    messages = refs[n_rep]
    outs, w_out, acc_ref = refs[n_rep + 1 : -2], refs[-2], refs[-1]
    r, q = lax.axis_index("row"), lax.axis_index("rep")
    acc_ref[...] = jnp.zeros(acc_ref.shape, F32)
    for k in range(n_row):
        j = (k % n_rep) ^ q
        for c in range(per_list):
            at = k // n_rep * per_list + c
            b = lists[0][at]
            for other in range(1, n_rep):
                b = jnp.where(j == other, lists[other][at], b)
            cell = (lax.div(b, quarter) ^ q) * quarter + lax.rem(b, quarter)
            cols = pl.ds(pl.multiple_of(cell * blk, blk), blk)
            acc_ref[:, cols] += messages[r ^ k, : acc_ref.shape[0], c * blk : (c + 1) * blk].astype(F32)
    width = outs[0].shape[1]
    part, depth = acc_ref.shape[0], w_out.shape[0] // 2
    for parity in range(2):
        total = messages[parity, part:].astype(F32)
        for other in range(parity + 2, n_row, 2):
            total += messages[other, part:].astype(F32)
        w_out[parity * depth : (parity + 1) * depth] = total.astype(BF16)
    for j, out in enumerate(outs):
        out[:part] = acc_ref[:, j * width : (j + 1) * width].astype(out.dtype)
        if j:
            fold_in(out, part, 0, w_out[...])


def collect(lists, messages, part, per_list, row_blocks, blk):
    n_rep = len(lists)
    n_row, rows, features = messages.shape
    depth = 2 * (rows - part)
    quarter = row_blocks // n_rep
    body = functools.partial(
        collect_body, n_row=n_row, n_rep=n_rep, per_list=per_list, quarter=quarter, blk=blk
    )
    return pl.pallas_call(
        body,
        out_shape=[shape((part, quarter * blk), F32)]
        + [shape((part + depth * features // (quarter * blk), quarter * blk), BF16)] * (n_rep - 1)
        + [shape((depth, features), BF16)],
        in_specs=[SMEM] * n_rep + [WHOLE],
        out_specs=[WHOLE] * (n_rep + 1),
        scratch_shapes=[pltpu.VMEM((part, row_blocks * blk), F32)],
        compiler_params=params(4 << 20),
        cost_estimate=pl.CostEstimate(
            flops=part * row_blocks * blk, bytes_accessed=part * row_blocks * blk * 5, transcendentals=0
        ),
        name="collect",
    )(*lists, messages)


def finish_body(*refs, n_rep):
    grads = refs[:n_rep]
    w_ref, node_ref, weight_ref, acc_ref = refs[n_rep:]
    q = lax.axis_index("rep")
    part = w_ref.shape[0]
    for j in range(n_rep):
        rows = pl.ds(pl.multiple_of((q ^ j) * part, part), part)
        acc_ref[rows, :] = grads[j][:part].astype(F32)
        weight_ref[rows, :] = fold_out(grads[j], part, 0, *w_ref.shape) if j else w_ref[...].astype(F32)
    node_ref[...] = acc_ref[...].T


def finish(grads, w):
    n_rep = len(grads)
    part, rows = grads[0].shape
    features = w.shape[1]
    return pl.pallas_call(
        functools.partial(finish_body, n_rep=n_rep),
        out_shape=[shape((rows, part * n_rep), F32), shape((features, features), F32)],
        in_specs=[WHOLE] * (n_rep + 1),
        out_specs=[WHOLE] * 2,
        scratch_shapes=[pltpu.VMEM((part * n_rep, rows), F32)],
        compiler_params=params(6 << 20),
        cost_estimate=pl.CostEstimate(flops=0, bytes_accessed=rows * part * n_rep * 8, transcendentals=0),
        name="finish",
    )(*grads, w)


def local(
    node_features, weight, out_grad, blocks, block_rows, block_fetch, fetch_lists, block_count
):
    n_row = lax.axis_size("row")
    n_rep = lax.axis_size("rep")
    n_hi = n_row // n_rep
    band_rows, features = node_features.shape
    blk = blocks.shape[1]
    row_blocks = band_rows // blk
    per_list = fetch_lists.shape[2]

    def to_rep(x, j):
        return lax.ppermute(x, "rep", xor_perm(n_rep, j))

    def to_row(x, k):
        return lax.ppermute(x, "row", xor_perm(n_row, k))

    def spread(x, hi):
        perm = [
            (r * n_rep + q, (r ^ (hi * n_rep + q)) * n_rep + q) for r in range(n_row) for q in range(n_rep)
        ]
        return lax.ppermute(x, ("row", "rep"), perm)

    def after(x, *done):
        return lax.optimization_barrier((x, *done))[0]

    wanted = [spread(fetch_lists, hi) for hi in range(n_hi)]
    *outgoing, own_list = pack(wanted, node_features, per_list, blk)
    own = [spread(x, hi) for hi, x in enumerate(outgoing)]
    deep = n_hi // 2
    table = slot_lists(block_rows, block_fetch, block_count, n_row, n_rep, per_list, row_blocks)
    lists = [own_list] + [to_rep(own_list, j) for j in range(1, n_rep)]
    own = after(jnp.concatenate(own, axis=0), table, lists)
    far = to_rep(own, 2)
    near = to_rep(own, 1)
    adj = densify(after(table, near), blocks, n_row, per_list, row_blocks)
    pieces = [own, near, far, to_rep(after(far, adj), 1)]

    send3, keep2 = forward(pieces, adj, 0)
    across = (keep2 + to_rep(send3, 1).astype(F32)).astype(BF16)
    arrived = to_rep(across, 2)
    send1, keep0 = forward(pieces, after(adj, across), 1)
    arrived = after(arrived, keep0)
    factor = float(n_row * band_rows) ** (-0.5)
    output, to_near, grad0, wkeep = middle(keep0, to_rep(send1, 1), arrived, weight, out_grad, n_rep, factor)

    grad2 = to_rep(grad0, 2)
    first, w = back_first(to_rep(to_near, 1), grad0, adj, wkeep)
    part = features // n_rep
    grad2 = after(grad2, first)
    grad3 = to_rep(grad2, 1)
    got = to_rep(after(w, grad2)[part:], 2)
    send_high, keep_high = back_second(grad3, grad2, adj, first, 1, n_rep, deep)
    send_high = after(send_high, got)
    near_high = to_rep(send_high, 1)
    send_low, keep_low = back_second(grad3, grad2, adj, after(first, send_high), 0, n_rep, deep)
    near_low = to_rep(after(send_low, near_high), 1)
    across = across_sum(keep_low, near_low, keep_high, near_high)
    far = to_rep(across, 2)
    w = after(w[:part], across) + got
    w = w + to_row(w, 1)
    messages = split(keep_low, near_low, keep_high, near_high, far, w, n_row, n_rep)
    returned = lax.all_to_all(messages, "row", split_axis=0, concat_axis=0, tiled=True)
    *grads, w = collect(lists, returned, part, per_list, row_blocks, blk)
    node_grad, weight_grad = finish([grads[0]] + [to_rep(grads[j], j) for j in range(1, n_rep)], w)
    return (output, weight_grad, node_grad)


def solution(mesh):
    in_specs = (
        P("row", None),
        P(),
        P(("row", "rep"), None),
        P(("row", "rep"), None, None),
        P(("row", "rep")),
        P(("row", "rep")),
        P(("row", "rep"), None, None),
        P(("row", "rep")),
    )
    out_specs = (P(("row", "rep"), None), P(), P(("row", "rep"), None))
    return jax.shard_map(local, mesh=mesh, in_specs=in_specs, out_specs=out_specs, check_vma=False)
```

```python
import functools

import jax
import jax.numpy as jnp
from jax import lax
from jax.experimental import pallas as pl
from jax.experimental.pallas import tpu as pltpu
from jax.sharding import PartitionSpec as P

BF16 = jnp.bfloat16
F32 = jnp.float32
COL_CHUNK = 16
W_SHARE = 4
ROW_TILE = 256
COL_TILE = 512
WHOLE = pl.BlockSpec(memory_space=pltpu.VMEM)
SMEM = pl.BlockSpec(memory_space=pltpu.SMEM)
ANY = pl.BlockSpec(memory_space=pl.ANY)


def params(*parts):
    return pltpu.CompilerParams(vmem_limit_bytes=min(sum(parts) + (6 << 20), 62 << 20))


def shape(dims, dtype):
    return jax.ShapeDtypeStruct(tuple(dims), dtype)


def dot(a, b, dims=((1,), (0,))):
    return lax.dot_general(a, b, (dims, ((), ())), preferred_element_type=F32)


def xor_perm(count, offset):
    return [(i, i ^ offset) for i in range(count)]


def div_rem(x, n):
    if n & (n - 1) == 0:
        return x >> (n.bit_length() - 1), x & (n - 1)
    return lax.div(x, n), lax.rem(x, n)


def lists_body(slots_ref, count_ref, out_ref, *, n_rep, n_hi, per_list, quarter):
    r, q = lax.axis_index("row"), lax.axis_index("rep")
    all_cols = n_rep * n_hi * per_list
    cells = n_rep * quarter * all_cols
    slots = slots_ref.shape[1]
    row_high, row_low = div_rem(slots_ref[0:1, :], quarter)
    source, c = div_rem(slots_ref[1:2, :], per_list)
    hi, low = div_rem(source ^ r, n_rep)
    half, hi = div_rem(hi, n_hi // 2)
    row = (n_rep - 1 - (row_high ^ q)) * quarter + row_low
    col = ((half * n_rep + (low ^ q)) * (n_hi // 2) + hi) * per_list + c
    across = lax.broadcasted_iota(jnp.int32, (1, slots), 1)
    cell = jnp.where(across < count_ref[0], row * all_cols + col, cells)
    down = lax.broadcasted_iota(jnp.int32, (slots, slots), 0)
    side = lax.broadcasted_iota(jnp.int32, (slots, slots), 1)
    cell_down = jnp.sum(jnp.where(down == side, jnp.broadcast_to(cell, (slots, slots)), 0), axis=1, keepdims=True)
    before = jnp.where((cell_down == cell) & (down < side), down, -1)
    out_ref[4:5, :slots] = jnp.max(before, axis=0, keepdims=True)
    width = 256
    for begin in range(0, cells, width):
        here = lax.broadcasted_iota(jnp.int32, (slots, width), 1) + begin
        slot = lax.broadcasted_iota(jnp.int32, (slots, width), 0)
        slot = jnp.where(cell_down == here, slot, -1)
        for depth in range(4):
            last = jnp.max(slot, axis=0, keepdims=True)
            out_ref[depth : depth + 1, begin : begin + width] = last
            slot = jnp.where(slot < last, slot, -1)


def slot_lists(block_rows, block_fetch, block_count, n_row, n_rep, per_list, row_blocks):
    cells = row_blocks * n_row * per_list
    body = functools.partial(
        lists_body, n_rep=n_rep, n_hi=n_row // n_rep, per_list=per_list, quarter=row_blocks // n_rep
    )
    return pl.pallas_call(
        body,
        out_shape=shape((8, cells), jnp.int32),
        in_specs=[WHOLE, SMEM],
        out_specs=WHOLE,
        compiler_params=params(8 << 20),
        cost_estimate=pl.CostEstimate(flops=3 << 30, bytes_accessed=32 * cells, transcendentals=0),
        name="slot_lists",
    )(jnp.stack([block_rows, block_fetch]), block_count)


def densify_body(table_ref, held, out_ref, *, all_cols):
    chunk, row_cell = pl.program_id(0), pl.program_id(1)
    blk = held.shape[1]
    base = row_cell * all_cols + chunk * COL_CHUNK
    zero = jnp.zeros((blk, blk), BF16)

    def block(slot):
        return jnp.where(slot >= 0, held[jnp.maximum(slot, 0)], zero)

    widest = jnp.int32(-1)
    for col in range(COL_CHUNK):
        cell = base + col
        out_ref[:, col * blk : (col + 1) * blk] = block(table_ref[0, cell]) + block(table_ref[1, cell])
        widest = jnp.maximum(widest, table_ref[2, cell])

    @pl.when(widest >= 0)
    def _():
        @pl.loop(0, COL_CHUNK)
        def _(col):
            cell = base + col
            three = table_ref[2, cell]

            @pl.when(three >= 0)
            def _():
                one, two, four = table_ref[0, cell], table_ref[1, cell], table_ref[3, cell]
                total = held[one].astype(F32) + held[two].astype(F32)
                total = total + (held[three].astype(F32) + block(four).astype(F32))
                place = (slice(None), pl.ds(pl.multiple_of(col * blk, blk), blk))
                out_ref[place] = total.astype(BF16)
                five = jnp.where(four >= 0, table_ref[4, jnp.maximum(four, 0)], -1)

                @pl.when(five >= 0)
                def _():
                    def more(carry):
                        slot, total = carry
                        return table_ref[4, slot], total + held[slot].astype(F32)

                    _, rest = lax.while_loop(lambda carry: carry[0] >= 0, more, (five, total))
                    out_ref[place] = rest.astype(BF16)


def densify(table, blocks, n_row, per_list, row_blocks):
    slots, blk, _ = blocks.shape
    all_cols = n_row * per_list
    width = COL_CHUNK * blk
    return pl.pallas_call(
        functools.partial(densify_body, all_cols=all_cols),
        out_shape=shape((row_blocks * blk, all_cols * blk), BF16),
        grid_spec=pltpu.PrefetchScalarGridSpec(
            num_scalar_prefetch=1,
            grid=(all_cols // COL_CHUNK, row_blocks),
            in_specs=[WHOLE],
            out_specs=pl.BlockSpec((blk, width), lambda c, i, *_: (i, c)),
        ),
        compiler_params=params(blocks.size * 2, blk * width * 4),
        cost_estimate=pl.CostEstimate(
            flops=slots * blk * blk,
            bytes_accessed=blocks.size * 2 + 2 * all_cols * row_blocks * blk * blk,
            transcendentals=0,
        ),
        name="densify",
    )(table, blocks)


def pack_body(*refs, n_hi, per_list, blk):
    lists = refs[:n_hi]
    features = refs[n_hi]
    outs = refs[n_hi + 1 : 2 * n_hi + 1]
    own_list, sems = refs[2 * n_hi + 1 :]
    r = lax.axis_index("row")
    copies = []
    for hi in range(n_hi):
        for c in range(per_list):
            b = lists[hi][0, r, c]
            own_list[hi * per_list + c] = b
            copy = pltpu.make_async_copy(
                features.at[pl.ds(pl.multiple_of(b * blk, blk), blk)],
                outs[hi].at[pl.ds(c * blk, blk)],
                sems.at[hi * per_list + c],
            )
            copy.start()
            copies.append(copy)
    for copy in copies:
        copy.wait()


def pack(lists, features, per_list, blk):
    n_hi = len(lists)
    return pl.pallas_call(
        functools.partial(pack_body, n_hi=n_hi, per_list=per_list, blk=blk),
        out_shape=[shape((per_list * blk, features.shape[1]), BF16)] * n_hi + [shape((128,), jnp.int32)],
        in_specs=[SMEM] * n_hi + [pl.BlockSpec(memory_space=pltpu.HBM)],
        out_specs=[ANY] * n_hi + [SMEM],
        scratch_shapes=[pltpu.SemaphoreType.DMA((n_hi * per_list,))],
        compiler_params=pltpu.CompilerParams(vmem_limit_bytes=53 << 20),
        name="pack",
    )(*lists, features)


def forward_body(*refs, n_rep):
    pieces = refs[:n_rep]
    adj_ref, send_ref, keep_ref = refs[n_rep:]
    i = pl.program_id(0)
    depth = pieces[0].shape[0] // 2
    total = 0.0
    for half in range(2):
        for j in range(n_rep):
            at = (half * n_rep + j) * depth
            total += dot(adj_ref[:, at : at + depth], pieces[j][half * depth : (half + 1) * depth])

    half = pl.num_programs(0) // 2

    @pl.when(i < half)
    def _():
        send_ref[...] = total.astype(BF16)

    @pl.when(i >= half)
    def _():
        keep_ref[...] = total


def forward(pieces, adj, half_index):
    rows, cols = adj.shape[0] // 2, adj.shape[1]
    features = pieces[0].shape[1]
    tiles = rows // ROW_TILE
    half = tiles // 2
    return pl.pallas_call(
        functools.partial(forward_body, n_rep=len(pieces)),
        grid=(tiles,),
        out_shape=[shape((rows // 2, features), BF16), shape((rows // 2, features), F32)],
        in_specs=[pl.BlockSpec(x.shape, lambda i: (0, 0)) for x in pieces]
        + [pl.BlockSpec((ROW_TILE, cols), lambda i: (i + half_index * tiles, 0))],
        out_specs=[
            pl.BlockSpec((ROW_TILE, features), lambda i: (jnp.minimum(i, half - 1), 0)),
            pl.BlockSpec((ROW_TILE, features), lambda i: (jnp.maximum(i - half, 0), 0)),
        ],
        compiler_params=params(ROW_TILE * cols * 4, cols * features * 4),
        cost_estimate=pl.CostEstimate(
            flops=2 * rows * cols * features, bytes_accessed=adj.size + cols * features * 2, transcendentals=0
        ),
        name="forward",
    )(*pieces, adj)


def middle_body(
    keep_ref, near_ref, far_ref, weight_ref, cot_ref, out_ref, near_out, far_out, wkeep_ref, acc_ref, *, factor
):
    q = lax.axis_index("rep")
    hidden = (keep_ref[...] + near_ref[...].astype(F32) + far_ref[...].astype(F32)).astype(BF16)
    weight = weight_ref[...]
    pre_act = dot(hidden, weight)
    sig = jax.nn.sigmoid(pre_act)
    pre_grad = (cot_ref[...].astype(F32) * (sig * (1.0 + pre_act * (1.0 - sig)))).astype(BF16)
    features, rows = weight.shape[0], hidden.shape[0]
    input_grad = dot(weight, pre_grad, ((1,), (1,))).astype(BF16)
    near_out[:features] = input_grad
    far_out[...] = input_grad
    out_ref[...] = (pre_act * sig).astype(BF16)
    acc_ref[...] = dot(hidden, pre_grad, ((0,), (0,))) * factor
    part = wkeep_ref.shape[0] // 2
    for j in range(4):
        piece = acc_ref[pl.ds(pl.multiple_of((q ^ j) * part, part), part), :]
        if j & 1:
            fold_in(near_out, features, j // 2, piece)
        else:
            wkeep_ref[j // 2 * part : (j // 2 + 1) * part] = piece


def fold_in(ref, base, at, piece):
    part, features = piece.shape
    folds = ref.shape[1] // features
    depth = part // folds
    for i in range(folds):
        ref[base + at * depth : base + (at + 1) * depth, i * features : (i + 1) * features] = piece[
            i * depth : (i + 1) * depth
        ].astype(ref.dtype)


def fold_out(ref, base, at, part, features):
    folds = ref.shape[1] // features
    depth = part // folds
    rows = ref[base + at * depth : base + (at + 1) * depth, :].astype(F32)
    return jnp.concatenate([rows[:, i * features : (i + 1) * features] for i in range(folds)], axis=0)


def middle(keep, near, far, weight, cot, n_rep, factor):
    rows, features = keep.shape
    part = features // n_rep
    extra = part * features // rows
    return pl.pallas_call(
        functools.partial(middle_body, factor=factor),
        out_shape=[
            shape((rows, features), BF16),
            shape((features + 2 * extra, rows), BF16),
            shape((features, rows), BF16),
            shape((2 * part, features), F32),
        ],
        in_specs=[WHOLE] * 5,
        out_specs=[WHOLE] * 4,
        scratch_shapes=[pltpu.VMEM((features, features), F32)],
        compiler_params=params(12 << 20),
        cost_estimate=pl.CostEstimate(
            flops=6 * rows * features * features, bytes_accessed=rows * features * 14, transcendentals=rows * features
        ),
        name="middle",
    )(keep, near, far, weight, cot)


def back_first_body(odd_ref, even_ref, adj_ref, wkeep_ref, out_ref, w_out):
    features, rows = out_ref.shape[0], odd_ref.shape[1]
    out_ref[...] = dot(odd_ref[:features], adj_ref[:rows]) + dot(even_ref[...], adj_ref[rows:])

    @pl.when(pl.program_id(0) == 0)
    def _():
        part = w_out.shape[0] // 2
        for at in range(2):
            rows_here = slice(at * part, (at + 1) * part)
            w_out[rows_here] = wkeep_ref[rows_here] + fold_out(odd_ref, features, at, part, features)


def back_first(odd, even, adj, wkeep):
    rows, cols = adj.shape[0] // 2, adj.shape[1]
    features = wkeep.shape[1]
    whole = lambda x: pl.BlockSpec(x.shape, lambda i: (0, 0))
    return pl.pallas_call(
        back_first_body,
        grid=(cols // COL_TILE,),
        out_shape=[shape((features, cols), F32), shape(wkeep.shape, F32)],
        in_specs=[whole(odd), whole(even), pl.BlockSpec((rows, COL_TILE), lambda i: (1, i)), whole(wkeep)],
        out_specs=[pl.BlockSpec((features, COL_TILE), lambda i: (0, i)), whole(wkeep)],
        compiler_params=params(4 << 20),
        cost_estimate=pl.CostEstimate(
            flops=2 * rows * cols * features, bytes_accessed=adj.size + cols * features * 4, transcendentals=0
        ),
        name="back_first",
    )(odd, even, adj, wkeep)


def back_second_body(odd_ref, even_ref, adj_ref, first_ref, send_ref, keep_ref, acc_ref):
    q = lax.axis_index("rep")
    rows = odd_ref.shape[1]
    acc_ref[...] = first_ref[...] + dot(odd_ref[...], adj_ref[:rows]) + dot(even_ref[...], adj_ref[rows:])
    part = send_ref.shape[0] // 2
    for j in range(4):
        out = send_ref if j & 1 else keep_ref
        at = (3 - j) // 2 * part
        piece = acc_ref[pl.ds(pl.multiple_of((q ^ j) * part, part), part), :]
        out[at : at + part] = piece.astype(out.dtype)


def back_second(odd, even, adj, first, half, n_rep, per_piece):
    rows, cols = adj.shape[0] // 2, adj.shape[1] // 2
    features = first.shape[0]
    width = cols // n_rep // per_piece
    tiles = cols // width
    whole = lambda x: pl.BlockSpec(x.shape, lambda i: (0, 0))
    return pl.pallas_call(
        back_second_body,
        grid=(tiles,),
        out_shape=[shape((features // 2, cols), BF16), shape((features // 2, cols), F32)],
        in_specs=[
            whole(odd),
            whole(even),
            pl.BlockSpec((rows, width), lambda i: (0, i + half * tiles)),
            pl.BlockSpec((features, width), lambda i: (0, i + half * tiles)),
        ],
        out_specs=[
            pl.BlockSpec(
                (features // 2, width), lambda i: (0, (lax.div(i, per_piece) ^ 1) * per_piece + lax.rem(i, per_piece))
            ),
            pl.BlockSpec((features // 2, width), lambda i: (0, i)),
        ],
        scratch_shapes=[pltpu.VMEM((features, width), F32)],
        compiler_params=params(4 << 20),
        cost_estimate=pl.CostEstimate(
            flops=2 * rows * cols * features, bytes_accessed=rows * cols * 2 + cols * features * 7, transcendentals=0
        ),
        name=f"back_second_{half}",
    )(odd, even, adj, first)


def across_body(low_ref, low_near, high_ref, high_near, out_ref):
    part, cols = out_ref.shape[0], low_ref.shape[1]
    for half, (keep, near) in enumerate(((low_ref, low_near), (high_ref, high_near))):
        out_ref[:, half * cols : (half + 1) * cols] = (keep[:part] + near[:part].astype(F32)).astype(BF16)


def across_sum(keep_low, near_low, keep_high, near_high):
    rows, cols = keep_low.shape
    return pl.pallas_call(
        across_body,
        out_shape=shape((rows // 2, 2 * cols), BF16),
        in_specs=[WHOLE] * 4,
        out_specs=WHOLE,
        compiler_params=params(rows * cols * 14),
        cost_estimate=pl.CostEstimate(flops=rows * cols, bytes_accessed=rows * cols * 8, transcendentals=0),
        name="across_sum",
    )(keep_low, near_low, keep_high, near_high)


def split_body(low_ref, low_near, high_ref, high_near, far_ref, w_ref, out_ref, *, n_rep, deep):
    r, q = lax.axis_index("row"), lax.axis_index("rep")
    part, width = far_ref.shape[0], out_ref.shape[2]
    depth = w_ref.shape[0] // W_SHARE
    w = w_ref[pl.ds(pl.multiple_of((r & (W_SHARE - 1)) * depth, depth), depth), :].astype(BF16)
    per_half = n_rep * deep
    for half, (own, near) in enumerate(((low_ref, low_near), (high_ref, high_near))):
        for i in range(per_half):
            low, hi = i % n_rep, i // n_rep
            j = low ^ q
            cols = pl.ds(pl.multiple_of((j * deep + hi) * width, width), width)
            far_cols = pl.ds(pl.multiple_of((half * per_half + (j ^ 2) * deep + hi) * width, width), width)
            total = own[part:, cols] + near[part:, cols].astype(F32) + far_ref[:, far_cols].astype(F32)
            out_ref[r ^ (half * per_half + i), :part] = total.astype(BF16)
            out_ref[r ^ (half * per_half + i), part:] = w


def split(keep_low, near_low, keep_high, near_high, far, w, n_row, n_rep):
    part, cols = far.shape
    return pl.pallas_call(
        functools.partial(split_body, n_rep=n_rep, deep=n_row // n_rep // 2),
        out_shape=shape((n_row, part + w.shape[0] // W_SHARE, cols // n_row), BF16),
        in_specs=[WHOLE] * 6,
        out_specs=WHOLE,
        compiler_params=params(cols * part * 20),
        cost_estimate=pl.CostEstimate(flops=2 * part * cols, bytes_accessed=part * cols * 10, transcendentals=0),
        name="split",
    )(keep_low, near_low, keep_high, near_high, far, w)


def collect_body(*refs, n_row, n_rep, per_list, quarter, blk):
    lists = refs[:n_rep]
    messages = refs[n_rep]
    outs, w_out, acc_ref = refs[n_rep + 1 : -2], refs[-2], refs[-1]
    r, q = lax.axis_index("row"), lax.axis_index("rep")
    acc_ref[...] = jnp.zeros(acc_ref.shape, F32)
    for k in range(n_row):
        j = (k % n_rep) ^ q
        for c in range(per_list):
            at = k // n_rep * per_list + c
            b = lists[0][at]
            for other in range(1, n_rep):
                b = jnp.where(j == other, lists[other][at], b)
            cell = (lax.div(b, quarter) ^ q) * quarter + lax.rem(b, quarter)
            cols = pl.ds(pl.multiple_of(cell * blk, blk), blk)
            acc_ref[:, cols] += messages[r ^ k, : acc_ref.shape[0], c * blk : (c + 1) * blk].astype(F32)
    width = outs[0].shape[1]
    part, depth = acc_ref.shape[0], w_out.shape[0] // W_SHARE
    for parity in range(W_SHARE):
        total = messages[parity, part:].astype(F32)
        for other in range(parity + W_SHARE, n_row, W_SHARE):
            total += messages[other, part:].astype(F32)
        w_out[parity * depth : (parity + 1) * depth] = total.astype(BF16)
    for j, out in enumerate(outs):
        out[:part] = acc_ref[:, j * width : (j + 1) * width].astype(out.dtype)
        if j:
            fold_in(out, part, 0, w_out[...])


def collect(lists, messages, part, per_list, row_blocks, blk):
    n_rep = len(lists)
    n_row, rows, features = messages.shape
    depth = W_SHARE * (rows - part)
    quarter = row_blocks // n_rep
    body = functools.partial(
        collect_body, n_row=n_row, n_rep=n_rep, per_list=per_list, quarter=quarter, blk=blk
    )
    return pl.pallas_call(
        body,
        out_shape=[shape((part, quarter * blk), F32)]
        + [shape((part + depth * features // (quarter * blk), quarter * blk), BF16)] * (n_rep - 1)
        + [shape((depth, features), BF16)],
        in_specs=[SMEM] * n_rep + [WHOLE],
        out_specs=[WHOLE] * (n_rep + 1),
        scratch_shapes=[pltpu.VMEM((part, row_blocks * blk), F32)],
        compiler_params=params(4 << 20),
        cost_estimate=pl.CostEstimate(
            flops=part * row_blocks * blk, bytes_accessed=part * row_blocks * blk * 5, transcendentals=0
        ),
        name="collect",
    )(*lists, messages)


def finish_body(*refs, n_rep):
    grads = refs[:n_rep]
    w_ref, node_ref, weight_ref, acc_ref = refs[n_rep:]
    q = lax.axis_index("rep")
    part = w_ref.shape[0]
    for j in range(n_rep):
        rows = pl.ds(pl.multiple_of((q ^ j) * part, part), part)
        acc_ref[rows, :] = grads[j][:part].astype(F32)
        weight_ref[rows, :] = fold_out(grads[j], part, 0, *w_ref.shape) if j else w_ref[...].astype(F32)
    node_ref[...] = acc_ref[...].T


def finish(grads, w):
    n_rep = len(grads)
    part, rows = grads[0].shape
    features = w.shape[1]
    return pl.pallas_call(
        functools.partial(finish_body, n_rep=n_rep),
        out_shape=[shape((rows, part * n_rep), F32), shape((features, features), F32)],
        in_specs=[WHOLE] * (n_rep + 1),
        out_specs=[WHOLE] * 2,
        scratch_shapes=[pltpu.VMEM((part * n_rep, rows), F32)],
        compiler_params=params(6 << 20),
        cost_estimate=pl.CostEstimate(flops=0, bytes_accessed=rows * part * n_rep * 8, transcendentals=0),
        name="finish",
    )(*grads, w)


def local(
    node_features, weight, out_grad, blocks, block_rows, block_fetch, fetch_lists, block_count
):
    n_row = lax.axis_size("row")
    n_rep = lax.axis_size("rep")
    n_hi = n_row // n_rep
    band_rows, features = node_features.shape
    blk = blocks.shape[1]
    row_blocks = band_rows // blk
    per_list = fetch_lists.shape[2]

    def to_rep(x, j):
        return lax.ppermute(x, "rep", xor_perm(n_rep, j))

    def to_row(x, k):
        return lax.ppermute(x, "row", xor_perm(n_row, k))

    def spread(x, hi):
        perm = [
            (r * n_rep + q, (r ^ (hi * n_rep + q)) * n_rep + q) for r in range(n_row) for q in range(n_rep)
        ]
        return lax.ppermute(x, ("row", "rep"), perm)

    def after(x, *done):
        return lax.optimization_barrier((x, *done))[0]

    wanted = [spread(fetch_lists, hi) for hi in range(n_hi)]
    *outgoing, own_list = pack(wanted, node_features, per_list, blk)
    own = [spread(x, hi) for hi, x in enumerate(outgoing)]
    deep = n_hi // 2
    table = slot_lists(block_rows, block_fetch, block_count, n_row, n_rep, per_list, row_blocks)
    lists = [own_list] + [to_rep(own_list, j) for j in range(1, n_rep)]
    own = after(jnp.concatenate(own, axis=0), table, lists)
    far = to_rep(own, 2)
    near = to_rep(own, 1)
    adj = densify(after(table, near), blocks, n_row, per_list, row_blocks)
    pieces = [own, near, far, to_rep(after(far, adj), 1)]

    send3, keep2 = forward(pieces, adj, 0)
    across = (keep2 + to_rep(send3, 1).astype(F32)).astype(BF16)
    arrived = to_rep(across, 2)
    send1, keep0 = forward(pieces, after(adj, across), 1)
    arrived = after(arrived, keep0)
    factor = float(n_row * band_rows) ** (-0.5)
    output, to_near, grad0, wkeep = middle(keep0, to_rep(send1, 1), arrived, weight, out_grad, n_rep, factor)

    grad2 = to_rep(grad0, 2)
    first, w = back_first(to_rep(to_near, 1), grad0, adj, wkeep)
    part = features // n_rep
    grad2 = after(grad2, first)
    grad3 = to_rep(grad2, 1)
    got = to_rep(after(w, grad2)[part:], 2)
    send_high, keep_high = back_second(grad3, grad2, adj, first, 1, n_rep, deep)
    send_high = after(send_high, got)
    near_high = to_rep(send_high, 1)
    send_low, keep_low = back_second(grad3, grad2, adj, after(first, send_high), 0, n_rep, deep)
    near_low = to_rep(after(send_low, near_high), 1)
    across = across_sum(keep_low, near_low, keep_high, near_high)
    far = to_rep(across, 2)
    w = after(w[:part], across) + got
    for step in (1, 2):
        w = w + to_row(w, step)
    messages = split(keep_low, near_low, keep_high, near_high, far, w, n_row, n_rep)
    returned = lax.all_to_all(messages, "row", split_axis=0, concat_axis=0, tiled=True)
    *grads, w = collect(lists, returned, part, per_list, row_blocks, blk)
    node_grad, weight_grad = finish([grads[0]] + [to_rep(grads[j], j) for j in range(1, n_rep)], w)
    return (output, weight_grad, node_grad)


def solution(mesh):
    in_specs = (
        P("row", None),
        P(),
        P(("row", "rep"), None),
        P(("row", "rep"), None, None),
        P(("row", "rep")),
        P(("row", "rep")),
        P(("row", "rep"), None, None),
        P(("row", "rep")),
    )
    out_specs = (P(("row", "rep"), None), P(), P(("row", "rep"), None))
    return jax.shard_map(local, mesh=mesh, in_specs=in_specs, out_specs=out_specs, check_vma=False)
```

```python
import functools

import jax
import jax.numpy as jnp
from jax import lax
from jax.experimental import pallas as pl
from jax.experimental.pallas import tpu as pltpu
from jax.sharding import PartitionSpec as P

BF16 = jnp.bfloat16
F32 = jnp.float32
COL_CHUNK = 16
W_SHARE = 4
ROW_TILE = 256
COL_TILE = 512
WHOLE = pl.BlockSpec(memory_space=pltpu.VMEM)
SMEM = pl.BlockSpec(memory_space=pltpu.SMEM)
ANY = pl.BlockSpec(memory_space=pl.ANY)


def params(*parts):
    return pltpu.CompilerParams(vmem_limit_bytes=min(sum(parts) + (6 << 20), 62 << 20))


def shape(dims, dtype):
    return jax.ShapeDtypeStruct(tuple(dims), dtype)


def dot(a, b, dims=((1,), (0,))):
    return lax.dot_general(a, b, (dims, ((), ())), preferred_element_type=F32)


def xor_perm(count, offset):
    return [(i, i ^ offset) for i in range(count)]


def div_rem(x, n):
    if n & (n - 1) == 0:
        return x >> (n.bit_length() - 1), x & (n - 1)
    return lax.div(x, n), lax.rem(x, n)


def lists_body(slots_ref, count_ref, out_ref, *, n_rep, n_hi, per_list, quarter):
    r, q = lax.axis_index("row"), lax.axis_index("rep")
    all_cols = n_rep * n_hi * per_list
    cells = n_rep * quarter * all_cols
    slots = slots_ref.shape[1]
    row_high, row_low = div_rem(slots_ref[0:1, :], quarter)
    source, c = div_rem(slots_ref[1:2, :], per_list)
    hi, low = div_rem(source ^ r, n_rep)
    half, hi = div_rem(hi, n_hi // 2)
    row = (n_rep - 1 - (row_high ^ q)) * quarter + row_low
    col = ((half * n_rep + (low ^ q)) * (n_hi // 2) + hi) * per_list + c
    across = lax.broadcasted_iota(jnp.int32, (1, slots), 1)
    cell = jnp.where(across < count_ref[0], row * all_cols + col, cells)
    down = lax.broadcasted_iota(jnp.int32, (slots, slots), 0)
    side = lax.broadcasted_iota(jnp.int32, (slots, slots), 1)
    cell_down = jnp.sum(jnp.where(down == side, jnp.broadcast_to(cell, (slots, slots)), 0), axis=1, keepdims=True)
    before = jnp.where((cell_down == cell) & (down < side), down, -1)
    out_ref[4:5, :slots] = jnp.max(before, axis=0, keepdims=True)
    width = 256
    for begin in range(0, cells, width):
        here = lax.broadcasted_iota(jnp.int32, (slots, width), 1) + begin
        slot = lax.broadcasted_iota(jnp.int32, (slots, width), 0)
        slot = jnp.where(cell_down == here, slot, -1)
        for depth in range(4):
            last = jnp.max(slot, axis=0, keepdims=True)
            out_ref[depth : depth + 1, begin : begin + width] = last
            slot = jnp.where(slot < last, slot, -1)


def slot_lists(block_rows, block_fetch, block_count, n_row, n_rep, per_list, row_blocks):
    cells = row_blocks * n_row * per_list
    body = functools.partial(
        lists_body, n_rep=n_rep, n_hi=n_row // n_rep, per_list=per_list, quarter=row_blocks // n_rep
    )
    return pl.pallas_call(
        body,
        out_shape=shape((8, cells), jnp.int32),
        in_specs=[WHOLE, SMEM],
        out_specs=WHOLE,
        compiler_params=params(8 << 20),
        cost_estimate=pl.CostEstimate(flops=3 << 30, bytes_accessed=32 * cells, transcendentals=0),
        name="slot_lists",
    )(jnp.stack([block_rows, block_fetch]), block_count)


def densify_body(table_ref, held, out_ref, *, all_cols):
    chunk, row_cell = pl.program_id(0), pl.program_id(1)
    blk = held.shape[1]
    base = row_cell * all_cols + chunk * COL_CHUNK
    zero = jnp.zeros((blk, blk), BF16)

    def block(slot):
        return jnp.where(slot >= 0, held[jnp.maximum(slot, 0)], zero)

    widest = jnp.int32(-1)
    for col in range(COL_CHUNK):
        cell = base + col
        out_ref[:, col * blk : (col + 1) * blk] = block(table_ref[0, cell]) + block(table_ref[1, cell])
        widest = jnp.maximum(widest, table_ref[2, cell])

    @pl.when(widest >= 0)
    def _():
        @pl.loop(0, COL_CHUNK)
        def _(col):
            cell = base + col
            three = table_ref[2, cell]

            @pl.when(three >= 0)
            def _():
                one, two, four = table_ref[0, cell], table_ref[1, cell], table_ref[3, cell]
                total = held[one].astype(F32) + held[two].astype(F32)
                total = total + (held[three].astype(F32) + block(four).astype(F32))
                place = (slice(None), pl.ds(pl.multiple_of(col * blk, blk), blk))
                out_ref[place] = total.astype(BF16)
                five = jnp.where(four >= 0, table_ref[4, jnp.maximum(four, 0)], -1)

                @pl.when(five >= 0)
                def _():
                    def more(carry):
                        slot, total = carry
                        return table_ref[4, slot], total + held[slot].astype(F32)

                    _, rest = lax.while_loop(lambda carry: carry[0] >= 0, more, (five, total))
                    out_ref[place] = rest.astype(BF16)


def densify(table, blocks, n_row, per_list, row_blocks):
    slots, blk, _ = blocks.shape
    all_cols = n_row * per_list
    width = COL_CHUNK * blk
    return pl.pallas_call(
        functools.partial(densify_body, all_cols=all_cols),
        out_shape=shape((row_blocks * blk, all_cols * blk), BF16),
        grid_spec=pltpu.PrefetchScalarGridSpec(
            num_scalar_prefetch=1,
            grid=(all_cols // COL_CHUNK, row_blocks),
            in_specs=[WHOLE],
            out_specs=pl.BlockSpec((blk, width), lambda c, i, *_: (i, c)),
        ),
        compiler_params=params(blocks.size * 2, blk * width * 4),
        cost_estimate=pl.CostEstimate(
            flops=slots * blk * blk,
            bytes_accessed=blocks.size * 2 + 2 * all_cols * row_blocks * blk * blk,
            transcendentals=0,
        ),
        name="densify",
    )(table, blocks)


def pack_body(*refs, n_hi, per_list, blk):
    lists = refs[:n_hi]
    features = refs[n_hi]
    outs = refs[n_hi + 1 : 2 * n_hi + 1]
    own_list, sems = refs[2 * n_hi + 1 :]
    r = lax.axis_index("row")
    copies = []
    for hi in range(n_hi):
        for c in range(per_list):
            b = lists[hi][0, r, c]
            own_list[hi * per_list + c] = b
            copy = pltpu.make_async_copy(
                features.at[pl.ds(pl.multiple_of(b * blk, blk), blk)],
                outs[hi].at[pl.ds(c * blk, blk)],
                sems.at[hi * per_list + c],
            )
            copy.start()
            copies.append(copy)
    for copy in copies:
        copy.wait()


def pack(lists, features, per_list, blk):
    n_hi = len(lists)
    return pl.pallas_call(
        functools.partial(pack_body, n_hi=n_hi, per_list=per_list, blk=blk),
        out_shape=[shape((per_list * blk, features.shape[1]), BF16)] * n_hi + [shape((128,), jnp.int32)],
        in_specs=[SMEM] * n_hi + [pl.BlockSpec(memory_space=pltpu.HBM)],
        out_specs=[ANY] * n_hi + [SMEM],
        scratch_shapes=[pltpu.SemaphoreType.DMA((n_hi * per_list,))],
        compiler_params=pltpu.CompilerParams(vmem_limit_bytes=53 << 20),
        name="pack",
    )(*lists, features)


def forward_body(*refs, n_rep):
    pieces = refs[:n_rep]
    adj_ref, send_ref, keep_ref = refs[n_rep:]
    i = pl.program_id(0)
    depth = pieces[0].shape[0] // 2
    total = 0.0
    for half in range(2):
        for j in range(n_rep):
            at = (half * n_rep + j) * depth
            total += dot(adj_ref[:, at : at + depth], pieces[j][half * depth : (half + 1) * depth])

    half = pl.num_programs(0) // 2

    @pl.when(i < half)
    def _():
        send_ref[...] = total.astype(BF16)

    @pl.when(i >= half)
    def _():
        keep_ref[...] = total


def forward(pieces, adj, half_index):
    rows, cols = adj.shape[0] // 2, adj.shape[1]
    features = pieces[0].shape[1]
    tiles = rows // ROW_TILE
    half = tiles // 2
    return pl.pallas_call(
        functools.partial(forward_body, n_rep=len(pieces)),
        grid=(tiles,),
        out_shape=[shape((rows // 2, features), BF16), shape((rows // 2, features), F32)],
        in_specs=[pl.BlockSpec(x.shape, lambda i: (0, 0)) for x in pieces]
        + [pl.BlockSpec((ROW_TILE, cols), lambda i: (i + half_index * tiles, 0))],
        out_specs=[
            pl.BlockSpec((ROW_TILE, features), lambda i: (jnp.minimum(i, half - 1), 0)),
            pl.BlockSpec((ROW_TILE, features), lambda i: (jnp.maximum(i - half, 0), 0)),
        ],
        compiler_params=params(ROW_TILE * cols * 4, cols * features * 4),
        cost_estimate=pl.CostEstimate(
            flops=2 * rows * cols * features, bytes_accessed=adj.size + cols * features * 2, transcendentals=0
        ),
        name="forward",
    )(*pieces, adj)


def middle_body(
    keep_ref, near_ref, far_ref, weight_ref, cot_ref, out_ref, near_out, far_out, wkeep_ref, acc_ref, *, factor
):
    q = lax.axis_index("rep")
    hidden = (keep_ref[...] + near_ref[...].astype(F32) + far_ref[...].astype(F32)).astype(BF16)
    weight = weight_ref[...]
    pre_act = dot(hidden, weight)
    sig = jax.nn.sigmoid(pre_act)
    pre_grad = (cot_ref[...].astype(F32) * (sig * (1.0 + pre_act * (1.0 - sig)))).astype(BF16)
    features, rows = weight.shape[0], hidden.shape[0]
    input_grad = dot(weight, pre_grad, ((1,), (1,))).astype(BF16)
    near_out[:features] = input_grad
    far_out[...] = input_grad
    out_ref[...] = (pre_act * sig).astype(BF16)
    acc_ref[...] = dot(hidden, pre_grad, ((0,), (0,))) * factor
    part = wkeep_ref.shape[0] // 2
    for j in range(4):
        piece = acc_ref[pl.ds(pl.multiple_of((q ^ j) * part, part), part), :]
        if j & 1:
            fold_in(near_out, features, j // 2, piece)
        else:
            wkeep_ref[j // 2 * part : (j // 2 + 1) * part] = piece


def fold_in(ref, base, at, piece):
    part, features = piece.shape
    folds = ref.shape[1] // features
    depth = part // folds
    for i in range(folds):
        ref[base + at * depth : base + (at + 1) * depth, i * features : (i + 1) * features] = piece[
            i * depth : (i + 1) * depth
        ].astype(ref.dtype)


def fold_out(ref, base, at, part, features):
    folds = ref.shape[1] // features
    depth = part // folds
    rows = ref[base + at * depth : base + (at + 1) * depth, :].astype(F32)
    return jnp.concatenate([rows[:, i * features : (i + 1) * features] for i in range(folds)], axis=0)


def middle(keep, near, far, weight, cot, n_rep, factor):
    rows, features = keep.shape
    part = features // n_rep
    extra = part * features // rows
    return pl.pallas_call(
        functools.partial(middle_body, factor=factor),
        out_shape=[
            shape((rows, features), BF16),
            shape((features + 2 * extra, rows), BF16),
            shape((features, rows), BF16),
            shape((2 * part, features), F32),
        ],
        in_specs=[WHOLE] * 5,
        out_specs=[WHOLE] * 4,
        scratch_shapes=[pltpu.VMEM((features, features), F32)],
        compiler_params=params(12 << 20),
        cost_estimate=pl.CostEstimate(
            flops=6 * rows * features * features, bytes_accessed=rows * features * 14, transcendentals=rows * features
        ),
        name="middle",
    )(keep, near, far, weight, cot)


def back_first_body(odd_ref, even_ref, adj_ref, wkeep_ref, out_ref, w_out):
    features, rows = out_ref.shape[0], odd_ref.shape[1]
    out_ref[...] = dot(odd_ref[:features], adj_ref[:rows]) + dot(even_ref[...], adj_ref[rows:])

    @pl.when(pl.program_id(0) == 0)
    def _():
        part = w_out.shape[0] // 2
        for at in range(2):
            rows_here = slice(at * part, (at + 1) * part)
            w_out[rows_here] = wkeep_ref[rows_here] + fold_out(odd_ref, features, at, part, features)


def back_first(odd, even, adj, wkeep):
    rows, cols = adj.shape[0] // 2, adj.shape[1]
    features = wkeep.shape[1]
    whole = lambda x: pl.BlockSpec(x.shape, lambda i: (0, 0))
    return pl.pallas_call(
        back_first_body,
        grid=(cols // COL_TILE,),
        out_shape=[shape((features, cols), F32), shape(wkeep.shape, F32)],
        in_specs=[whole(odd), whole(even), pl.BlockSpec((rows, COL_TILE), lambda i: (1, i)), whole(wkeep)],
        out_specs=[pl.BlockSpec((features, COL_TILE), lambda i: (0, i)), whole(wkeep)],
        compiler_params=params(4 << 20),
        cost_estimate=pl.CostEstimate(
            flops=2 * rows * cols * features, bytes_accessed=adj.size + cols * features * 4, transcendentals=0
        ),
        name="back_first",
    )(odd, even, adj, wkeep)


def back_second_body(odd_ref, even_ref, adj_ref, first_ref, send_ref, keep_ref, acc_ref):
    q = lax.axis_index("rep")
    rows = odd_ref.shape[1]
    acc_ref[...] = first_ref[...] + dot(odd_ref[...], adj_ref[:rows]) + dot(even_ref[...], adj_ref[rows:])
    part = send_ref.shape[0] // 2
    for j in range(4):
        out = send_ref if j & 1 else keep_ref
        at = (3 - j) // 2 * part
        piece = acc_ref[pl.ds(pl.multiple_of((q ^ j) * part, part), part), :]
        out[at : at + part] = piece.astype(out.dtype)


def back_second(odd, even, adj, first, half, n_rep, per_piece):
    rows, cols = adj.shape[0] // 2, adj.shape[1] // 2
    features = first.shape[0]
    width = cols // n_rep // per_piece
    tiles = cols // width
    whole = lambda x: pl.BlockSpec(x.shape, lambda i: (0, 0))
    return pl.pallas_call(
        back_second_body,
        grid=(tiles,),
        out_shape=[shape((features // 2, cols), BF16), shape((features // 2, cols), F32)],
        in_specs=[
            whole(odd),
            whole(even),
            pl.BlockSpec((rows, width), lambda i: (0, i + half * tiles)),
            pl.BlockSpec((features, width), lambda i: (0, i + half * tiles)),
        ],
        out_specs=[
            pl.BlockSpec(
                (features // 2, width), lambda i: (0, (lax.div(i, per_piece) ^ 1) * per_piece + lax.rem(i, per_piece))
            ),
            pl.BlockSpec((features // 2, width), lambda i: (0, i)),
        ],
        scratch_shapes=[pltpu.VMEM((features, width), F32)],
        compiler_params=params(4 << 20),
        cost_estimate=pl.CostEstimate(
            flops=2 * rows * cols * features, bytes_accessed=rows * cols * 2 + cols * features * 7, transcendentals=0
        ),
        name=f"back_second_{half}",
    )(odd, even, adj, first)


def across_body(low_ref, low_near, high_ref, high_near, out_ref):
    part, cols = out_ref.shape[0], low_ref.shape[1]
    for half, (keep, near) in enumerate(((low_ref, low_near), (high_ref, high_near))):
        out_ref[:, half * cols : (half + 1) * cols] = (keep[:part] + near[:part].astype(F32)).astype(BF16)


def across_sum(keep_low, near_low, keep_high, near_high):
    rows, cols = keep_low.shape
    return pl.pallas_call(
        across_body,
        out_shape=shape((rows // 2, 2 * cols), BF16),
        in_specs=[WHOLE] * 4,
        out_specs=WHOLE,
        compiler_params=params(rows * cols * 14),
        cost_estimate=pl.CostEstimate(flops=rows * cols, bytes_accessed=rows * cols * 8, transcendentals=0),
        name="across_sum",
    )(keep_low, near_low, keep_high, near_high)


def split_body(low_ref, low_near, high_ref, high_near, far_ref, w_ref, out_ref, *, n_rep, deep):
    r, q = lax.axis_index("row"), lax.axis_index("rep")
    part, width = far_ref.shape[0], out_ref.shape[2]
    depth = w_ref.shape[0] // W_SHARE
    w = w_ref[pl.ds(pl.multiple_of((r & (W_SHARE - 1)) * depth, depth), depth), :].astype(BF16)
    per_half = n_rep * deep
    for half, (own, near) in enumerate(((low_ref, low_near), (high_ref, high_near))):
        for i in range(per_half):
            low, hi = i % n_rep, i // n_rep
            j = low ^ q
            cols = pl.ds(pl.multiple_of((j * deep + hi) * width, width), width)
            far_cols = pl.ds(pl.multiple_of((half * per_half + (j ^ 2) * deep + hi) * width, width), width)
            total = own[part:, cols] + near[part:, cols].astype(F32) + far_ref[:, far_cols].astype(F32)
            out_ref[r ^ (half * per_half + i), :part] = total.astype(BF16)
            out_ref[r ^ (half * per_half + i), part:] = w


def split(keep_low, near_low, keep_high, near_high, far, w, n_row, n_rep):
    part, cols = far.shape
    return pl.pallas_call(
        functools.partial(split_body, n_rep=n_rep, deep=n_row // n_rep // 2),
        out_shape=shape((n_row, part + w.shape[0] // W_SHARE, cols // n_row), BF16),
        in_specs=[WHOLE] * 6,
        out_specs=WHOLE,
        compiler_params=params(cols * part * 20),
        cost_estimate=pl.CostEstimate(flops=2 * part * cols, bytes_accessed=part * cols * 10, transcendentals=0),
        name="split",
    )(keep_low, near_low, keep_high, near_high, far, w)


def collect_body(*refs, n_row, n_rep, per_list, quarter, blk):
    lists = refs[:n_rep]
    messages = refs[n_rep]
    outs, w_out, acc_ref = refs[n_rep + 1 : -2], refs[-2], refs[-1]
    r, q = lax.axis_index("row"), lax.axis_index("rep")
    acc_ref[...] = jnp.zeros(acc_ref.shape, F32)
    for k in range(n_row):
        j = (k % n_rep) ^ q
        for c in range(per_list):
            at = k // n_rep * per_list + c
            b = lists[0][at]
            for other in range(1, n_rep):
                b = jnp.where(j == other, lists[other][at], b)
            cell = (lax.div(b, quarter) ^ q) * quarter + lax.rem(b, quarter)
            cols = pl.ds(pl.multiple_of(cell * blk, blk), blk)
            acc_ref[:, cols] += messages[r ^ k, : acc_ref.shape[0], c * blk : (c + 1) * blk].astype(F32)
    width = outs[0].shape[1]
    part, depth = acc_ref.shape[0], w_out.shape[0] // W_SHARE
    for parity in range(W_SHARE):
        total = messages[parity, part:].astype(F32)
        for other in range(parity + W_SHARE, n_row, W_SHARE):
            total += messages[other, part:].astype(F32)
        w_out[parity * depth : (parity + 1) * depth] = total.astype(BF16)
    for j, out in enumerate(outs):
        out[:part] = acc_ref[:, j * width : (j + 1) * width].astype(out.dtype)
        if j:
            fold_in(out, part, 0, w_out[...])


def collect(lists, messages, part, per_list, row_blocks, blk):
    n_rep = len(lists)
    n_row, rows, features = messages.shape
    depth = W_SHARE * (rows - part)
    quarter = row_blocks // n_rep
    body = functools.partial(
        collect_body, n_row=n_row, n_rep=n_rep, per_list=per_list, quarter=quarter, blk=blk
    )
    return pl.pallas_call(
        body,
        out_shape=[shape((part, quarter * blk), F32)]
        + [shape((part + depth * features // (quarter * blk), quarter * blk), BF16)] * (n_rep - 1)
        + [shape((depth, features), BF16)],
        in_specs=[SMEM] * n_rep + [WHOLE],
        out_specs=[WHOLE] * (n_rep + 1),
        scratch_shapes=[pltpu.VMEM((part, row_blocks * blk), F32)],
        compiler_params=params(4 << 20),
        cost_estimate=pl.CostEstimate(
            flops=part * row_blocks * blk, bytes_accessed=part * row_blocks * blk * 5, transcendentals=0
        ),
        name="collect",
    )(*lists, messages)


def finish_body(*refs, n_rep):
    grads = refs[:n_rep]
    w_ref, node_ref, weight_ref, acc_ref = refs[n_rep:]
    q = lax.axis_index("rep")
    part = w_ref.shape[0]
    for j in range(n_rep):
        rows = pl.ds(pl.multiple_of((q ^ j) * part, part), part)
        acc_ref[rows, :] = grads[j][:part].astype(F32)
        weight_ref[rows, :] = fold_out(grads[j], part, 0, *w_ref.shape) if j else w_ref[...].astype(F32)
    node_ref[...] = acc_ref[...].T


def finish(grads, w):
    n_rep = len(grads)
    part, rows = grads[0].shape
    features = w.shape[1]
    return pl.pallas_call(
        functools.partial(finish_body, n_rep=n_rep),
        out_shape=[shape((rows, part * n_rep), F32), shape((features, features), F32)],
        in_specs=[WHOLE] * (n_rep + 1),
        out_specs=[WHOLE] * 2,
        scratch_shapes=[pltpu.VMEM((part * n_rep, rows), F32)],
        compiler_params=params(6 << 20),
        cost_estimate=pl.CostEstimate(flops=0, bytes_accessed=rows * part * n_rep * 8, transcendentals=0),
        name="finish",
    )(*grads, w)


def local(
    node_features, weight, out_grad, blocks, block_rows, block_fetch, fetch_lists, block_count
):
    n_row = lax.axis_size("row")
    n_rep = lax.axis_size("rep")
    n_hi = n_row // n_rep
    band_rows, features = node_features.shape
    blk = blocks.shape[1]
    row_blocks = band_rows // blk
    per_list = fetch_lists.shape[2]

    def to_rep(x, j):
        return lax.ppermute(x, "rep", xor_perm(n_rep, j))

    def to_row(x, k):
        return lax.ppermute(x, "row", xor_perm(n_row, k))

    def spread(x, hi):
        perm = [
            (r * n_rep + q, (r ^ (hi * n_rep + q)) * n_rep + q) for r in range(n_row) for q in range(n_rep)
        ]
        return lax.ppermute(x, ("row", "rep"), perm)

    def after(x, *done):
        return lax.optimization_barrier((x, *done))[0]

    wanted = [spread(fetch_lists, hi) for hi in range(n_hi)]
    *outgoing, own_list = pack(wanted, node_features, per_list, blk)
    own = [spread(x, hi) for hi, x in enumerate(outgoing)]
    deep = n_hi // 2
    table = slot_lists(after(block_rows, own_list), block_fetch, block_count, n_row, n_rep, per_list, row_blocks)
    own_list = after(own_list, table)
    lists = [own_list] + [to_rep(own_list, j) for j in range(1, n_rep)]
    own = after(jnp.concatenate(own, axis=0), table, lists)
    far = to_rep(own, 2)
    near = to_rep(own, 1)
    adj = densify(after(table, near), blocks, n_row, per_list, row_blocks)
    pieces = [own, near, far, to_rep(after(far, adj), 1)]

    send3, keep2 = forward(pieces, adj, 0)
    across = (keep2 + to_rep(send3, 1).astype(F32)).astype(BF16)
    arrived = to_rep(across, 2)
    send1, keep0 = forward(pieces, after(adj, across), 1)
    arrived = after(arrived, keep0)
    factor = float(n_row * band_rows) ** (-0.5)
    output, to_near, grad0, wkeep = middle(keep0, to_rep(send1, 1), arrived, weight, out_grad, n_rep, factor)

    grad2 = to_rep(grad0, 2)
    first, w = back_first(to_rep(to_near, 1), grad0, adj, wkeep)
    part = features // n_rep
    grad2 = after(grad2, first)
    grad3 = to_rep(grad2, 1)
    got = to_rep(after(w, grad2)[part:], 2)
    send_high, keep_high = back_second(grad3, grad2, adj, first, 1, n_rep, deep)
    send_high = after(send_high, got)
    near_high = to_rep(send_high, 1)
    send_low, keep_low = back_second(grad3, grad2, adj, after(first, send_high), 0, n_rep, deep)
    near_low = to_rep(after(send_low, near_high), 1)
    across = across_sum(keep_low, near_low, keep_high, near_high)
    far = to_rep(across, 2)
    w = after(w[:part], across) + got
    for step in (1, 2):
        w = w + to_row(w, step)
    messages = split(keep_low, near_low, keep_high, near_high, far, w, n_row, n_rep)
    returned = lax.all_to_all(messages, "row", split_axis=0, concat_axis=0, tiled=True)
    *grads, w = collect(lists, returned, part, per_list, row_blocks, blk)
    node_grad, weight_grad = finish([grads[0]] + [to_rep(grads[j], j) for j in range(1, n_rep)], w)
    return (output, weight_grad, node_grad)


def solution(mesh):
    in_specs = (
        P("row", None),
        P(),
        P(("row", "rep"), None),
        P(("row", "rep"), None, None),
        P(("row", "rep")),
        P(("row", "rep")),
        P(("row", "rep"), None, None),
        P(("row", "rep")),
    )
    out_specs = (P(("row", "rep"), None), P(), P(("row", "rep"), None))
    return jax.shard_map(local, mesh=mesh, in_specs=in_specs, out_specs=out_specs, check_vma=False)
```
